32 devices in a mesh: seq: 8 (over z, core), fsdp: 4 (over y, x).
Axes of the slice: x: 2, y: 2, z: 4, core: 2. Of those that a mesh axis runs over, the one named last changes fastest.
Arguments:
- inputs: bfloat16 [4, 2048, 2048], P('fsdp', 'seq'), may hold values from -6 to 6
- cotangent: bfloat16 [4, 2048, 2048], P('fsdp', 'seq'), may hold values from -6 to 6
- w_inward: float32 [2048, 2560], P(('seq', 'fsdp')), may hold values from -0.125 to 0.125
- w_outward: float32 [2048, 2048], P(('seq', 'fsdp')), may hold values from -1 to 1
- w_gate_up: float32 [2048, 11264], P(('seq', 'fsdp')), may hold values from -0.125 to 0.125
- w_down: float32 [2048, 5632], P(('seq', 'fsdp')), may hold values from -0.078125 to 0.078125
- gains: float32 [2, 2048], P(None, ('seq', 'fsdp')), may hold values from 0.5 to 1.5
- first_inward: float32 [2048, 2560], P(('seq', 'fsdp')), may hold values from -64 to 64
- first_outward: float32 [2048, 2048], P(('seq', 'fsdp')), may hold values from -3 to 3
- first_gate_up: float32 [2048, 11264], P(('seq', 'fsdp')), may hold values from -16 to 16
- first_down: float32 [2048, 5632], P(('seq', 'fsdp')), may hold values from -32 to 32
- first_gains: float32 [2, 2048], P(None, ('seq', 'fsdp')), may hold values from -128 to 128
- second_inward: float32 [2048, 2560], P(('seq', 'fsdp')), may hold values from 430.8992 to 1723.5968
- second_outward: float32 [2048, 2048], P(('seq', 'fsdp')), may hold values from 1.077248 to 4.308992
- second_gate_up: float32 [2048, 11264], P(('seq', 'fsdp')), may hold values from 38.78093 to 155.15648
- second_down: float32 [2048, 5632], P(('seq', 'fsdp')), may hold values from 107.7248 to 430.8992
- second_gains: float32 [2, 2048], P(None, ('seq', 'fsdp')), may hold values from 1723.5968 to 6894.387
Outputs:
- output: bfloat16 [4, 2048, 2048], P('fsdp', 'seq')
- input_grad: float32 [4, 2048, 2048], P('fsdp', 'seq')
- first_inward_new: float32 [2048, 2560], P(('seq', 'fsdp'))
- second_inward_new: float32 [2048, 2560], P(('seq', 'fsdp'))
- inward_new: float32 [2048, 2560], P(('seq', 'fsdp'))
- first_outward_new: float32 [2048, 2048], P(('seq', 'fsdp'))
- second_outward_new: float32 [2048, 2048], P(('seq', 'fsdp'))
- outward_new: float32 [2048, 2048], P(('seq', 'fsdp'))
- first_gate_up_new: float32 [2048, 11264], P(('seq', 'fsdp'))
- second_gate_up_new: float32 [2048, 11264], P(('seq', 'fsdp'))
- gate_up_new: float32 [2048, 11264], P(('seq', 'fsdp'))
- first_down_new: float32 [2048, 5632], P(('seq', 'fsdp'))
- second_down_new: float32 [2048, 5632], P(('seq', 'fsdp'))
- down_new: float32 [2048, 5632], P(('seq', 'fsdp'))
- first_gains_new: float32 [2, 2048], P(None, ('seq', 'fsdp'))
- second_gains_new: float32 [2, 2048], P(None, ('seq', 'fsdp'))
- gains_new: float32 [2, 2048], P(None, ('seq', 'fsdp'))
The draws below stay inside these ranges and needn't reach their ends.
All inputs are finite; a program needn't handle non-finite values.
Results may differ from the reference program's by a relative error of at most 0.015.
Values may be sent and summed in bfloat16 or wider, within the bound.
A program may use at most 640 MiB of HBM per device.

```python
import math
import jax
import jax.numpy as jnp
from jax import lax

D = 2048
FF = 5632
HEADS = 32
KV_HEADS = 4
HEAD_DIM = 64
TOK_DEV = 256
STEP = 10
SEQS = 4
LEN = 2048
ALL_TOKENS = 8192
N_SEQ = 8


def shard_levels(key, extent, shards, smallest, largest):
    loudness = 1.0
    for dim, parts in shards:
        draws = jax.random.uniform(jax.random.fold_in(jax.random.fold_in(key, 6), dim), (parts,), jnp.float32, smallest / len(shards), largest / len(shards))
        loudness = loudness * jnp.repeat(jnp.exp(draws), extent[dim] // parts).reshape((-1,) + (1,) * (len(extent) - 1 - dim))
    return loudness


def bell_draw(stream_key, dims, spread, bound, cuts=(), kind=jnp.bfloat16):
    values = spread * jax.random.normal(stream_key, dims, jnp.float32)
    if cuts:
        values = values * shard_levels(stream_key, dims, cuts, -0.22, 0.18)
    return jnp.clip(values, -bound, bound).astype(kind)


def setup_inputs(seed: int = 0) -> dict:
    key_list = jax.random.split(jax.random.key(seed), 18)
    return {
        "inputs": bell_draw(key_list[0], (SEQS, LEN, D), 1.0, 6.0, ((0, 4), (1, 8))),
        "cotangent": bell_draw(key_list[1], (SEQS, LEN, D), 1.0, 6.0, ((0, 4), (1, 8))),
        "w_inward": bell_draw(key_list[2], (D, D + 2 * KV_HEADS * HEAD_DIM), D ** -0.5, 0.125, ((0, 32),), jnp.float32),
        "w_outward": bell_draw(key_list[3], (D, D), (max(4, 32 * D // (TOK_DEV * N_SEQ))) ** -0.5, 1.0, ((0, 32),), jnp.float32),
        "w_gate_up": bell_draw(key_list[4], (D, 2 * FF), D ** -0.5, 0.125, ((0, 32),), jnp.float32),
        "w_down": bell_draw(key_list[5], (D, FF), FF ** -0.5, 0.078125, ((0, 32),), jnp.float32),
        "gains": jnp.clip(1.0 + 0.1 * jax.random.normal(key_list[6], (2, D), jnp.float32), 0.5, 1.5),
        "first_inward": bell_draw(key_list[7], (D, D + 2 * KV_HEADS * HEAD_DIM), (0.111 * ALL_TOKENS ** 0.5), 64.0, ((0, 32),), jnp.float32),
        "first_outward": bell_draw(key_list[8], (D, D), (0.00555 * ALL_TOKENS ** 0.5), 3.0, ((0, 32),), jnp.float32),
        "first_gate_up": bell_draw(key_list[9], (D, 2 * FF), (0.0333 * ALL_TOKENS ** 0.5), 16.0, ((0, 32),), jnp.float32),
        "first_down": bell_draw(key_list[10], (D, FF), (0.0555 * ALL_TOKENS ** 0.5), 32.0, ((0, 32),), jnp.float32),
        "first_gains": bell_draw(key_list[11], (2, D), (0.222 * ALL_TOKENS ** 0.5), 128.0, ((1, 32),), jnp.float32),
        "second_inward": jnp.clip(jnp.exp(math.log(1723.5968) - 1.3862944 * jax.random.uniform(key_list[12], (D, D + 2 * KV_HEADS * HEAD_DIM), jnp.float32) ** shard_levels(key_list[12], (D, D + 2 * KV_HEADS * HEAD_DIM), ((0, 32),), -0.2, 0.2)), 430.8992, 1723.5968),
        "second_outward": jnp.clip(jnp.exp(math.log(4.308992) - 1.3862944 * jax.random.uniform(key_list[13], (D, D), jnp.float32) ** shard_levels(key_list[13], (D, D), ((0, 32),), -0.2, 0.2)), 1.077248, 4.308992),
        "second_gate_up": jnp.clip(jnp.exp(math.log(155.15648) - 1.3865055 * jax.random.uniform(key_list[14], (D, 2 * FF), jnp.float32) ** shard_levels(key_list[14], (D, 2 * FF), ((0, 32),), -0.2, 0.2)), 38.78093, 155.15648),
        "second_down": jnp.clip(jnp.exp(math.log(430.8992) - 1.3862944 * jax.random.uniform(key_list[15], (D, FF), jnp.float32) ** shard_levels(key_list[15], (D, FF), ((0, 32),), -0.2, 0.2)), 107.7248, 430.8992),
        "second_gains": jnp.clip(jnp.exp(math.log(6894.387) - 1.3862944 * jax.random.uniform(key_list[16], (2, D), jnp.float32) ** shard_levels(key_list[16], (2, D), ((1, 32),), -0.2, 0.2)), 1723.5968, 6894.387),
    }


epsilon = 1e-05
adam_epsilon = 1e-08
beta_first = 0.9
beta_second = 0.95
rope_base = 10000.0
weight_decay = 0.1
masked_value = -1e+30
highest = lax.Precision.HIGHEST

@jax.custom_vjp
def low(v):
    return lax.optimization_barrier(v.astype(jnp.bfloat16)).astype(jnp.float32)

@jax.custom_vjp
def low_back(v):
    return v

def low_keep(v):
    return (low(v), None)

def low_pass(kept, grad):
    return (grad,)

def back_keep(v):
    return (v, None)

def back_low(kept, grad):
    return (low(grad),)
low.defvjp(low_keep, low_pass)
low_back.defvjp(back_keep, back_low)

def rotate(field, position, sign):
    half = field.shape[-1] // 2
    exponent = jnp.arange(half).astype(jnp.float32) * (-2.0 / field.shape[-1])
    frequency = jnp.power(rope_base, exponent)
    angle = position[:, None] * frequency[None, :]
    cosine = jnp.cos(angle)[:, None, :]
    sine = sign * jnp.sin(angle)[:, None, :]
    first = field[..., :half]
    second = field[..., half:]
    return jnp.concatenate([first * cosine - second * sine, second * cosine + first * sine], axis=-1)

def normalize(rows, gain):
    return rows * lax.rsqrt(lax.optimization_barrier(jnp.mean(rows * rows, axis=-1, keepdims=True)) + epsilon) * gain

def attend(query, key, value):
    raw = jnp.einsum('lhd,md->hlm', query, key, precision=highest)
    scores = low_back(raw) * query.shape[-1] ** (-0.5)
    place = jnp.arange(query.shape[0])
    scores = jnp.where(place[None, None, :] <= place[None, :, None], scores, masked_value)
    scores = scores - lax.optimization_barrier(jnp.max(scores, axis=-1, keepdims=True))
    weights = jnp.exp(scores)
    shares = weights / lax.optimization_barrier(jnp.sum(weights, axis=-1, keepdims=True))
    return jnp.einsum('hlm,md->lhd', low(shares), value, precision=highest)

def attend_item(item):
    return jax.checkpoint(attend)(item[0], item[1], item[2])

def forward_seq(rows, w_inward, w_outward, w_gate_up, w_down, gains):
    gain = low(gains)
    length = rows.shape[0]
    group = N_SEQ
    per_group = HEADS // group
    kv_width = KV_HEADS * HEAD_DIM
    position = jnp.arange(length).astype(jnp.float32)
    normed = low(normalize(rows, gain[0]))
    mixed = low_back(jnp.dot(normed, low(w_inward), precision=highest))
    query = rotate(mixed[:, :D].reshape(length, HEADS, HEAD_DIM), position, 1.0)
    key = rotate(mixed[:, D:D + kv_width].reshape(length, KV_HEADS, HEAD_DIM), position, 1.0)
    value = mixed[:, D + kv_width:].reshape(length, KV_HEADS, HEAD_DIM)
    query = low_back(low(query))
    key_copies = low_back(jnp.repeat(low(key), group // KV_HEADS, axis=1))
    value_copies = low_back(jnp.repeat(low(value), group // KV_HEADS, axis=1))
    grouped = query.reshape(length, group, per_group, HEAD_DIM).transpose(1, 0, 2, 3)
    attended = lax.map(attend_item, (grouped, key_copies.transpose(1, 0, 2), value_copies.transpose(1, 0, 2)))
    attended = low_back(low(attended.transpose(1, 0, 2, 3).reshape(length, D)))
    branch = low_back(jnp.dot(attended, low(w_outward), precision=highest))
    middle = rows + branch
    normed_second = low(normalize(middle, gain[1]))
    gate_up = low_back(jnp.dot(normed_second, low(w_gate_up), precision=highest))
    hidden = low(jax.nn.silu(gate_up[:, :FF]) * gate_up[:, FF:])
    return middle + jnp.dot(hidden, low(w_down).T, precision=highest)

def adam_update(weight, first, second, grad, rate, decay):
    first_new = beta_first * first + (1.0 - beta_first) * grad
    second_new = beta_second * second + (1.0 - beta_second) * grad * grad
    first_hat = first_new / (1.0 - beta_first ** STEP)
    second_hat = second_new / (1.0 - beta_second ** STEP)
    weight_new = weight - rate * (first_hat / (jnp.sqrt(second_hat) + adam_epsilon) + decay * weight)
    return (first_new, second_new, weight_new)

def reference(inputs, cotangent, w_inward, w_outward, w_gate_up, w_down, gains, first_inward, first_outward, first_gate_up, first_down, first_gains, second_inward, second_outward, second_gate_up, second_down, second_gains):
    weights = (w_inward, w_outward, w_gate_up, w_down, gains)

    def one_sequence(totals, item):
        result, pullback = jax.vjp(forward_seq, item[0].astype(jnp.float32), w_inward, w_outward, w_gate_up, w_down, gains)
        grads = pullback(item[1].astype(jnp.float32))
        return (jax.tree.map(jnp.add, totals, tuple(grads[1:])), (result.astype(jnp.bfloat16), grads[0]))
    zeros = tuple((jnp.zeros_like(weight) for weight in weights))
    totals, (output, input_grad) = lax.scan(one_sequence, zeros, (inputs, cotangent))
    first_inward_new, second_inward_new, inward_new = adam_update(w_inward, first_inward, second_inward, totals[0], 0.02, weight_decay)
    first_outward_new, second_outward_new, outward_new = adam_update(w_outward, first_outward, second_outward, totals[1], 0.15, weight_decay)
    first_gate_up_new, second_gate_up_new, gate_up_new = adam_update(w_gate_up, first_gate_up, second_gate_up, totals[2], 0.02, weight_decay)
    first_down_new, second_down_new, down_new = adam_update(w_down, first_down, second_down, totals[3], 0.015, weight_decay)
    first_gains_new, second_gains_new, gains_new = adam_update(gains, first_gains, second_gains, totals[4], 0.6, 0.0)
    return (output, input_grad, first_inward_new, second_inward_new, inward_new, first_outward_new, second_outward_new, outward_new, first_gate_up_new, second_gate_up_new, gate_up_new, first_down_new, second_down_new, down_new, first_gains_new, second_gains_new, gains_new)
```

```python
import functools

import jax
import jax.numpy as jnp
from jax import lax
from jax.experimental import pallas as pl
from jax.experimental.pallas import tpu as pltpu
from jax.sharding import PartitionSpec as P

D = 2048
FF = 5632
HEADS = 32
KV_HEADS = 4
HEAD_DIM = 64
STEP = 10


epsilon = 1e-05
adam_epsilon = 1e-08
beta_first = 0.9
beta_second = 0.95
rope_base = 10000.0
weight_decay = 0.1
masked_value = -1e30


def rotate(field, position, sign):
    half = field.shape[-1] // 2
    exponent = jnp.arange(half).astype(jnp.float32) * (-2.0 / field.shape[-1])
    frequency = jnp.power(rope_base, exponent)
    angle = position[:, None] * frequency[None, :]
    cosine = jnp.cos(angle)[:, None, :]
    sine = sign * jnp.sin(angle)[:, None, :]
    first = field[..., :half]
    second = field[..., half:]
    return jnp.concatenate(
        [first * cosine - second * sine, second * cosine + first * sine], axis=-1
    )


def rms_scale(rows):
    return lax.rsqrt(jnp.mean(rows * rows, axis=-1, keepdims=True) + epsilon)


def norm_back(rows, scale_rows, gain, grad):
    weighted = grad * gain
    row_grad = scale_rows * weighted - rows * scale_rows**3 * jnp.mean(
        weighted * rows, axis=-1, keepdims=True
    )
    gain_grad = jnp.sum(grad * rows * scale_rows, axis=0)
    return (row_grad, gain_grad)


def dot(left, right):
    return jnp.dot(left, right, preferred_element_type=jnp.float32)


def outer(left, right):
    return lax.dot_general(
        left, right, (((0,), (0,)), ((), ())), preferred_element_type=jnp.float32
    )


def against(left, right):
    return lax.dot_general(
        left, right, (((1,), (1,)), ((), ())), preferred_element_type=jnp.float32
    )


def stack_heads(field, heads):
    return jnp.concatenate(
        [field[:, h * HEAD_DIM : (h + 1) * HEAD_DIM] for h in range(heads)], axis=0
    )


def unstack_heads(field, heads):
    rows = field.shape[0] // heads
    return jnp.concatenate([field[h * rows : (h + 1) * rows] for h in range(heads)], axis=1)


def masked_scores(keys, queries, start, first, block):
    scores = against(keys, queries)
    key_place = start + lax.broadcasted_iota(jnp.int32, scores.shape, 0)
    query_place = first + lax.rem(lax.broadcasted_iota(jnp.int32, scores.shape, 1), block)
    return jnp.where(key_place <= query_place, scores, masked_value)


def forward_kernel(query_ref, kv_ref, out_ref, log_ref, *, heads, block):
    index = pl.program_id(0)
    queries = stack_heads(query_ref[...], heads) * jnp.bfloat16(HEAD_DIM**-0.5)
    width = heads * block

    def step(j, carry, masked):
        largest, total, mixed = carry
        start = pl.multiple_of(j * block, block)
        kv = kv_ref[pl.ds(start, block), :]
        keys, values = kv[:, :HEAD_DIM], kv[:, HEAD_DIM:]
        if masked:
            scores = masked_scores(keys, queries, start, index * block, block)
        else:
            scores = against(keys, queries)
        new = jnp.maximum(largest, jnp.max(scores, axis=0, keepdims=True))
        fade = jnp.exp(largest - new)
        weights = jnp.exp(scores - new)
        total = total * fade + jnp.sum(weights, axis=0, keepdims=True)
        mixed = mixed * fade + outer(values, weights.astype(jnp.bfloat16))
        return new, total, mixed

    carry = (
        jnp.full((1, width), masked_value, jnp.float32),
        jnp.zeros((1, width), jnp.float32),
        jnp.zeros((HEAD_DIM, width), jnp.float32),
    )
    carry = lax.fori_loop(0, index, lambda j, c: step(j, c, False), carry)
    largest, total, mixed = step(index, carry, True)
    log_ref[0] = largest + jnp.log(total)
    out_ref[...] = unstack_heads((mixed / total).T, heads).astype(out_ref.dtype)


def backward_kernel(
    query_ref, kv_ref, grad_ref, out_ref, log_ref, query_grad_ref, kv_grad_ref,
    key_sum, value_sum, *, heads, block
):
    index = pl.program_id(0)
    scale = HEAD_DIM**-0.5

    @pl.when(index == 0)
    def _():
        key_sum[...] = jnp.zeros_like(key_sum)
        value_sum[...] = jnp.zeros_like(value_sum)

    queries = stack_heads(query_ref[...], heads) * jnp.bfloat16(scale)
    grads = stack_heads(grad_ref[...], heads)
    mixed = stack_heads(out_ref[...], heads)
    inner = jnp.sum(
        (grads.astype(jnp.float32) * mixed.astype(jnp.float32)).T, axis=0, keepdims=True
    )
    log_total = log_ref[0]

    def step(j, query_grad, masked):
        start = pl.multiple_of(j * block, block)
        place = pl.ds(start, block)
        kv = kv_ref[place, :]
        keys, values = kv[:, :HEAD_DIM], kv[:, HEAD_DIM:]
        if masked:
            scores = masked_scores(keys, queries, start, index * block, block)
        else:
            scores = against(keys, queries)
        shares = jnp.exp(scores - log_total)
        share_grad = against(values, grads)
        score_grad = (shares * (share_grad - inner)).astype(jnp.bfloat16)
        value_sum[place, :] += dot(shares.astype(jnp.bfloat16), grads)
        key_sum[place, :] += dot(score_grad, queries)
        return query_grad + outer(keys, score_grad)

    query_grad = lax.fori_loop(
        0,
        index,
        lambda j, c: step(j, c, False),
        jnp.zeros((HEAD_DIM, heads * block), jnp.float32),
    )
    query_grad = step(index, query_grad, True)
    query_grad_ref[...] = unstack_heads((query_grad * scale).T, heads).astype(jnp.bfloat16)

    @pl.when(index == pl.num_programs(0) - 1)
    def _():
        kv_grad_ref[...] = jnp.concatenate([key_sum[...], value_sum[...]], axis=1).astype(
            jnp.bfloat16
        )


def attention_specs(length, width, heads, block):
    rows = pl.BlockSpec((block, width), lambda i: (i, 0))
    kv = pl.BlockSpec((length, 2 * HEAD_DIM), lambda i: (0, width // (2 * HEAD_DIM)))
    logs = pl.BlockSpec((1, 1, heads * block), lambda i: (i, 0, 0))
    return rows, kv, logs


def attend_forward(packed, heads, block):
    length, width = packed.shape[0], heads * HEAD_DIM
    rows, kv, logs = attention_specs(length, width, heads, block)
    pairs = heads * length * length // 2
    return pl.pallas_call(
        functools.partial(forward_kernel, heads=heads, block=block),
        grid=(length // block,),
        in_specs=[rows, kv],
        out_specs=[rows, logs],
        out_shape=[
            jax.ShapeDtypeStruct((length, width), jnp.bfloat16),
            jax.ShapeDtypeStruct((length // block, 1, heads * block), jnp.float32),
        ],
        compiler_params=pltpu.CompilerParams(vmem_limit_bytes=48 << 20),
        cost_estimate=pl.CostEstimate(
            flops=pairs * HEAD_DIM * 16, bytes_accessed=length * 4 * width, transcendentals=pairs
        ),
    )(packed, packed)


def attend_backward(packed, grads, mixed, logs_in, heads, block):
    length, width = packed.shape[0], heads * HEAD_DIM
    rows, kv, logs = attention_specs(length, width, heads, block)
    pairs = heads * length * length // 2
    return pl.pallas_call(
        functools.partial(backward_kernel, heads=heads, block=block),
        grid=(length // block,),
        in_specs=[rows, kv, rows, rows, logs],
        out_specs=[rows, pl.BlockSpec((length, 2 * HEAD_DIM), lambda i: (0, 0))],
        out_shape=[
            jax.ShapeDtypeStruct((length, width), jnp.bfloat16),
            jax.ShapeDtypeStruct((length, 2 * HEAD_DIM), jnp.bfloat16),
        ],
        scratch_shapes=[
            pltpu.VMEM((length, HEAD_DIM), jnp.float32),
            pltpu.VMEM((length, HEAD_DIM), jnp.float32),
        ],
        compiler_params=pltpu.CompilerParams(vmem_limit_bytes=48 << 20),
        cost_estimate=pl.CostEstimate(
            flops=pairs * HEAD_DIM * 40, bytes_accessed=length * 8 * width, transcendentals=pairs
        ),
    )(packed, packed, grads, mixed, logs_in)


def swap(piece, axis, offset):
    size = lax.axis_size(axis)
    return lax.ppermute(piece, axis, [(i, i ^ offset) for i in range(size)])


def gather_swap(piece, axis):
    return [piece] + [swap(piece, axis, d) for d in range(1, lax.axis_size(axis))]


def exchange_swap(stack, axis):
    me = lax.axis_index(axis)
    pieces = [
        lax.dynamic_index_in_dim(stack, me ^ d, 0, keepdims=False)
        for d in range(lax.axis_size(axis))
    ]
    return [pieces[0]] + [swap(p, axis, d) for d, p in enumerate(pieces) if d]


def reduce_swap(parts, axis):
    total = parts[0].astype(jnp.float32)
    for d in range(1, len(parts)):
        total = total + swap(parts[d], axis, d).astype(jnp.float32)
    return total


def in_order(pieces, axis):
    me = lax.axis_index(axis)
    stack = jnp.stack(pieces)
    return [
        lax.dynamic_index_in_dim(stack, j ^ me, 0, keepdims=False) for j in range(len(pieces))
    ]


def return_columns(partial):
    mine = lax.psum_scatter(partial, "seq", scatter_dimension=0, tiled=True)
    size = lax.axis_size("fsdp")
    stack = mine.reshape(size, mine.shape[0] // size, mine.shape[1])
    return in_order(exchange_swap(stack, "fsdp"), "fsdp")


def adam_update(weight, first, second, grad, rate, decay):
    first_new = beta_first * first + (1.0 - beta_first) * grad
    second_new = beta_second * second + (1.0 - beta_second) * grad * grad
    first_hat = first_new / (1.0 - beta_first**STEP)
    second_hat = second_new / (1.0 - beta_second**STEP)
    weight_new = weight - rate * (
        first_hat / (jnp.sqrt(second_hat) + adam_epsilon) + decay * weight
    )
    return (first_new, second_new, weight_new)


def body(
    inputs,
    cotangent,
    w_inward,
    w_outward,
    w_gate_up,
    w_down,
    gains,
    first_inward,
    first_outward,
    first_gate_up,
    first_down,
    first_gains,
    second_inward,
    second_outward,
    second_gate_up,
    second_down,
    second_gains,
):
    rows = inputs[0].astype(jnp.float32)
    upstream = cotangent[0]
    local = rows.shape[0]
    group = lax.axis_size("seq")
    slices = lax.axis_size("fsdp")
    heads_here = HEADS // group
    copies = group // KV_HEADS
    kv_width = KV_HEADS * HEAD_DIM
    head_cols = heads_here * HEAD_DIM
    inward_cols = D + 2 * kv_width
    ff_cols = FF // slices
    depth = w_inward.shape[0]
    position = (lax.axis_index("seq") * local + jnp.arange(local)).astype(jnp.float32)

    low_inward = w_inward.astype(jnp.bfloat16)
    low_gains = jnp.pad(jnp.transpose(gains.astype(jnp.bfloat16)), ((0, 0), (0, 126)))
    inward_gains = lax.all_gather(
        jnp.concatenate([low_inward, low_gains], axis=1), ("seq", "fsdp"), axis=0, tiled=True
    )
    inward_full = inward_gains[:, :inward_cols]
    gain_first = inward_gains[:, inward_cols].astype(jnp.float32)
    gain_second = inward_gains[:, inward_cols + 1].astype(jnp.float32)
    outward_full = lax.all_gather(
        w_outward.astype(jnp.bfloat16), ("seq", "fsdp"), axis=0, tiled=True
    )

    low_feed = jnp.concatenate(
        [
            w_gate_up.astype(jnp.bfloat16).reshape(depth, 2, slices, ff_cols),
            w_down.astype(jnp.bfloat16).reshape(depth, 1, slices, ff_cols),
        ],
        axis=1,
    )
    low_feed = low_feed.transpose(2, 0, 1, 3).reshape(slices, depth, 3 * ff_cols)
    low_feed = lax.all_to_all(low_feed, "fsdp", 0, 0, tiled=True).reshape(
        slices * depth, 3 * ff_cols
    )
    gate_up_slice = lax.all_gather(low_feed[:, : 2 * ff_cols], "seq", axis=0, tiled=True)
    down_slice = lax.all_gather(low_feed[:, 2 * ff_cols :], "seq", axis=0, tiled=True)

    scale_first = rms_scale(rows)
    normed = (rows * scale_first * gain_first).astype(jnp.bfloat16)
    mixed = dot(normed, inward_full)
    query = rotate(mixed[:, :D].reshape(local, HEADS, HEAD_DIM), position, 1.0).astype(jnp.bfloat16)
    key = rotate(
        mixed[:, D : D + kv_width].reshape(local, KV_HEADS, HEAD_DIM), position, 1.0
    ).astype(jnp.bfloat16)
    value = mixed[:, D + kv_width :].reshape(local, KV_HEADS, HEAD_DIM).astype(jnp.bfloat16)
    packed = jnp.concatenate(
        [
            query.reshape(local, group, head_cols),
            jnp.repeat(key, copies, axis=1),
            jnp.repeat(value, copies, axis=1),
        ],
        axis=-1,
    ).transpose(1, 0, 2)
    arrived = lax.all_to_all(packed, "seq", 0, 0, tiled=True)
    length = group * local
    arrived = arrived.reshape(length, head_cols + 2 * HEAD_DIM)
    block = min(512, length)
    mixed_here, logs = attend_forward(arrived, heads_here, block)
    attended = lax.all_to_all(
        mixed_here.reshape(group, local, head_cols), "seq", 0, 0, tiled=True
    )
    attended = attended.transpose(1, 0, 2).reshape(local, D)
    middle = rows + dot(attended, outward_full)
    scale_second = rms_scale(middle)
    normed_second = (middle * scale_second * gain_second).astype(jnp.bfloat16)

    upstream_blocks = gather_swap(upstream, "fsdp")
    upstream_all = jnp.concatenate(upstream_blocks, axis=0)
    normed_all = jnp.concatenate(gather_swap(normed_second, "fsdp"), axis=0)
    gate_up = dot(normed_all, gate_up_slice)
    gate = gate_up[:, :ff_cols]
    up_part = gate_up[:, ff_cols:]
    sigmoid = jax.nn.sigmoid(gate)
    hidden = (gate * sigmoid * up_part).astype(jnp.bfloat16)
    hidden_grad = dot(upstream_all, down_slice)
    gate_grad = hidden_grad * up_part * sigmoid * (1.0 + gate * (1.0 - sigmoid))
    up_grad = hidden_grad * gate * sigmoid
    gate_up_grad = jnp.concatenate([gate_grad, up_grad], axis=-1).astype(jnp.bfloat16)

    def send_back(part):
        part = part.astype(jnp.bfloat16)
        return reduce_swap(
            [part[d * local : (d + 1) * local] for d in range(slices)], "fsdp"
        )

    normed_second_grad = send_back(against(gate_up_grad, gate_up_slice))
    result = middle + send_back(against(hidden, down_slice))
    down_back = return_columns(outer(upstream_all, hidden).astype(jnp.bfloat16))
    gate_up_back = return_columns(outer(normed_all, gate_up_grad).astype(jnp.bfloat16))

    middle_back, gain_second_grad = norm_back(middle, scale_second, gain_second, normed_second_grad)
    middle_grad = upstream.astype(jnp.float32) + middle_back
    branch_low = middle_grad.astype(jnp.bfloat16)
    attended_grad = against(branch_low, outward_full).astype(jnp.bfloat16)
    grad_here = lax.all_to_all(
        attended_grad.reshape(local, group, head_cols).transpose(1, 0, 2), "seq", 0, 0, tiled=True
    ).reshape(length, head_cols)
    query_part, kv_part = attend_backward(arrived, grad_here, mixed_here, logs, heads_here, block)
    back = lax.all_to_all(
        jnp.concatenate([query_part, kv_part], axis=-1).reshape(group, local, -1),
        "seq",
        0,
        0,
        tiled=True,
    ).astype(jnp.float32)
    query_grad = rotate(
        back[:, :, :head_cols].transpose(1, 0, 2).reshape(local, HEADS, HEAD_DIM), position, -1.0
    )

    def sum_copies(field):
        field = field.reshape(KV_HEADS, copies, local, HEAD_DIM)
        return jnp.sum(field, axis=1).transpose(1, 0, 2)

    key_grad = rotate(
        sum_copies(back[:, :, head_cols : head_cols + HEAD_DIM]), position, -1.0
    )
    value_grad = sum_copies(back[:, :, head_cols + HEAD_DIM :])
    inward_grad = jnp.concatenate(
        [
            query_grad.reshape(local, D),
            key_grad.reshape(local, kv_width),
            value_grad.reshape(local, kv_width),
        ],
        axis=-1,
    ).astype(jnp.bfloat16)
    normed_grad = against(inward_grad, inward_full)
    rows_back, gain_first_grad = norm_back(rows, scale_first, gain_first, normed_grad)
    input_grad = middle_grad + rows_back

    def column_slices(field):
        width = field.shape[1] // slices
        return field.reshape(local, slices, width).transpose(1, 0, 2)

    attended_all = jnp.concatenate(gather_swap(attended, "fsdp"), axis=0)
    branch_all = jnp.concatenate(exchange_swap(column_slices(branch_low), "fsdp"), axis=0)
    outward_back = return_columns(outer(attended_all, branch_all).astype(jnp.bfloat16))
    first_all = jnp.concatenate(gather_swap(normed, "fsdp"), axis=0)
    inward_grad_all = jnp.concatenate(exchange_swap(column_slices(inward_grad), "fsdp"), axis=0)
    inward_back = return_columns(outer(first_all, inward_grad_all).astype(jnp.bfloat16))

    gain_grads = jnp.stack([gain_first_grad, gain_second_grad], axis=1)
    gains_sum = jnp.transpose(
        lax.psum_scatter(gain_grads, ("seq", "fsdp"), scatter_dimension=0, tiled=True)
    )
    inward_sum = jnp.concatenate(inward_back, axis=1).astype(jnp.float32)
    outward_sum = jnp.concatenate(outward_back, axis=1).astype(jnp.float32)
    gate_up_sum = jnp.concatenate(
        [piece[:, :ff_cols] for piece in gate_up_back]
        + [piece[:, ff_cols:] for piece in gate_up_back],
        axis=1,
    ).astype(jnp.float32)
    down_sum = jnp.concatenate(down_back, axis=1).astype(jnp.float32)
    first_inward_new, second_inward_new, inward_new = adam_update(
        w_inward, first_inward, second_inward, inward_sum, 0.02, weight_decay
    )
    first_outward_new, second_outward_new, outward_new = adam_update(
        w_outward, first_outward, second_outward, outward_sum, 0.15, weight_decay
    )
    first_gate_up_new, second_gate_up_new, gate_up_new = adam_update(
        w_gate_up, first_gate_up, second_gate_up, gate_up_sum, 0.02, weight_decay
    )
    first_down_new, second_down_new, down_new = adam_update(
        w_down, first_down, second_down, down_sum, 0.015, weight_decay
    )
    first_gains_new, second_gains_new, gains_new = adam_update(
        gains, first_gains, second_gains, gains_sum, 0.6, 0.0
    )
    return (
        result[None].astype(jnp.bfloat16),
        input_grad[None],
        first_inward_new,
        second_inward_new,
        inward_new,
        first_outward_new,
        second_outward_new,
        outward_new,
        first_gate_up_new,
        second_gate_up_new,
        gate_up_new,
        first_down_new,
        second_down_new,
        down_new,
        first_gains_new,
        second_gains_new,
        gains_new,
    )


def solution(mesh):
    in_specs = (
        P("fsdp", "seq", None),
        P("fsdp", "seq", None),
        P(("seq", "fsdp"), None),
        P(("seq", "fsdp"), None),
        P(("seq", "fsdp"), None),
        P(("seq", "fsdp"), None),
        P(None, ("seq", "fsdp")),
        P(("seq", "fsdp"), None),
        P(("seq", "fsdp"), None),
        P(("seq", "fsdp"), None),
        P(("seq", "fsdp"), None),
        P(None, ("seq", "fsdp")),
        P(("seq", "fsdp"), None),
        P(("seq", "fsdp"), None),
        P(("seq", "fsdp"), None),
        P(("seq", "fsdp"), None),
        P(None, ("seq", "fsdp")),
    )
    out_specs = (
        P("fsdp", "seq", None),
        P("fsdp", "seq", None),
        P(("seq", "fsdp"), None),
        P(("seq", "fsdp"), None),
        P(("seq", "fsdp"), None),
        P(("seq", "fsdp"), None),
        P(("seq", "fsdp"), None),
        P(("seq", "fsdp"), None),
        P(("seq", "fsdp"), None),
        P(("seq", "fsdp"), None),
        P(("seq", "fsdp"), None),
        P(("seq", "fsdp"), None),
        P(("seq", "fsdp"), None),
        P(("seq", "fsdp"), None),
        P(None, ("seq", "fsdp")),
        P(None, ("seq", "fsdp")),
        P(None, ("seq", "fsdp")),
    )
    return jax.shard_map(body, mesh=mesh, in_specs=in_specs, out_specs=out_specs, check_vma=False)
```

```python
import functools

import jax
import jax.numpy as jnp
from jax import lax
from jax.experimental import pallas as pl
from jax.experimental.pallas import tpu as pltpu
from jax.sharding import PartitionSpec as P

D = 2048
FF = 5632
HEADS = 32
KV_HEADS = 4
HEAD_DIM = 64
STEP = 10


epsilon = 1e-05
adam_epsilon = 1e-08
beta_first = 0.9
beta_second = 0.95
rope_base = 10000.0
weight_decay = 0.1
masked_value = -1e30


def rotate(field, position, sign):
    half = field.shape[-1] // 2
    exponent = jnp.arange(half).astype(jnp.float32) * (-2.0 / field.shape[-1])
    frequency = jnp.power(rope_base, exponent)
    angle = position[:, None] * frequency[None, :]
    cosine = jnp.cos(angle)[:, None, :]
    sine = sign * jnp.sin(angle)[:, None, :]
    first = field[..., :half]
    second = field[..., half:]
    return jnp.concatenate(
        [first * cosine - second * sine, second * cosine + first * sine], axis=-1
    )


def rms_scale(rows):
    return lax.rsqrt(jnp.mean(rows * rows, axis=-1, keepdims=True) + epsilon)


def norm_back(rows, scale_rows, gain, grad):
    weighted = grad * gain
    row_grad = scale_rows * weighted - rows * scale_rows**3 * jnp.mean(
        weighted * rows, axis=-1, keepdims=True
    )
    gain_grad = jnp.sum(grad * rows * scale_rows, axis=0)
    return (row_grad, gain_grad)


def dot(left, right):
    return jnp.dot(left, right, preferred_element_type=jnp.float32)


def outer(left, right):
    return lax.dot_general(
        left, right, (((0,), (0,)), ((), ())), preferred_element_type=jnp.float32
    )


def against(left, right):
    return lax.dot_general(
        left, right, (((1,), (1,)), ((), ())), preferred_element_type=jnp.float32
    )


def stack_heads(field, heads):
    return jnp.concatenate(
        [field[:, h * HEAD_DIM : (h + 1) * HEAD_DIM] for h in range(heads)], axis=0
    )


def unstack_heads(field, heads):
    rows = field.shape[0] // heads
    return jnp.concatenate([field[h * rows : (h + 1) * rows] for h in range(heads)], axis=1)


def masked_scores(keys, queries, block):
    scores = against(keys, queries)
    key_place = lax.broadcasted_iota(jnp.int32, scores.shape, 0)
    query_place = lax.rem(lax.broadcasted_iota(jnp.int32, scores.shape, 1), block)
    return jnp.where(key_place <= query_place, scores, masked_value)


def remote(source, target, send, arrive, axis, device):
    return pltpu.make_async_remote_copy(
        src_ref=source,
        dst_ref=target,
        send_sem=send,
        recv_sem=arrive,
        device_id={axis: device},
        device_id_type=pl.DeviceIdType.MESH,
    )


VMEM = pl.BlockSpec(memory_space=pltpu.VMEM)


def core_pair(index):
    return index // 2, lax.rem(index, 2)


def share_kernel(
    in_ref, gain_ref, out_ref, gate_up_ref, down_ref,
    feed_gate, feed_up, feed_down, in_rows, out_rows,
    low_gate, low_up, low_down,
    send_feed, come_feed, send_in, come_in, send_out, come_out,
    pass_in, passed_in, pass_out, passed_out,
):
    group, slices = lax.axis_size("seq"), lax.axis_size("fsdp")
    s, f = lax.axis_index("seq"), lax.axis_index("fsdp")
    pair, core = core_pair(s)
    depth, inward_cols = in_ref.shape
    ff_cols = FF // slices
    in_rows[pair, core, :, pl.ds(0, inward_cols)] = in_ref[...].astype(jnp.bfloat16)
    in_rows[pair, core, :, pl.ds(inward_cols, 128)] = gain_ref[...]
    out_rows[pair, core] = out_ref[...].astype(jnp.bfloat16)
    for t in range(slices):
        columns = pl.ds(t * ff_cols, ff_cols)
        low_gate[t] = gate_up_ref[:, columns].astype(jnp.bfloat16)
        low_up[t] = gate_up_ref[:, pl.ds(FF + t * ff_cols, ff_cols)].astype(jnp.bfloat16)
        low_down[t] = down_ref[:, columns].astype(jnp.bfloat16)

    barrier = pltpu.get_barrier_semaphore()
    near = [1] + list(range(2, group, 2))
    for d in near:
        pl.semaphore_signal(
            barrier, inc=1, device_id={"seq": s ^ d}, device_id_type=pl.DeviceIdType.MESH
        )
    for d in range(1, slices):
        pl.semaphore_signal(
            barrier, inc=1, device_id={"fsdp": f ^ d}, device_id_type=pl.DeviceIdType.MESH
        )
    pl.semaphore_wait(barrier, len(near) + slices - 1)

    feeds = ((low_gate, feed_gate), (low_up, feed_up), (low_down, feed_down))

    def feed_copy(k, d, owner, target):
        low, feed = feeds[k]
        return remote(
            low.at[target],
            feed.at[pl.ds(pl.multiple_of(owner * depth, depth), depth), :],
            send_feed.at[k, d], come_feed.at[k, d], "fsdp", target,
        )

    def row_copy(rows, send, come, d, owner, target):
        place, half = core_pair(owner)
        return remote(
            rows.at[place, half], rows.at[place, half], send.at[d], come.at[d], "seq", target
        )

    for d in near:
        row_copy(in_rows, send_in, come_in, d, s, s ^ d).start()
    for d in near:
        row_copy(out_rows, send_out, come_out, d, s, s ^ d).start()
    for d in range(1, slices):
        for k in range(3):
            feed_copy(k, d, f, f ^ d).start()
    mine = pl.ds(pl.multiple_of(f * depth, depth), depth)
    for low, feed in feeds:
        feed[mine, :] = low[f]
    for d in near[1:]:
        row_copy(in_rows, send_in, come_in, d, s ^ d, s ^ d).wait_recv()
        row_copy(in_rows, pass_in, passed_in, d, s ^ d, s ^ 1).start()
    for d in near[1:]:
        row_copy(out_rows, send_out, come_out, d, s ^ d, s ^ d).wait_recv()
        row_copy(out_rows, pass_out, passed_out, d, s ^ d, s ^ 1).start()
    for rows, send, come, forward, passed in (
        (in_rows, send_in, come_in, pass_in, passed_in),
        (out_rows, send_out, come_out, pass_out, passed_out),
    ):
        row_copy(rows, send, come, 1, s ^ 1, s ^ 1).wait()
        for d in near[1:]:
            row_copy(rows, send, come, d, s, s ^ d).wait_send()
            row_copy(rows, forward, passed, d, s ^ d, s ^ 1).wait_send()
            row_copy(rows, forward, passed, d, s ^ 1 ^ d, s ^ 1).wait_recv()
    for d in range(1, slices):
        for k in range(3):
            feed_copy(k, d, f ^ d, f ^ d).wait()


def share_weights(w_inward, gain_columns, w_outward, w_gate_up, w_down, group, slices):
    depth = w_inward.shape[0]
    ff_cols = FF // slices
    feed = jax.ShapeDtypeStruct((slices * depth, ff_cols), jnp.bfloat16)
    low = pltpu.VMEM((slices, depth, ff_cols), jnp.bfloat16)
    rows = lambda width: jax.ShapeDtypeStruct((group // 2, 2, depth, width), jnp.bfloat16)
    sems = [pltpu.SemaphoreType.DMA((3, slices))] * 2 + [pltpu.SemaphoreType.DMA((group,))] * 8
    return pl.pallas_call(
        share_kernel,
        in_specs=[VMEM] * 5,
        out_specs=[VMEM] * 5,
        out_shape=[feed, feed, feed, rows(w_inward.shape[1] + 128), rows(w_outward.shape[1])],
        scratch_shapes=[low, low, low] + sems,
        compiler_params=pltpu.CompilerParams(
            vmem_limit_bytes=48 << 20, collective_id=2, has_side_effects=True
        ),
    )(w_inward, gain_columns, w_outward, w_gate_up, w_down)


def spread_copies(rows, full, send, come, forward, passed):
    s, f = lax.axis_index("seq"), lax.axis_index("fsdp")
    core = lax.rem(s, 2)
    slices = lax.axis_size("fsdp")

    def first(d, owner, target):
        return remote(
            rows.at[:, core], full.at[:, core, owner], send.at[d], come.at[d], "fsdp", target
        )

    def second(d, half):
        block = full.at[:, half, f ^ d]
        return remote(block, block, forward.at[d], passed.at[d], "seq", s ^ 1)

    def start():
        for d in range(1, slices):
            first(d, f, f ^ d).start()

    def local():
        full[:, :, f] = rows[...]

    def finish():
        for d in range(1, slices):
            first(d, f ^ d, f ^ d).wait_recv()
            second(d, core).start()
        for d in range(1, slices):
            first(d, f, f ^ d).wait_send()
            second(d, core).wait_send()
            second(d, 1 - core).wait_recv()

    return start, local, finish


def meet_spread(extra=()):
    barrier = pltpu.get_barrier_semaphore()
    s, f = lax.axis_index("seq"), lax.axis_index("fsdp")
    near = sorted({1, *extra})
    slices = lax.axis_size("fsdp")
    for d in near:
        pl.semaphore_signal(
            barrier, inc=1, device_id={"seq": s ^ d}, device_id_type=pl.DeviceIdType.MESH
        )
    for d in range(1, slices):
        pl.semaphore_signal(
            barrier, inc=1, device_id={"fsdp": f ^ d}, device_id_type=pl.DeviceIdType.MESH
        )
    pl.semaphore_wait(barrier, len(near) + slices - 1)


def spread_kernel(rows, full, send, come, forward, passed):
    meet_spread()
    start, local, finish = spread_copies(rows, full, send, come, forward, passed)
    start()
    local()
    finish()


def spread_rows(rows, slices):
    pairs, two, depth, width = rows.shape
    full = pl.pallas_call(
        spread_kernel,
        in_specs=[VMEM],
        out_specs=VMEM,
        out_shape=jax.ShapeDtypeStruct((pairs, two, slices, depth, width), rows.dtype),
        scratch_shapes=[pltpu.SemaphoreType.DMA((slices,))] * 4,
        compiler_params=pltpu.CompilerParams(
            vmem_limit_bytes=48 << 20, collective_id=3, has_side_effects=True
        ),
    )(rows)
    return full.reshape(pairs * two * slices * depth, width)


def forward_kernel(
    query_ref, kv_ref, out_rows, query_here, kv_here, mixed_here, logs, attended, out_full,
    send_query, come_query, send_kv, come_kv, send_out, come_out, local_sem,
    send_rows, come_rows, pass_rows, passed_rows, *, heads, block
):
    group = lax.axis_size("seq")
    me = lax.axis_index("seq")
    local, width = query_ref.shape[0], heads * HEAD_DIM
    pair = 2 * HEAD_DIM
    copies = group // KV_HEADS
    length = group * local
    per_block = block // local
    meet_spread(range(1, group))
    spread_start, spread_local, spread_finish = spread_copies(
        out_rows, out_full, send_rows, come_rows, pass_rows, passed_rows
    )

    def query_copy(d, owner, target):
        return remote(
            query_ref.at[:, pl.ds(pl.multiple_of(target * width, 128), width)],
            query_here.at[pl.ds(pl.multiple_of(owner * local, local), local), :],
            send_query.at[d], come_query.at[d], "seq", target,
        )

    def kv_copy(d, owner, target):
        return remote(
            kv_ref.at[:, pl.ds(pl.multiple_of(target // copies * pair, 128), pair)],
            kv_here.at[pl.ds(pl.multiple_of(owner * local, local), local), :],
            send_kv.at[d], come_kv.at[d], "seq", target,
        )

    def out_copy(d, owner, target):
        return remote(
            mixed_here.at[pl.ds(pl.multiple_of(target * local, local), local), :],
            attended.at[:, pl.ds(pl.multiple_of(owner * width, 128), width)],
            send_out.at[d], come_out.at[d], "seq", target,
        )

    for d in range(1, group):
        kv_copy(d, me, me ^ d).start()
        query_copy(d, me, me ^ d).start()
    spread_start()
    mine = pl.ds(pl.multiple_of(me * local, local), local)
    own_columns = pl.ds(pl.multiple_of(me * width, 128), width)
    own_query = pltpu.make_async_copy(
        query_ref.at[:, own_columns], query_here.at[mine, :], local_sem.at[0]
    )
    own_kv = pltpu.make_async_copy(
        kv_ref.at[:, pl.ds(pl.multiple_of(me // copies * pair, 128), pair)],
        kv_here.at[mine, :],
        local_sem.at[1],
    )
    own_query.start()
    own_kv.start()
    spread_local()
    own_query.wait()
    own_kv.wait()

    def query_block(index, _):
        for part in range(per_block):
            source = index * per_block + part

            @pl.when(source != me)
            def _():
                kv_copy(source ^ me, source, source).wait_recv()
                query_copy(source ^ me, source, source).wait_recv()

        place = pl.ds(pl.multiple_of(index * block, block), block)
        queries = stack_heads(query_here[place, :], heads) * jnp.bfloat16(HEAD_DIM**-0.5)
        columns = heads * block

        def step(j, carry, masked):
            largest, total, mixed = carry
            start = pl.multiple_of(j * block, block)
            kv = kv_here[pl.ds(start, block), :]
            keys, values = kv[:, :HEAD_DIM], kv[:, HEAD_DIM:]
            if masked:
                scores = masked_scores(keys, queries, block)
            else:
                scores = against(keys, queries)
            new = jnp.maximum(largest, jnp.max(scores, axis=0, keepdims=True))
            fade = jnp.exp(largest - new)
            weights = jnp.exp(scores - new)
            total = total * fade + jnp.sum(weights, axis=0, keepdims=True)
            mixed = mixed * fade + outer(values, weights.astype(jnp.bfloat16))
            return new, total, mixed

        carry = (
            jnp.full((1, columns), masked_value, jnp.float32),
            jnp.zeros((1, columns), jnp.float32),
            jnp.zeros((HEAD_DIM, columns), jnp.float32),
        )
        carry = lax.fori_loop(0, index, lambda j, c: step(j, c, False), carry)
        largest, total, mixed = step(index, carry, True)
        logs[index] = largest + jnp.log(total)
        mixed_here[place, :] = unstack_heads((mixed / total).T, heads).astype(mixed_here.dtype)
        for part in range(per_block):
            target = index * per_block + part

            @pl.when(target != me)
            def _():
                out_copy(target ^ me, me, target).start()

        return 0

    lax.fori_loop(0, length // block, query_block, 0)
    own_out = pltpu.make_async_copy(
        mixed_here.at[mine, :], attended.at[:, own_columns], local_sem.at[0]
    )
    own_out.start()
    own_out.wait()
    spread_finish()
    for d in range(1, group):
        other = me ^ d
        kv_copy(d, me, other).wait_send()
        query_copy(d, me, other).wait_send()
        out_copy(d, other, other).wait()


def backward_kernel(
    grad_ref, query_here, kv_here, mixed_here, logs, query_back, kv_back,
    grad_here, query_grad, kv_grad, key_sum, value_sum,
    send_grad, come_grad, send_query, come_query, send_kv, come_kv, local_sem, *, heads, block
):
    group = lax.axis_size("seq")
    me = lax.axis_index("seq")
    local, width = grad_ref.shape[0], heads * HEAD_DIM
    length = group * local
    per_block = block // local
    blocks = length // block
    scale = HEAD_DIM**-0.5
    barrier = pltpu.get_barrier_semaphore()
    for d in range(1, group):
        pl.semaphore_signal(
            barrier, inc=1, device_id={"seq": me ^ d}, device_id_type=pl.DeviceIdType.MESH
        )
    pl.semaphore_wait(barrier, group - 1)

    def grad_copy(d, owner, target):
        return remote(
            grad_ref.at[:, pl.ds(pl.multiple_of(target * width, 128), width)],
            grad_here.at[pl.ds(pl.multiple_of(owner * local, local), local), :],
            send_grad.at[d], come_grad.at[d], "seq", target,
        )

    def query_copy(d, owner, target):
        return remote(
            query_grad.at[pl.ds(pl.multiple_of(target * local, local), local), :],
            query_back.at[:, pl.ds(pl.multiple_of(owner * width, 128), width)],
            send_query.at[d], come_query.at[d], "seq", target,
        )

    def kv_copy(d, owner, target):
        return remote(
            kv_grad.at[pl.ds(pl.multiple_of(target * local, local), local), :],
            kv_back.at[owner],
            send_kv.at[d], come_kv.at[d], "seq", target,
        )

    for d in range(1, group):
        grad_copy(d, me, me ^ d).start()
    mine = pl.ds(pl.multiple_of(me * local, local), local)
    own_columns = pl.ds(pl.multiple_of(me * width, 128), width)
    own_grad = pltpu.make_async_copy(
        grad_ref.at[:, own_columns], grad_here.at[mine, :], local_sem.at[0]
    )
    own_grad.start()
    own_grad.wait()
    key_sum[...] = jnp.zeros_like(key_sum)
    value_sum[...] = jnp.zeros_like(value_sum)

    def query_block(turn, _):
        index = blocks - 1 - turn
        for part in range(per_block):
            source = index * per_block + part

            @pl.when(source != me)
            def _():
                grad_copy(source ^ me, source, source).wait_recv()

        place = pl.ds(pl.multiple_of(index * block, block), block)
        queries = stack_heads(query_here[place, :], heads) * jnp.bfloat16(scale)
        grads = stack_heads(grad_here[place, :], heads)
        mixed = stack_heads(mixed_here[place, :], heads)
        inner = jnp.sum(
            (grads.astype(jnp.float32) * mixed.astype(jnp.float32)).T, axis=0, keepdims=True
        )
        log_total = logs[index]

        def step(j, total, masked):
            start = pl.multiple_of(j * block, block)
            rows = pl.ds(start, block)
            kv = kv_here[rows, :]
            keys, values = kv[:, :HEAD_DIM], kv[:, HEAD_DIM:]
            if masked:
                scores = masked_scores(keys, queries, block)
            else:
                scores = against(keys, queries)
            shares = jnp.exp(scores - log_total)
            share_grad = against(values, grads)
            score_grad = (shares * (share_grad - inner)).astype(jnp.bfloat16)
            value_sum[rows, :] += dot(shares.astype(jnp.bfloat16), grads)
            key_sum[rows, :] += dot(score_grad, queries)
            return total + outer(keys, score_grad)

        total = lax.fori_loop(
            0,
            index,
            lambda j, c: step(j, c, False),
            jnp.zeros((HEAD_DIM, heads * block), jnp.float32),
        )
        total = step(index, total, True)
        query_grad[place, :] = unstack_heads((total * scale).T, heads).astype(jnp.bfloat16)
        kv_grad[place, :] = jnp.concatenate(
            [key_sum[place, :], value_sum[place, :]], axis=1
        ).astype(jnp.bfloat16)
        for part in range(per_block):
            target = index * per_block + part

            @pl.when(target != me)
            def _():
                query_copy(target ^ me, me, target).start()
                kv_copy(target ^ me, me, target).start()

        return 0

    lax.fori_loop(0, blocks, query_block, 0)
    own_query = pltpu.make_async_copy(
        query_grad.at[mine, :], query_back.at[:, own_columns], local_sem.at[0]
    )
    own_kv = pltpu.make_async_copy(kv_grad.at[mine, :], kv_back.at[me], local_sem.at[1])
    own_query.start()
    own_kv.start()
    own_query.wait()
    own_kv.wait()
    for d in range(1, group):
        other = me ^ d
        grad_copy(d, me, other).wait_send()
        query_copy(d, other, other).wait()
        kv_copy(d, other, other).wait()


def attend_forward(query, kv, out_rows, group, slices, heads, block):
    local, width = query.shape[0], heads * HEAD_DIM
    length = group * local
    pairs = heads * length * length // 2
    sems = pltpu.SemaphoreType.DMA((group,))
    pairs_seq, _, depth, _ = out_rows.shape
    return pl.pallas_call(
        functools.partial(forward_kernel, heads=heads, block=block),
        in_specs=[VMEM] * 3,
        out_specs=[VMEM] * 6,
        out_shape=[
            jax.ShapeDtypeStruct((length, width), jnp.bfloat16),
            jax.ShapeDtypeStruct((length, 2 * HEAD_DIM), jnp.bfloat16),
            jax.ShapeDtypeStruct((length, width), jnp.bfloat16),
            jax.ShapeDtypeStruct((length // block, 1, heads * block), jnp.float32),
            jax.ShapeDtypeStruct((local, group * width), jnp.bfloat16),
            jax.ShapeDtypeStruct(
                (pairs_seq, 2, slices, depth, out_rows.shape[3]), jnp.bfloat16
            ),
        ],
        scratch_shapes=[sems] * 6
        + [pltpu.SemaphoreType.DMA((2,))]
        + [pltpu.SemaphoreType.DMA((slices,))] * 4,
        compiler_params=pltpu.CompilerParams(
            vmem_limit_bytes=48 << 20, collective_id=0, has_side_effects=True
        ),
        cost_estimate=pl.CostEstimate(
            flops=pairs * HEAD_DIM * 60, bytes_accessed=length * 4 * width, transcendentals=pairs
        ),
    )(query, kv, out_rows)


def attend_backward(grads, query_here, kv_here, mixed_here, logs, group, heads, block):
    local, width = grads.shape[0], heads * HEAD_DIM
    length = group * local
    pairs = heads * length * length // 2
    sems = pltpu.SemaphoreType.DMA((group,))
    return pl.pallas_call(
        functools.partial(backward_kernel, heads=heads, block=block),
        in_specs=[VMEM] * 5,
        out_specs=[VMEM] * 2,
        out_shape=[
            jax.ShapeDtypeStruct((local, group * width), jnp.bfloat16),
            jax.ShapeDtypeStruct((group, local, 2 * HEAD_DIM), jnp.bfloat16),
        ],
        scratch_shapes=[
            pltpu.VMEM((length, width), jnp.bfloat16),
            pltpu.VMEM((length, width), jnp.bfloat16),
            pltpu.VMEM((length, 2 * HEAD_DIM), jnp.bfloat16),
            pltpu.VMEM((length, HEAD_DIM), jnp.float32),
            pltpu.VMEM((length, HEAD_DIM), jnp.float32),
        ]
        + [sems] * 6
        + [pltpu.SemaphoreType.DMA((2,))],
        compiler_params=pltpu.CompilerParams(
            vmem_limit_bytes=48 << 20, collective_id=1, has_side_effects=True
        ),
        cost_estimate=pl.CostEstimate(
            flops=pairs * HEAD_DIM * 4, bytes_accessed=length * 8 * width, transcendentals=pairs
        ),
    )(grads, query_here, kv_here, mixed_here, logs)


def swap(piece, axis, offset):
    size = lax.axis_size(axis)
    return lax.ppermute(piece, axis, [(i, i ^ offset) for i in range(size)])


def gather_swap(piece, axis):
    return [piece] + [swap(piece, axis, d) for d in range(1, lax.axis_size(axis))]


def exchange_swap(stack, axis):
    me = lax.axis_index(axis)
    pieces = [
        lax.dynamic_index_in_dim(stack, me ^ d, 0, keepdims=False)
        for d in range(lax.axis_size(axis))
    ]
    return [pieces[0]] + [swap(p, axis, d) for d, p in enumerate(pieces) if d]


def reduce_swap(parts, axis):
    total = parts[0].astype(jnp.float32)
    for d in range(1, len(parts)):
        total = total + swap(parts[d], axis, d).astype(jnp.float32)
    return total


def in_order(pieces, axis):
    me = lax.axis_index(axis)
    stack = jnp.stack(pieces)
    return [
        lax.dynamic_index_in_dim(stack, j ^ me, 0, keepdims=False) for j in range(len(pieces))
    ]


def scatter_rows(partial, after=()):
    partial, *_ = lax.optimization_barrier((partial, *after))
    return lax.psum_scatter(partial, "seq", scatter_dimension=0, tiled=True)


def return_columns(mine):
    size = lax.axis_size("fsdp")
    stack = mine.reshape(size, mine.shape[0] // size, mine.shape[1])
    return in_order(exchange_swap(stack, "fsdp"), "fsdp")


def adam_update(weight, first, second, grad, rate, decay):
    first_new = beta_first * first + (1.0 - beta_first) * grad
    second_new = beta_second * second + (1.0 - beta_second) * grad * grad
    first_hat = first_new / (1.0 - beta_first**STEP)
    second_hat = second_new / (1.0 - beta_second**STEP)
    weight_new = weight - rate * (
        first_hat / (jnp.sqrt(second_hat) + adam_epsilon) + decay * weight
    )
    return (first_new, second_new, weight_new)


def body(
    inputs,
    cotangent,
    w_inward,
    w_outward,
    w_gate_up,
    w_down,
    gains,
    first_inward,
    first_outward,
    first_gate_up,
    first_down,
    first_gains,
    second_inward,
    second_outward,
    second_gate_up,
    second_down,
    second_gains,
):
    rows = inputs[0].astype(jnp.float32)
    upstream = cotangent[0]
    local = rows.shape[0]
    group = lax.axis_size("seq")
    slices = lax.axis_size("fsdp")
    heads_here = HEADS // group
    copies = group // KV_HEADS
    kv_width = KV_HEADS * HEAD_DIM
    head_cols = heads_here * HEAD_DIM
    inward_cols = D + 2 * kv_width
    ff_cols = FF // slices
    depth = w_inward.shape[0]
    position = (lax.axis_index("seq") * local + jnp.arange(local)).astype(jnp.float32)

    low_gains = jnp.pad(jnp.transpose(gains.astype(jnp.bfloat16)), ((0, 0), (0, 126)))
    feed_gate, feed_up, feed_down, in_rows, out_rows = share_weights(
        w_inward, low_gains, w_outward, w_gate_up, w_down, group, slices
    )
    gate_slice = lax.all_gather(feed_gate, "seq", axis=0, tiled=True)
    up_slice = lax.all_gather(feed_up, "seq", axis=0, tiled=True)
    down_slice = lax.all_gather(feed_down, "seq", axis=0, tiled=True)
    inward_gains = spread_rows(in_rows, slices)
    inward_full = inward_gains[:, :inward_cols]
    gain_first = inward_gains[:, inward_cols].astype(jnp.float32)
    gain_second = inward_gains[:, inward_cols + 1].astype(jnp.float32)

    scale_first = rms_scale(rows)
    normed = (rows * scale_first * gain_first).astype(jnp.bfloat16)
    mixed = dot(normed, inward_full)
    query = rotate(mixed[:, :D].reshape(local, HEADS, HEAD_DIM), position, 1.0).astype(jnp.bfloat16)
    key = rotate(
        mixed[:, D : D + kv_width].reshape(local, KV_HEADS, HEAD_DIM), position, 1.0
    ).astype(jnp.bfloat16)
    value = mixed[:, D + kv_width :].reshape(local, KV_HEADS, HEAD_DIM).astype(jnp.bfloat16)
    kv = jnp.concatenate([key, value], axis=-1).reshape(local, 2 * kv_width)
    length = group * local
    block = min(512, length)
    query_here, kv_here, mixed_here, logs, attended, outward_full = attend_forward(
        query.reshape(local, D), kv, out_rows, group, slices, heads_here, block
    )
    outward_full = outward_full.reshape(D, D)
    upstream_blocks = gather_swap(upstream, "fsdp")
    attended, upstream_blocks = lax.optimization_barrier((attended, upstream_blocks))
    upstream_all = jnp.concatenate(upstream_blocks, axis=0)
    middle = rows + dot(attended, outward_full)
    scale_second = rms_scale(middle)
    normed_second = (middle * scale_second * gain_second).astype(jnp.bfloat16)

    normed_all = jnp.concatenate(gather_swap(normed_second, "fsdp"), axis=0)
    gate = dot(normed_all, gate_slice)
    up_part = dot(normed_all, up_slice)
    sigmoid = jax.nn.sigmoid(gate)
    hidden = (gate * sigmoid * up_part).astype(jnp.bfloat16)
    down_partial = outer(upstream_all, hidden).astype(jnp.bfloat16)
    upstream_late, down_partial = lax.optimization_barrier((upstream_all, down_partial))
    hidden_grad = dot(upstream_late, down_slice)
    gate_grad = hidden_grad * up_part * sigmoid * (1.0 + gate * (1.0 - sigmoid))
    gate_grad = gate_grad.astype(jnp.bfloat16)
    up_grad = (hidden_grad * gate * sigmoid).astype(jnp.bfloat16)

    def send_back(part):
        part = part.astype(jnp.bfloat16)
        parts = [part[d * local : (d + 1) * local] for d in range(slices)]
        return [parts[0]] + [swap(p, "fsdp", d) for d, p in enumerate(parts) if d]

    def add_up(parts):
        return functools.reduce(jnp.add, [p.astype(jnp.float32) for p in parts])

    back_parts = send_back(against(gate_grad, gate_slice) + against(up_grad, up_slice))
    attended_blocks = gather_swap(attended, "fsdp")
    gate_grad, attended_blocks = lax.optimization_barrier((gate_grad, attended_blocks))
    gate_partial = outer(normed_all, gate_grad).astype(jnp.bfloat16)
    up_partial = outer(normed_all, up_grad).astype(jnp.bfloat16)
    back_parts, hidden, gate_partial, up_partial = lax.optimization_barrier(
        (back_parts, hidden, gate_partial, up_partial)
    )
    normed_second_grad = add_up(back_parts)
    down_mine = scatter_rows(down_partial)
    gate_mine = scatter_rows(gate_partial)
    up_mine = scatter_rows(up_partial)
    middle_back, gain_second_grad = norm_back(middle, scale_second, gain_second, normed_second_grad)
    middle_grad = upstream.astype(jnp.float32) + middle_back
    branch_low = middle_grad.astype(jnp.bfloat16)
    branch_low, down_mine = lax.optimization_barrier((branch_low, down_mine))
    attended_grad = against(branch_low, outward_full).astype(jnp.bfloat16)
    attended_grad, gate_mine = lax.optimization_barrier((attended_grad, gate_mine))
    query_back, kv_back = attend_backward(
        attended_grad, query_here, kv_here, mixed_here, logs, group, heads_here, block
    )
    first_blocks = gather_swap(normed, "fsdp")
    query_back, kv_back, up_mine, first_blocks = lax.optimization_barrier(
        (query_back, kv_back, up_mine, first_blocks)
    )
    query_grad = rotate(
        query_back.astype(jnp.float32).reshape(local, HEADS, HEAD_DIM), position, -1.0
    )
    kv_grad = kv_back.astype(jnp.float32).reshape(KV_HEADS, copies, local, 2 * HEAD_DIM)
    kv_grad = jnp.sum(kv_grad, axis=1).transpose(1, 0, 2)
    key_grad = rotate(kv_grad[:, :, :HEAD_DIM], position, -1.0)
    value_grad = kv_grad[:, :, HEAD_DIM:]
    inward_grad = jnp.concatenate(
        [
            query_grad.reshape(local, D),
            key_grad.reshape(local, kv_width),
            value_grad.reshape(local, kv_width),
        ],
        axis=-1,
    ).astype(jnp.bfloat16)
    normed_grad = against(inward_grad, inward_full)
    rows_back, gain_first_grad = norm_back(rows, scale_first, gain_first, normed_grad)
    input_grad = middle_grad + rows_back

    def column_slices(field):
        width = field.shape[1] // slices
        return field.reshape(local, slices, width).transpose(1, 0, 2)

    attended_all = jnp.concatenate(attended_blocks, axis=0)
    branch_all = jnp.concatenate(exchange_swap(column_slices(branch_low), "fsdp"), axis=0)
    outward_mine = scatter_rows(outer(attended_all, branch_all).astype(jnp.bfloat16))
    first_all = jnp.concatenate(first_blocks, axis=0)
    inward_grad_all = jnp.concatenate(exchange_swap(column_slices(inward_grad), "fsdp"), axis=0)
    gain_grads = jnp.stack([gain_first_grad, gain_second_grad], axis=1)
    gain_grads = jnp.pad(gain_grads.astype(jnp.bfloat16), ((0, 0), (0, 126)))
    inward_partial = outer(first_all, inward_grad_all).astype(jnp.bfloat16)
    slice_cols = inward_partial.shape[1]
    inward_mine = scatter_rows(
        jnp.concatenate([inward_partial, gain_grads], axis=1), (outward_mine,)
    )
    result = middle + add_up(send_back(against(hidden, down_slice)))
    down_back = return_columns(down_mine)
    gate_back = return_columns(gate_mine)
    up_back = return_columns(up_mine)
    outward_back = return_columns(outward_mine)
    inward_back = return_columns(inward_mine)

    gains_sum = add_up([piece[:, slice_cols : slice_cols + 2] for piece in inward_back])
    gains_sum = jnp.transpose(gains_sum)
    inward_back = [piece[:, :slice_cols] for piece in inward_back]
    inward_sum = jnp.concatenate(inward_back, axis=1).astype(jnp.float32)
    outward_sum = jnp.concatenate(outward_back, axis=1).astype(jnp.float32)
    gate_up_sum = jnp.concatenate(gate_back + up_back, axis=1).astype(jnp.float32)
    down_sum = jnp.concatenate(down_back, axis=1).astype(jnp.float32)
    first_inward_new, second_inward_new, inward_new = adam_update(
        w_inward, first_inward, second_inward, inward_sum, 0.02, weight_decay
    )
    first_outward_new, second_outward_new, outward_new = adam_update(
        w_outward, first_outward, second_outward, outward_sum, 0.15, weight_decay
    )
    first_gate_up_new, second_gate_up_new, gate_up_new = adam_update(
        w_gate_up, first_gate_up, second_gate_up, gate_up_sum, 0.02, weight_decay
    )
    first_down_new, second_down_new, down_new = adam_update(
        w_down, first_down, second_down, down_sum, 0.015, weight_decay
    )
    first_gains_new, second_gains_new, gains_new = adam_update(
        gains, first_gains, second_gains, gains_sum, 0.6, 0.0
    )
    return (
        result[None].astype(jnp.bfloat16),
        input_grad[None],
        first_inward_new,
        second_inward_new,
        inward_new,
        first_outward_new,
        second_outward_new,
        outward_new,
        first_gate_up_new,
        second_gate_up_new,
        gate_up_new,
        first_down_new,
        second_down_new,
        down_new,
        first_gains_new,
        second_gains_new,
        gains_new,
    )


def solution(mesh):
    in_specs = (
        P("fsdp", "seq", None),
        P("fsdp", "seq", None),
        P(("seq", "fsdp"), None),
        P(("seq", "fsdp"), None),
        P(("seq", "fsdp"), None),
        P(("seq", "fsdp"), None),
        P(None, ("seq", "fsdp")),
        P(("seq", "fsdp"), None),
        P(("seq", "fsdp"), None),
        P(("seq", "fsdp"), None),
        P(("seq", "fsdp"), None),
        P(None, ("seq", "fsdp")),
        P(("seq", "fsdp"), None),
        P(("seq", "fsdp"), None),
        P(("seq", "fsdp"), None),
        P(("seq", "fsdp"), None),
        P(None, ("seq", "fsdp")),
    )
    out_specs = (
        P("fsdp", "seq", None),
        P("fsdp", "seq", None),
        P(("seq", "fsdp"), None),
        P(("seq", "fsdp"), None),
        P(("seq", "fsdp"), None),
        P(("seq", "fsdp"), None),
        P(("seq", "fsdp"), None),
        P(("seq", "fsdp"), None),
        P(("seq", "fsdp"), None),
        P(("seq", "fsdp"), None),
        P(("seq", "fsdp"), None),
        P(("seq", "fsdp"), None),
        P(("seq", "fsdp"), None),
        P(("seq", "fsdp"), None),
        P(None, ("seq", "fsdp")),
        P(None, ("seq", "fsdp")),
        P(None, ("seq", "fsdp")),
    )
    return jax.shard_map(body, mesh=mesh, in_specs=in_specs, out_specs=out_specs, check_vma=False)
```

```python
import functools

import jax
import jax.numpy as jnp
from jax import lax
from jax.experimental import pallas as pl
from jax.experimental.pallas import tpu as pltpu
from jax.sharding import PartitionSpec as P

D = 2048
FF = 5632
HEADS = 32
KV_HEADS = 4
HEAD_DIM = 64
STEP = 10


epsilon = 1e-05
adam_epsilon = 1e-08
beta_first = 0.9
beta_second = 0.95
rope_base = 10000.0
weight_decay = 0.1
masked_value = -1e30


def rotate(field, position, sign):
    half = field.shape[-1] // 2
    exponent = jnp.arange(half).astype(jnp.float32) * (-2.0 / field.shape[-1])
    frequency = jnp.power(rope_base, exponent)
    angle = position[:, None] * frequency[None, :]
    cosine = jnp.cos(angle)[:, None, :]
    sine = sign * jnp.sin(angle)[:, None, :]
    first = field[..., :half]
    second = field[..., half:]
    return jnp.concatenate(
        [first * cosine - second * sine, second * cosine + first * sine], axis=-1
    )


def rms_scale(rows):
    return lax.rsqrt(jnp.mean(rows * rows, axis=-1, keepdims=True) + epsilon)


def norm_back(rows, scale_rows, gain, grad):
    weighted = grad * gain
    row_grad = scale_rows * weighted - rows * scale_rows**3 * jnp.mean(
        weighted * rows, axis=-1, keepdims=True
    )
    gain_grad = jnp.sum(grad * rows * scale_rows, axis=0)
    return (row_grad, gain_grad)


def dot(left, right):
    return jnp.dot(left, right, preferred_element_type=jnp.float32)


def outer(left, right):
    return lax.dot_general(
        left, right, (((0,), (0,)), ((), ())), preferred_element_type=jnp.float32
    )


def against(left, right):
    return lax.dot_general(
        left, right, (((1,), (1,)), ((), ())), preferred_element_type=jnp.float32
    )


def stack_heads(field, heads):
    return jnp.concatenate(
        [field[:, h * HEAD_DIM : (h + 1) * HEAD_DIM] for h in range(heads)], axis=0
    )


def unstack_heads(field, heads):
    rows = field.shape[0] // heads
    return jnp.concatenate([field[h * rows : (h + 1) * rows] for h in range(heads)], axis=1)


def masked_scores(keys, queries, block):
    scores = against(keys, queries)
    key_place = lax.broadcasted_iota(jnp.int32, scores.shape, 0)
    query_place = lax.rem(lax.broadcasted_iota(jnp.int32, scores.shape, 1), block)
    return jnp.where(key_place <= query_place, scores, masked_value)


def remote(source, target, send, arrive, axis, device):
    return pltpu.make_async_remote_copy(
        src_ref=source,
        dst_ref=target,
        send_sem=send,
        recv_sem=arrive,
        device_id={axis: device},
        device_id_type=pl.DeviceIdType.MESH,
    )


VMEM = pl.BlockSpec(memory_space=pltpu.VMEM)


def core_pair(index):
    return index // 2, lax.rem(index, 2)


def pass_rows_start(rows, send, come, near):
    s = lax.axis_index("seq")
    for d in [1] + near:
        rows_copy(rows, send, come, d, s, s ^ d).start()


def pass_rows_finish(rows, send, come, forward, passed, near):
    s = lax.axis_index("seq")
    for d in near:
        rows_copy(rows, send, come, d, s ^ d, s ^ d).wait_recv()
        rows_copy(rows, forward, passed, d, s ^ d, s ^ 1).start()
    rows_copy(rows, send, come, 1, s ^ 1, s ^ 1).wait()
    for d in near:
        rows_copy(rows, send, come, d, s, s ^ d).wait_send()
        rows_copy(rows, forward, passed, d, s ^ d, s ^ 1).wait_send()
        rows_copy(rows, forward, passed, d, s ^ 1 ^ d, s ^ 1).wait_recv()


def rows_copy(rows, send, come, d, owner, target):
    place, half = core_pair(owner)
    return remote(rows.at[place, half], rows.at[place, half], send.at[d], come.at[d], "seq", target)


def share_kernel(
    in_ref, gain_ref, gate_up_ref, down_ref, feed_gate_up, feed_down, in_rows,
    low_gate_up, low_down, send_feed, come_feed, send_in, come_in, pass_in, passed_in,
):
    group, slices = lax.axis_size("seq"), lax.axis_size("fsdp")
    s, f = lax.axis_index("seq"), lax.axis_index("fsdp")
    pair, core = core_pair(s)
    depth, inward_cols = in_ref.shape
    ff_cols = FF // slices
    near = list(range(2, group, 2))
    in_rows[pair, core, :, pl.ds(0, inward_cols)] = in_ref[...].astype(jnp.bfloat16)
    in_rows[pair, core, :, pl.ds(inward_cols, 128)] = gain_ref[...]
    meet_spread(near)
    pass_rows_start(in_rows, send_in, come_in, near)
    for t in range(slices):
        columns = pl.ds(t * ff_cols, ff_cols)
        low_gate_up[t, :, pl.ds(0, ff_cols)] = gate_up_ref[:, columns].astype(jnp.bfloat16)
        low_gate_up[t, :, pl.ds(ff_cols, ff_cols)] = gate_up_ref[
            :, pl.ds(FF + t * ff_cols, ff_cols)
        ].astype(jnp.bfloat16)
        low_down[t] = down_ref[:, columns].astype(jnp.bfloat16)

    feeds = ((low_gate_up, feed_gate_up), (low_down, feed_down))

    def feed_copy(k, d, owner, target):
        low, feed = feeds[k]
        return remote(
            low.at[target],
            feed.at[pl.ds(pl.multiple_of(owner * depth, depth), depth), :],
            send_feed.at[k, d], come_feed.at[k, d], "fsdp", target,
        )

    for d in range(1, slices):
        for k in range(2):
            feed_copy(k, d, f, f ^ d).start()
    mine = pl.ds(pl.multiple_of(f * depth, depth), depth)
    for low, feed in feeds:
        feed[mine, :] = low[f]
    pass_rows_finish(in_rows, send_in, come_in, pass_in, passed_in, near)
    for d in range(1, slices):
        for k in range(2):
            feed_copy(k, d, f ^ d, f ^ d).wait()


def share_weights(w_inward, gain_columns, w_gate_up, w_down, group, slices):
    depth = w_inward.shape[0]
    ff_cols = FF // slices
    width = w_inward.shape[1] + 128
    sems = [pltpu.SemaphoreType.DMA((2, slices))] * 2 + [pltpu.SemaphoreType.DMA((group,))] * 4
    return pl.pallas_call(
        share_kernel,
        in_specs=[VMEM] * 4,
        out_specs=[VMEM] * 3,
        out_shape=[
            jax.ShapeDtypeStruct((slices * depth, 2 * ff_cols), jnp.bfloat16),
            jax.ShapeDtypeStruct((slices * depth, ff_cols), jnp.bfloat16),
            jax.ShapeDtypeStruct((group // 2, 2, depth, width), jnp.bfloat16),
        ],
        scratch_shapes=[
            pltpu.VMEM((slices, depth, 2 * ff_cols), jnp.bfloat16),
            pltpu.VMEM((slices, depth, ff_cols), jnp.bfloat16),
        ]
        + sems,
        compiler_params=pltpu.CompilerParams(
            vmem_limit_bytes=48 << 20, collective_id=2, has_side_effects=True
        ),
    )(w_inward, gain_columns, w_gate_up, w_down)


def spread_copies(rows, full, send, come, forward, passed):
    s, f = lax.axis_index("seq"), lax.axis_index("fsdp")
    core = lax.rem(s, 2)
    slices = lax.axis_size("fsdp")

    def first(d, owner, target):
        return remote(
            rows.at[:, core], full.at[:, core, owner], send.at[d], come.at[d], "fsdp", target
        )

    def second(d, half):
        block = full.at[:, half, f ^ d]
        return remote(block, block, forward.at[d], passed.at[d], "seq", s ^ 1)

    def start():
        for d in range(1, slices):
            first(d, f, f ^ d).start()

    def local():
        full[:, :, f] = rows[...]

    def finish():
        for d in range(1, slices):
            first(d, f ^ d, f ^ d).wait_recv()
            second(d, core).start()
        for d in range(1, slices):
            first(d, f, f ^ d).wait_send()
            second(d, core).wait_send()
            second(d, 1 - core).wait_recv()

    return start, local, finish


def meet_spread(extra=()):
    barrier = pltpu.get_barrier_semaphore()
    s, f = lax.axis_index("seq"), lax.axis_index("fsdp")
    near = sorted({1, *extra})
    slices = lax.axis_size("fsdp")
    for d in near:
        pl.semaphore_signal(
            barrier, inc=1, device_id={"seq": s ^ d}, device_id_type=pl.DeviceIdType.MESH
        )
    for d in range(1, slices):
        pl.semaphore_signal(
            barrier, inc=1, device_id={"fsdp": f ^ d}, device_id_type=pl.DeviceIdType.MESH
        )
    pl.semaphore_wait(barrier, len(near) + slices - 1)


def spread_kernel(
    rows, out_ref, full, out_rows, send, come, forward, passed,
    send_out, come_out, pass_out, passed_out,
):
    near = list(range(2, lax.axis_size("seq"), 2))
    pair, core = core_pair(lax.axis_index("seq"))
    meet_spread(near)
    start, local, finish = spread_copies(rows, full, send, come, forward, passed)
    start()
    out_rows[pair, core] = out_ref[...].astype(jnp.bfloat16)
    pass_rows_start(out_rows, send_out, come_out, near)
    local()
    pass_rows_finish(out_rows, send_out, come_out, pass_out, passed_out, near)
    finish()


def spread_rows(rows, w_outward, slices):
    pairs, two, depth, width = rows.shape
    full, out_rows = pl.pallas_call(
        spread_kernel,
        in_specs=[VMEM] * 2,
        out_specs=[VMEM] * 2,
        out_shape=[
            jax.ShapeDtypeStruct((pairs, two, slices, depth, width), rows.dtype),
            jax.ShapeDtypeStruct((pairs, two, depth, w_outward.shape[1]), rows.dtype),
        ],
        scratch_shapes=[pltpu.SemaphoreType.DMA((slices,))] * 4
        + [pltpu.SemaphoreType.DMA((2 * pairs,))] * 4,
        compiler_params=pltpu.CompilerParams(
            vmem_limit_bytes=48 << 20, collective_id=3, has_side_effects=True
        ),
    )(rows, w_outward)
    return full.reshape(pairs * two * slices * depth, width), out_rows


def forward_kernel(
    query_ref, kv_ref, out_rows, query_here, kv_here, mixed_here, logs, attended, out_full,
    send_query, come_query, send_kv, come_kv, send_out, come_out, local_sem,
    send_rows, come_rows, pass_rows, passed_rows, *, heads, block
):
    group = lax.axis_size("seq")
    me = lax.axis_index("seq")
    local, width = query_ref.shape[0], heads * HEAD_DIM
    pair = 2 * HEAD_DIM
    copies = group // KV_HEADS
    length = group * local
    per_block = block // local
    meet_spread(range(1, group))
    spread_start, spread_local, spread_finish = spread_copies(
        out_rows, out_full, send_rows, come_rows, pass_rows, passed_rows
    )

    def query_copy(d, owner, target):
        return remote(
            query_ref.at[:, pl.ds(pl.multiple_of(target * width, 128), width)],
            query_here.at[pl.ds(pl.multiple_of(owner * local, local), local), :],
            send_query.at[d], come_query.at[d], "seq", target,
        )

    def kv_copy(d, owner, target):
        return remote(
            kv_ref.at[:, pl.ds(pl.multiple_of(target // copies * pair, 128), pair)],
            kv_here.at[pl.ds(pl.multiple_of(owner * local, local), local), :],
            send_kv.at[d], come_kv.at[d], "seq", target,
        )

    def out_copy(d, owner, target):
        return remote(
            mixed_here.at[pl.ds(pl.multiple_of(target * local, local), local), :],
            attended.at[:, pl.ds(pl.multiple_of(owner * width, 128), width)],
            send_out.at[d], come_out.at[d], "seq", target,
        )

    for d in range(1, group):
        kv_copy(d, me, me ^ d).start()
        query_copy(d, me, me ^ d).start()
    spread_start()
    mine = pl.ds(pl.multiple_of(me * local, local), local)
    own_columns = pl.ds(pl.multiple_of(me * width, 128), width)
    own_query = pltpu.make_async_copy(
        query_ref.at[:, own_columns], query_here.at[mine, :], local_sem.at[0]
    )
    own_kv = pltpu.make_async_copy(
        kv_ref.at[:, pl.ds(pl.multiple_of(me // copies * pair, 128), pair)],
        kv_here.at[mine, :],
        local_sem.at[1],
    )
    own_query.start()
    own_kv.start()
    spread_local()
    own_query.wait()
    own_kv.wait()

    def query_block(index, _):
        for part in range(per_block):
            source = index * per_block + part

            @pl.when(source != me)
            def _():
                kv_copy(source ^ me, source, source).wait_recv()
                query_copy(source ^ me, source, source).wait_recv()

        place = pl.ds(pl.multiple_of(index * block, block), block)
        queries = stack_heads(query_here[place, :], heads) * jnp.bfloat16(HEAD_DIM**-0.5)
        columns = heads * block

        def step(j, carry, masked):
            largest, total, mixed = carry
            start = pl.multiple_of(j * block, block)
            kv = kv_here[pl.ds(start, block), :]
            keys, values = kv[:, :HEAD_DIM], kv[:, HEAD_DIM:]
            if masked:
                scores = masked_scores(keys, queries, block)
            else:
                scores = against(keys, queries)
            new = jnp.maximum(largest, jnp.max(scores, axis=0, keepdims=True))
            fade = jnp.exp(largest - new)
            weights = jnp.exp(scores - new)
            total = total * fade + jnp.sum(weights, axis=0, keepdims=True)
            mixed = mixed * fade + outer(values, weights.astype(jnp.bfloat16))
            return new, total, mixed

        carry = (
            jnp.full((1, columns), masked_value, jnp.float32),
            jnp.zeros((1, columns), jnp.float32),
            jnp.zeros((HEAD_DIM, columns), jnp.float32),
        )
        carry = lax.fori_loop(0, index, lambda j, c: step(j, c, False), carry)
        largest, total, mixed = step(index, carry, True)
        logs[index] = largest + jnp.log(total)
        mixed_here[place, :] = unstack_heads((mixed / total).T, heads).astype(mixed_here.dtype)
        for part in range(per_block):
            target = index * per_block + part

            @pl.when(target != me)
            def _():
                out_copy(target ^ me, me, target).start()

        return 0

    lax.fori_loop(0, length // block, query_block, 0)
    own_out = pltpu.make_async_copy(
        mixed_here.at[mine, :], attended.at[:, own_columns], local_sem.at[0]
    )
    own_out.start()
    own_out.wait()
    spread_finish()
    for d in range(1, group):
        other = me ^ d
        kv_copy(d, me, other).wait_send()
        query_copy(d, me, other).wait_send()
        out_copy(d, other, other).wait()


def backward_kernel(
    grad_ref, query_here, kv_here, mixed_here, logs, normed_ref, attended_ref, branch_ref,
    query_back, kv_back, normed_all, attended_all, branch_all,
    grad_here, query_grad, kv_grad, key_sum, value_sum,
    send_grad, come_grad, send_query, come_query, send_kv, come_kv, local_sem,
    send_slice, come_slice, *, heads, block
):
    group = lax.axis_size("seq")
    me = lax.axis_index("seq")
    local, width = grad_ref.shape[0], heads * HEAD_DIM
    length = group * local
    per_block = block // local
    blocks = length // block
    scale = HEAD_DIM**-0.5
    slices, f = lax.axis_size("fsdp"), lax.axis_index("fsdp")
    share = branch_all.shape[2]
    meet_spread(range(1, group))

    def slice_copy(k, d, target):
        columns = pl.ds(pl.multiple_of(target * share, 128), share)
        source = (branch_ref.at[:, columns], attended_ref, normed_ref)[k]
        into = (branch_all, attended_all, normed_all)[k]
        return remote(
            source, into.at[d], send_slice.at[k, d], come_slice.at[k, d], "fsdp", target
        )

    def grad_copy(d, owner, target):
        return remote(
            grad_ref.at[:, pl.ds(pl.multiple_of(target * width, 128), width)],
            grad_here.at[pl.ds(pl.multiple_of(owner * local, local), local), :],
            send_grad.at[d], come_grad.at[d], "seq", target,
        )

    def query_copy(d, owner, target):
        return remote(
            query_grad.at[pl.ds(pl.multiple_of(target * local, local), local), :],
            query_back.at[:, pl.ds(pl.multiple_of(owner * width, 128), width)],
            send_query.at[d], come_query.at[d], "seq", target,
        )

    def kv_copy(d, owner, target):
        return remote(
            kv_grad.at[pl.ds(pl.multiple_of(target * local, local), local), :],
            kv_back.at[owner],
            send_kv.at[d], come_kv.at[d], "seq", target,
        )

    for d in range(1, group):
        grad_copy(d, me, me ^ d).start()
    for k in range(3):
        for d in range(1, slices):
            slice_copy(k, d, f ^ d).start()
    normed_all[0] = normed_ref[...]
    attended_all[0] = attended_ref[...]
    branch_all[0] = branch_ref[:, pl.ds(pl.multiple_of(f * share, 128), share)]
    mine = pl.ds(pl.multiple_of(me * local, local), local)
    own_columns = pl.ds(pl.multiple_of(me * width, 128), width)
    own_grad = pltpu.make_async_copy(
        grad_ref.at[:, own_columns], grad_here.at[mine, :], local_sem.at[0]
    )
    own_grad.start()
    own_grad.wait()
    key_sum[...] = jnp.zeros_like(key_sum)
    value_sum[...] = jnp.zeros_like(value_sum)

    def query_block(turn, _):
        index = blocks - 1 - turn
        for part in range(per_block):
            source = index * per_block + part

            @pl.when(source != me)
            def _():
                grad_copy(source ^ me, source, source).wait_recv()

        place = pl.ds(pl.multiple_of(index * block, block), block)
        queries = stack_heads(query_here[place, :], heads) * jnp.bfloat16(scale)
        grads = stack_heads(grad_here[place, :], heads)
        mixed = stack_heads(mixed_here[place, :], heads)
        inner = jnp.sum(
            (grads.astype(jnp.float32) * mixed.astype(jnp.float32)).T, axis=0, keepdims=True
        )
        log_total = logs[index]

        def step(j, total, masked):
            start = pl.multiple_of(j * block, block)
            rows = pl.ds(start, block)
            kv = kv_here[rows, :]
            keys, values = kv[:, :HEAD_DIM], kv[:, HEAD_DIM:]
            if masked:
                scores = masked_scores(keys, queries, block)
            else:
                scores = against(keys, queries)
            shares = jnp.exp(scores - log_total)
            share_grad = against(values, grads)
            score_grad = (shares * (share_grad - inner)).astype(jnp.bfloat16)
            value_sum[rows, :] += dot(shares.astype(jnp.bfloat16), grads)
            key_sum[rows, :] += dot(score_grad, queries)
            return total + outer(keys, score_grad)

        total = lax.fori_loop(
            0,
            index,
            lambda j, c: step(j, c, False),
            jnp.zeros((HEAD_DIM, heads * block), jnp.float32),
        )
        total = step(index, total, True)
        query_grad[place, :] = unstack_heads((total * scale).T, heads).astype(jnp.bfloat16)
        kv_grad[place, :] = jnp.concatenate(
            [key_sum[place, :], value_sum[place, :]], axis=1
        ).astype(jnp.bfloat16)
        for part in range(per_block):
            target = index * per_block + part

            @pl.when(target != me)
            def _():
                query_copy(target ^ me, me, target).start()
                kv_copy(target ^ me, me, target).start()

        return 0

    lax.fori_loop(0, blocks, query_block, 0)
    own_query = pltpu.make_async_copy(
        query_grad.at[mine, :], query_back.at[:, own_columns], local_sem.at[0]
    )
    own_kv = pltpu.make_async_copy(kv_grad.at[mine, :], kv_back.at[me], local_sem.at[1])
    own_query.start()
    own_kv.start()
    own_query.wait()
    own_kv.wait()
    for d in range(1, group):
        other = me ^ d
        grad_copy(d, me, other).wait_send()
        query_copy(d, other, other).wait()
        kv_copy(d, other, other).wait()
    for k in range(3):
        for d in range(1, slices):
            slice_copy(k, d, f ^ d).wait()


def attend_forward(query, kv, out_rows, group, slices, heads, block):
    local, width = query.shape[0], heads * HEAD_DIM
    length = group * local
    pairs = heads * length * length // 2
    sems = pltpu.SemaphoreType.DMA((group,))
    pairs_seq, _, depth, _ = out_rows.shape
    return pl.pallas_call(
        functools.partial(forward_kernel, heads=heads, block=block),
        in_specs=[VMEM] * 3,
        out_specs=[VMEM] * 6,
        out_shape=[
            jax.ShapeDtypeStruct((length, width), jnp.bfloat16),
            jax.ShapeDtypeStruct((length, 2 * HEAD_DIM), jnp.bfloat16),
            jax.ShapeDtypeStruct((length, width), jnp.bfloat16),
            jax.ShapeDtypeStruct((length // block, 1, heads * block), jnp.float32),
            jax.ShapeDtypeStruct((local, group * width), jnp.bfloat16),
            jax.ShapeDtypeStruct(
                (pairs_seq, 2, slices, depth, out_rows.shape[3]), jnp.bfloat16
            ),
        ],
        scratch_shapes=[sems] * 6
        + [pltpu.SemaphoreType.DMA((2,))]
        + [pltpu.SemaphoreType.DMA((slices,))] * 4,
        compiler_params=pltpu.CompilerParams(
            vmem_limit_bytes=48 << 20, collective_id=0, has_side_effects=True
        ),
        cost_estimate=pl.CostEstimate(
            flops=pairs * HEAD_DIM * 160, bytes_accessed=length * 4 * width, transcendentals=pairs
        ),
    )(query, kv, out_rows)


def attend_backward(
    grads, query_here, kv_here, mixed_here, logs, normed, attended, branch, group, slices, heads, block
):
    local, width = grads.shape[0], heads * HEAD_DIM
    length = group * local
    pairs = heads * length * length // 2
    features = normed.shape[1]
    gathered = jax.ShapeDtypeStruct((slices, local, features), jnp.bfloat16)
    sems = pltpu.SemaphoreType.DMA((group,))
    return pl.pallas_call(
        functools.partial(backward_kernel, heads=heads, block=block),
        in_specs=[VMEM] * 8,
        out_specs=[VMEM] * 5,
        out_shape=[
            jax.ShapeDtypeStruct((local, group * width), jnp.bfloat16),
            jax.ShapeDtypeStruct((group, local, 2 * HEAD_DIM), jnp.bfloat16),
            gathered,
            gathered,
            jax.ShapeDtypeStruct((slices, local, features // slices), jnp.bfloat16),
        ],
        scratch_shapes=[
            pltpu.VMEM((length, width), jnp.bfloat16),
            pltpu.VMEM((length, width), jnp.bfloat16),
            pltpu.VMEM((length, 2 * HEAD_DIM), jnp.bfloat16),
            pltpu.VMEM((length, HEAD_DIM), jnp.float32),
            pltpu.VMEM((length, HEAD_DIM), jnp.float32),
        ]
        + [sems] * 6
        + [pltpu.SemaphoreType.DMA((2,))]
        + [pltpu.SemaphoreType.DMA((3, slices))] * 2,
        compiler_params=pltpu.CompilerParams(
            vmem_limit_bytes=48 << 20, collective_id=1, has_side_effects=True
        ),
        cost_estimate=pl.CostEstimate(
            flops=pairs * HEAD_DIM * 160, bytes_accessed=length * 8 * width, transcendentals=pairs
        ),
    )(grads, query_here, kv_here, mixed_here, logs, normed, attended, branch)


def meet_slices():
    slices, f = lax.axis_size("fsdp"), lax.axis_index("fsdp")
    barrier = pltpu.get_barrier_semaphore()
    for d in range(1, slices):
        pl.semaphore_signal(
            barrier, inc=1, device_id={"fsdp": f ^ d}, device_id_type=pl.DeviceIdType.MESH
        )
    pl.semaphore_wait(barrier, slices - 1)


def row_copy(stage, target, sem, r):
    width = stage.shape[0]
    rows = pl.ds(pl.multiple_of(r * width, width), width)
    return pltpu.make_async_copy(stage, target.at[rows, :], sem)


def grad_rows(field, grads, target, stage, sems):
    width = stage.shape[1]
    steps = target.shape[0] // width

    def step(r, _):
        columns = pl.ds(pl.multiple_of(r * width, width), width)
        slot = lax.rem(r, 2)
        left = field[:, :, columns].reshape(grads[0].shape[0], width)

        @pl.when(r > 1)
        def _():
            row_copy(stage.at[slot], target, sems.at[slot], r - 2).wait()

        for k, grad in enumerate(grads):
            units = grad.shape[1]
            stage[slot, :, pl.ds(k * units, units)] = outer(left, grad[...]).astype(jnp.bfloat16)
        row_copy(stage.at[slot], target, sems.at[slot], r).start()
        return 0

    lax.fori_loop(0, steps, step, 0)
    for r in (steps - 2, steps - 1):
        row_copy(stage.at[r % 2], target, sems.at[r % 2], r).wait()


def feed_first_kernel(
    x_ref, dy_ref, gate_up_ref, x_all, gate_all, up_all, hidden, down_grad_out,
    gate_sum, up_sum, grad_stage, send_x, come_x, grad_sem, *, strip
):
    slices, f = lax.axis_size("fsdp"), lax.axis_index("fsdp")
    local = x_ref.shape[0]
    meet_slices()

    def x_copy(d):
        return remote(x_ref, x_all.at[d], send_x.at[d], come_x.at[d], "fsdp", f ^ d)

    for d in range(1, slices):
        x_copy(d).start()
    x_all[0] = x_ref[...]

    def token_block(d, _):
        @pl.when(d > 0)
        def _():
            x_copy(d).wait_recv()

        x = x_all[d]
        units = hidden.shape[1]
        gate_sum[...] = dot(x, gate_up_ref[:, pl.ds(0, units)])
        up_sum[...] = dot(x, gate_up_ref[:, pl.ds(units, units)])

        def part(i, _):
            rows = pl.ds(pl.multiple_of(i * strip, strip), strip)
            place = pl.ds(pl.multiple_of(d * local + i * strip, strip), strip)
            gate, up = gate_sum[rows, :], up_sum[rows, :]
            hidden[place, :] = (gate / (1.0 + jnp.exp(-gate)) * up).astype(jnp.bfloat16)
            gate_all[place, :] = gate.astype(jnp.bfloat16)
            up_all[place, :] = up.astype(jnp.bfloat16)
            return 0

        lax.fori_loop(0, local // strip, part, 0)
        return 0

    lax.fori_loop(0, slices, token_block, 0)
    grad_rows(dy_ref, [hidden], down_grad_out, grad_stage, grad_sem)
    for d in range(1, slices):
        x_copy(d).wait_send()


def feed_second_kernel(
    x_ref, dy_ref, gate_all, up_all, hidden, gate_up_ref, down_ref,
    back_ref, out_parts, gate_up_grad_out,
    gate_grad, up_grad, hidden_sum, back_send, back_come, out_stage, grad_stage,
    send_back, come_back, out_sem, grad_sem, *, strip
):
    slices, f = lax.axis_size("fsdp"), lax.axis_index("fsdp")
    local = back_ref.shape[0]
    meet_slices()

    def back_copy(d):
        return remote(
            back_send.at[d], back_come.at[d - 1], send_back.at[d], come_back.at[d], "fsdp", f ^ d
        )

    def out_copy(d):
        slot = lax.rem(d, 2)
        return pltpu.make_async_copy(out_stage.at[slot], out_parts.at[d], out_sem.at[slot])

    def token_block(turn, _):
        d = slices - 1 - turn
        place = pl.ds(pl.multiple_of(d * local, local), local)
        hidden_sum[...] = dot(dy_ref[d], down_ref[...])

        def part(i, _):
            rows = pl.ds(pl.multiple_of(i * strip, strip), strip)
            here = pl.ds(pl.multiple_of(d * local + i * strip, strip), strip)
            gate = gate_all[here, :].astype(jnp.float32)
            up = up_all[here, :].astype(jnp.float32)
            sigmoid = 1.0 / (1.0 + jnp.exp(-gate))
            grad = hidden_sum[rows, :]
            gate_grad[here, :] = (
                grad * up * sigmoid * (1.0 + gate * (1.0 - sigmoid))
            ).astype(jnp.bfloat16)
            up_grad[here, :] = (grad * gate * sigmoid).astype(jnp.bfloat16)
            return 0

        lax.fori_loop(0, local // strip, part, 0)
        units = hidden.shape[1]
        back = against(gate_grad[place, :], gate_up_ref[:, pl.ds(0, units)])
        back = back + against(up_grad[place, :], gate_up_ref[:, pl.ds(units, units)])
        back_send[d] = back.astype(jnp.bfloat16)

        @pl.when(d > 0)
        def _():
            back_copy(d).start()

        @pl.when(turn > 1)
        def _():
            out_copy(d + 2).wait()

        out_stage[lax.rem(d, 2)] = against(hidden[place, :], down_ref[...]).astype(jnp.bfloat16)
        out_copy(d).start()
        return 0

    lax.fori_loop(0, slices, token_block, 0)
    out_copy(1).wait()
    out_copy(0).wait()
    grad_rows(x_ref, [gate_grad, up_grad], gate_up_grad_out, grad_stage, grad_sem)
    for d in range(1, slices):
        back_copy(d).wait()
    back_ref[...] = functools.reduce(
        jnp.add, [back_send[0].astype(jnp.float32)]
        + [back_come[d - 1].astype(jnp.float32) for d in range(1, slices)],
    )


ANY = pl.BlockSpec(memory_space=pl.ANY)


def feed_first(x, upstream_all, gate_up_slice):
    slices, local, width = upstream_all.shape
    ff_cols = gate_up_slice.shape[1] // 2
    tokens = slices * local
    units = jax.ShapeDtypeStruct((tokens, ff_cols), jnp.bfloat16)
    high = pltpu.VMEM((local, ff_cols), jnp.float32)
    sems = pltpu.SemaphoreType.DMA((slices,))
    return pl.pallas_call(
        functools.partial(feed_first_kernel, strip=32),
        in_specs=[VMEM] * 3,
        out_specs=[VMEM] * 4 + [ANY],
        out_shape=[
            jax.ShapeDtypeStruct((slices, local, width), jnp.bfloat16),
            units,
            units,
            units,
            jax.ShapeDtypeStruct((width, ff_cols), jnp.bfloat16),
        ],
        scratch_shapes=[high, high, pltpu.VMEM((2, 256, ff_cols), jnp.bfloat16)]
        + [sems] * 2
        + [pltpu.SemaphoreType.DMA((2,))],
        compiler_params=pltpu.CompilerParams(
            vmem_limit_bytes=60 << 20, collective_id=4, has_side_effects=True
        ),
        cost_estimate=pl.CostEstimate(
            flops=10 * tokens * width * ff_cols, bytes_accessed=30 << 20, transcendentals=0
        ),
    )(x, upstream_all, gate_up_slice)


def feed_second(x_all, upstream_all, gate_all, up_all, hidden, gate_up_slice, down_slice):
    slices, local, width = upstream_all.shape
    ff_cols = gate_up_slice.shape[1] // 2
    tokens = slices * local
    blocks = pltpu.VMEM((slices, local, width), jnp.bfloat16)
    low = pltpu.VMEM((tokens, ff_cols), jnp.bfloat16)
    sems = pltpu.SemaphoreType.DMA((slices,))
    return pl.pallas_call(
        functools.partial(feed_second_kernel, strip=32),
        in_specs=[VMEM] * 7,
        out_specs=[VMEM] + [ANY] * 2,
        out_shape=[
            jax.ShapeDtypeStruct((local, width), jnp.float32),
            jax.ShapeDtypeStruct((slices, local, width), jnp.bfloat16),
            jax.ShapeDtypeStruct((width, 2 * ff_cols), jnp.bfloat16),
        ],
        scratch_shapes=[low, low, pltpu.VMEM((local, ff_cols), jnp.float32), blocks]
        + [
            pltpu.VMEM((slices - 1, local, width), jnp.bfloat16),
            pltpu.VMEM((2, local, width), jnp.bfloat16),
            pltpu.VMEM((2, 256, 2 * ff_cols), jnp.bfloat16),
        ]
        + [sems] * 2
        + [pltpu.SemaphoreType.DMA((2,)), pltpu.SemaphoreType.DMA((2,))],
        compiler_params=pltpu.CompilerParams(
            vmem_limit_bytes=62 << 20, collective_id=5, has_side_effects=True
        ),
        cost_estimate=pl.CostEstimate(
            flops=20 * tokens * width * ff_cols, bytes_accessed=40 << 20, transcendentals=0
        ),
    )(x_all, upstream_all, gate_all, up_all, hidden, gate_up_slice, down_slice)


def swap(piece, axis, offset):
    size = lax.axis_size(axis)
    return lax.ppermute(piece, axis, [(i, i ^ offset) for i in range(size)])


def gather_swap(piece, axis):
    return [piece] + [swap(piece, axis, d) for d in range(1, lax.axis_size(axis))]


def exchange_swap(stack, axis):
    me = lax.axis_index(axis)
    pieces = [
        lax.dynamic_index_in_dim(stack, me ^ d, 0, keepdims=False)
        for d in range(lax.axis_size(axis))
    ]
    return [pieces[0]] + [swap(p, axis, d) for d, p in enumerate(pieces) if d]


def reduce_swap(parts, axis):
    total = parts[0].astype(jnp.float32)
    for d in range(1, len(parts)):
        total = total + swap(parts[d], axis, d).astype(jnp.float32)
    return total


def in_order(pieces, axis):
    me = lax.axis_index(axis)
    stack = jnp.stack(pieces)
    return [
        lax.dynamic_index_in_dim(stack, j ^ me, 0, keepdims=False) for j in range(len(pieces))
    ]


def scatter_rows(partial, after=()):
    partial, *_ = lax.optimization_barrier((partial, *after))
    return lax.psum_scatter(partial, "seq", scatter_dimension=0, tiled=True)


def return_columns(mine):
    size = lax.axis_size("fsdp")
    stack = mine.reshape(size, mine.shape[0] // size, mine.shape[1])
    return in_order(exchange_swap(stack, "fsdp"), "fsdp")


def adam_update(weight, first, second, grad, rate, decay):
    first_new = beta_first * first + (1.0 - beta_first) * grad
    second_new = beta_second * second + (1.0 - beta_second) * grad * grad
    first_hat = first_new / (1.0 - beta_first**STEP)
    second_hat = second_new / (1.0 - beta_second**STEP)
    weight_new = weight - rate * (
        first_hat / (jnp.sqrt(second_hat) + adam_epsilon) + decay * weight
    )
    return (first_new, second_new, weight_new)


def body(
    inputs,
    cotangent,
    w_inward,
    w_outward,
    w_gate_up,
    w_down,
    gains,
    first_inward,
    first_outward,
    first_gate_up,
    first_down,
    first_gains,
    second_inward,
    second_outward,
    second_gate_up,
    second_down,
    second_gains,
):
    rows = inputs[0].astype(jnp.float32)
    upstream = cotangent[0]
    local = rows.shape[0]
    group = lax.axis_size("seq")
    slices = lax.axis_size("fsdp")
    heads_here = HEADS // group
    copies = group // KV_HEADS
    kv_width = KV_HEADS * HEAD_DIM
    head_cols = heads_here * HEAD_DIM
    inward_cols = D + 2 * kv_width
    ff_cols = FF // slices
    depth = w_inward.shape[0]
    position = (lax.axis_index("seq") * local + jnp.arange(local)).astype(jnp.float32)

    low_gains = jnp.pad(jnp.transpose(gains.astype(jnp.bfloat16)), ((0, 0), (0, 126)))
    feed_gate_up, feed_down, in_rows = share_weights(
        w_inward, low_gains, w_gate_up, w_down, group, slices
    )
    gate_up_slice = lax.all_gather(feed_gate_up, "seq", axis=0, tiled=True)
    inward_gains, out_rows = spread_rows(in_rows, w_outward, slices)
    inward_full = inward_gains[:, :inward_cols]
    gain_first = inward_gains[:, inward_cols].astype(jnp.float32)
    gain_second = inward_gains[:, inward_cols + 1].astype(jnp.float32)

    scale_first = rms_scale(rows)
    normed = (rows * scale_first * gain_first).astype(jnp.bfloat16)
    mixed = dot(normed, inward_full)
    query = rotate(mixed[:, :D].reshape(local, HEADS, HEAD_DIM), position, 1.0).astype(jnp.bfloat16)
    key = rotate(
        mixed[:, D : D + kv_width].reshape(local, KV_HEADS, HEAD_DIM), position, 1.0
    ).astype(jnp.bfloat16)
    value = mixed[:, D + kv_width :].reshape(local, KV_HEADS, HEAD_DIM).astype(jnp.bfloat16)
    kv = jnp.concatenate([key, value], axis=-1).reshape(local, 2 * kv_width)
    length = group * local
    block = min(512, length)
    query_here, kv_here, mixed_here, logs, attended, outward_full = attend_forward(
        query.reshape(local, D), kv, out_rows, group, slices, heads_here, block
    )
    outward_full = outward_full.reshape(D, D)
    upstream_late, _ = lax.optimization_barrier((upstream, inward_gains))
    upstream_blocks = gather_swap(upstream_late, "fsdp")
    attended, upstream_blocks, feed_down = lax.optimization_barrier(
        (attended, upstream_blocks, feed_down)
    )
    down_slice = lax.all_gather(feed_down, "seq", axis=0, tiled=True)
    upstream_all = jnp.stack(upstream_blocks)
    middle = rows + dot(attended, outward_full)
    scale_second = rms_scale(middle)
    normed_second = (middle * scale_second * gain_second).astype(jnp.bfloat16)

    def add_up(parts):
        return functools.reduce(jnp.add, [p.astype(jnp.float32) for p in parts])

    normed_all, gate_all, up_all, hidden, down_partial = feed_first(
        normed_second, upstream_all, gate_up_slice
    )
    normed_second_grad, out_parts, gate_up_partial = feed_second(
        normed_all, upstream_all, gate_all, up_all, hidden, gate_up_slice, down_slice
    )
    down_mine = scatter_rows(down_partial)
    gate_up_mine = scatter_rows(gate_up_partial)
    middle_back, gain_second_grad = norm_back(middle, scale_second, gain_second, normed_second_grad)
    middle_grad = upstream.astype(jnp.float32) + middle_back
    branch_low = middle_grad.astype(jnp.bfloat16)
    attended_grad = against(branch_low, outward_full).astype(jnp.bfloat16)
    query_back, kv_back, normed_all, attended_all, branch_all = attend_backward(
        attended_grad, query_here, kv_here, mixed_here, logs, normed, attended, branch_low,
        group, slices, heads_here, block,
    )
    query_back, kv_back, normed_all, attended_all, branch_all, down_mine, gate_up_mine = (
        lax.optimization_barrier(
            (query_back, kv_back, normed_all, attended_all, branch_all, down_mine, gate_up_mine)
        )
    )
    outward_mine = scatter_rows(
        outer(attended_all.reshape(-1, D), branch_all.reshape(-1, D // slices)).astype(jnp.bfloat16)
    )

    def column_slices(field):
        width = field.shape[1] // slices
        return field.reshape(local, slices, width).transpose(1, 0, 2)

    query_grad = rotate(
        query_back.astype(jnp.float32).reshape(local, HEADS, HEAD_DIM), position, -1.0
    )
    kv_grad = kv_back.astype(jnp.float32).reshape(KV_HEADS, copies, local, 2 * HEAD_DIM)
    kv_grad = jnp.sum(kv_grad, axis=1).transpose(1, 0, 2)
    key_grad = rotate(kv_grad[:, :, :HEAD_DIM], position, -1.0)
    value_grad = kv_grad[:, :, HEAD_DIM:]
    inward_grad = jnp.concatenate(
        [
            query_grad.reshape(local, D),
            key_grad.reshape(local, kv_width),
            value_grad.reshape(local, kv_width),
        ],
        axis=-1,
    ).astype(jnp.bfloat16)
    inward_grad_blocks = exchange_swap(column_slices(inward_grad), "fsdp")
    normed_grad = against(inward_grad, inward_full)
    rows_back, gain_first_grad = norm_back(rows, scale_first, gain_first, normed_grad)
    input_grad = middle_grad + rows_back

    inward_grad_blocks, gain_first_grad, out_parts, down_mine, gate_up_mine = (
        lax.optimization_barrier(
            (inward_grad_blocks, gain_first_grad, out_parts, down_mine, gate_up_mine)
        )
    )
    gain_grads = jnp.stack([gain_first_grad, gain_second_grad], axis=1)
    gain_grads = jnp.pad(gain_grads.astype(jnp.bfloat16), ((0, 0), (0, 126)))
    inward_partial = outer(normed_all.reshape(-1, D), jnp.concatenate(inward_grad_blocks, axis=0))
    inward_partial = inward_partial.astype(jnp.bfloat16)
    slice_cols = inward_partial.shape[1]
    inward_mine = scatter_rows(jnp.concatenate([inward_partial, gain_grads], axis=1))
    out_parts = [out_parts[0]] + [swap(out_parts[d], "fsdp", d) for d in range(1, slices)]
    result = middle + add_up(out_parts)
    back = return_columns(jnp.concatenate([gate_up_mine, down_mine], axis=1))
    gate_back = [piece[:, :ff_cols] for piece in back]
    up_back = [piece[:, ff_cols : 2 * ff_cols] for piece in back]
    down_back = [piece[:, 2 * ff_cols :] for piece in back]
    inward_back = return_columns(jnp.concatenate([inward_mine, outward_mine], axis=1))
    outward_back = [piece[:, slice_cols + 128 :] for piece in inward_back]
    gains_sum = add_up([piece[:, slice_cols : slice_cols + 2] for piece in inward_back])
    gains_sum = jnp.transpose(gains_sum)
    inward_back = [piece[:, :slice_cols] for piece in inward_back]
    inward_sum = jnp.concatenate(inward_back, axis=1).astype(jnp.float32)
    outward_sum = jnp.concatenate(outward_back, axis=1).astype(jnp.float32)
    gate_up_sum = jnp.concatenate(gate_back + up_back, axis=1).astype(jnp.float32)
    down_sum = jnp.concatenate(down_back, axis=1).astype(jnp.float32)
    first_inward_new, second_inward_new, inward_new = adam_update(
        w_inward, first_inward, second_inward, inward_sum, 0.02, weight_decay
    )
    first_outward_new, second_outward_new, outward_new = adam_update(
        w_outward, first_outward, second_outward, outward_sum, 0.15, weight_decay
    )
    first_gate_up_new, second_gate_up_new, gate_up_new = adam_update(
        w_gate_up, first_gate_up, second_gate_up, gate_up_sum, 0.02, weight_decay
    )
    first_down_new, second_down_new, down_new = adam_update(
        w_down, first_down, second_down, down_sum, 0.015, weight_decay
    )
    first_gains_new, second_gains_new, gains_new = adam_update(
        gains, first_gains, second_gains, gains_sum, 0.6, 0.0
    )
    return (
        result[None].astype(jnp.bfloat16),
        input_grad[None],
        first_inward_new,
        second_inward_new,
        inward_new,
        first_outward_new,
        second_outward_new,
        outward_new,
        first_gate_up_new,
        second_gate_up_new,
        gate_up_new,
        first_down_new,
        second_down_new,
        down_new,
        first_gains_new,
        second_gains_new,
        gains_new,
    )


def solution(mesh):
    in_specs = (
        P("fsdp", "seq", None),
        P("fsdp", "seq", None),
        P(("seq", "fsdp"), None),
        P(("seq", "fsdp"), None),
        P(("seq", "fsdp"), None),
        P(("seq", "fsdp"), None),
        P(None, ("seq", "fsdp")),
        P(("seq", "fsdp"), None),
        P(("seq", "fsdp"), None),
        P(("seq", "fsdp"), None),
        P(("seq", "fsdp"), None),
        P(None, ("seq", "fsdp")),
        P(("seq", "fsdp"), None),
        P(("seq", "fsdp"), None),
        P(("seq", "fsdp"), None),
        P(("seq", "fsdp"), None),
        P(None, ("seq", "fsdp")),
    )
    out_specs = (
        P("fsdp", "seq", None),
        P("fsdp", "seq", None),
        P(("seq", "fsdp"), None),
        P(("seq", "fsdp"), None),
        P(("seq", "fsdp"), None),
        P(("seq", "fsdp"), None),
        P(("seq", "fsdp"), None),
        P(("seq", "fsdp"), None),
        P(("seq", "fsdp"), None),
        P(("seq", "fsdp"), None),
        P(("seq", "fsdp"), None),
        P(("seq", "fsdp"), None),
        P(("seq", "fsdp"), None),
        P(("seq", "fsdp"), None),
        P(None, ("seq", "fsdp")),
        P(None, ("seq", "fsdp")),
        P(None, ("seq", "fsdp")),
    )
    return jax.shard_map(body, mesh=mesh, in_specs=in_specs, out_specs=out_specs, check_vma=False)
```

```python
import functools

import jax
import jax.numpy as jnp
from jax import lax
from jax.experimental import pallas as pl
from jax.experimental.pallas import tpu as pltpu
from jax.sharding import PartitionSpec as P

D = 2048
FF = 5632
HEADS = 32
KV_HEADS = 4
HEAD_DIM = 64
STEP = 10


epsilon = 1e-05
adam_epsilon = 1e-08
beta_first = 0.9
beta_second = 0.95
rope_base = 10000.0
weight_decay = 0.1
masked_value = -1e30


def rotate(field, position, sign):
    half = field.shape[-1] // 2
    exponent = jnp.arange(half).astype(jnp.float32) * (-2.0 / field.shape[-1])
    frequency = jnp.power(rope_base, exponent)
    angle = position[:, None] * frequency[None, :]
    cosine = jnp.cos(angle)[:, None, :]
    sine = sign * jnp.sin(angle)[:, None, :]
    first = field[..., :half]
    second = field[..., half:]
    return jnp.concatenate(
        [first * cosine - second * sine, second * cosine + first * sine], axis=-1
    )


def rms_scale(rows):
    return lax.rsqrt(jnp.mean(rows * rows, axis=-1, keepdims=True) + epsilon)


def norm_back(rows, scale_rows, gain, grad):
    weighted = grad * gain
    row_grad = scale_rows * weighted - rows * scale_rows**3 * jnp.mean(
        weighted * rows, axis=-1, keepdims=True
    )
    gain_grad = jnp.sum(grad * rows * scale_rows, axis=0)
    return (row_grad, gain_grad)


def dot(left, right):
    return jnp.dot(left, right, preferred_element_type=jnp.float32)


def outer(left, right):
    return lax.dot_general(
        left, right, (((0,), (0,)), ((), ())), preferred_element_type=jnp.float32
    )


def against(left, right):
    return lax.dot_general(
        left, right, (((1,), (1,)), ((), ())), preferred_element_type=jnp.float32
    )


def stack_heads(field, heads):
    return jnp.concatenate(
        [field[:, h * HEAD_DIM : (h + 1) * HEAD_DIM] for h in range(heads)], axis=0
    )


def unstack_heads(field, heads):
    rows = field.shape[0] // heads
    return jnp.concatenate([field[h * rows : (h + 1) * rows] for h in range(heads)], axis=1)


def masked_scores(keys, queries, block, first):
    scores = against(keys, queries)
    key_place = lax.broadcasted_iota(jnp.int32, scores.shape, 0)
    query_place = first + lax.rem(lax.broadcasted_iota(jnp.int32, scores.shape, 1), block)
    return jnp.where(key_place <= query_place, scores, masked_value)


def remote(source, target, send, arrive, axis, device):
    return pltpu.make_async_remote_copy(
        src_ref=source,
        dst_ref=target,
        send_sem=send,
        recv_sem=arrive,
        device_id={axis: device},
        device_id_type=pl.DeviceIdType.MESH,
    )


VMEM = pl.BlockSpec(memory_space=pltpu.VMEM)


def core_pair(index):
    return index // 2, lax.rem(index, 2)


def pass_rows_start(rows, send, come, near):
    s = lax.axis_index("seq")
    for d in [1] + near:
        rows_copy(rows, send, come, d, s, s ^ d).start()


def pass_rows_finish(rows, send, come, forward, passed, near):
    s = lax.axis_index("seq")
    for d in near:
        rows_copy(rows, send, come, d, s ^ d, s ^ d).wait_recv()
        rows_copy(rows, forward, passed, d, s ^ d, s ^ 1).start()
    rows_copy(rows, send, come, 1, s ^ 1, s ^ 1).wait()
    for d in near:
        rows_copy(rows, send, come, d, s, s ^ d).wait_send()
        rows_copy(rows, forward, passed, d, s ^ d, s ^ 1).wait_send()
        rows_copy(rows, forward, passed, d, s ^ 1 ^ d, s ^ 1).wait_recv()


def rows_copy(rows, send, come, d, owner, target):
    place, half = core_pair(owner)
    return remote(rows.at[place, half], rows.at[place, half], send.at[d], come.at[d], "seq", target)


def share_kernel(
    in_ref, gain_ref, gate_up_ref, down_ref, feed_gate_up, feed_down, in_rows,
    low_gate_up, low_down, send_feed, come_feed, send_in, come_in, pass_in, passed_in,
):
    group, slices = lax.axis_size("seq"), lax.axis_size("fsdp")
    s, f = lax.axis_index("seq"), lax.axis_index("fsdp")
    pair, core = core_pair(s)
    depth, inward_cols = in_ref.shape
    ff_cols = FF // slices
    near = list(range(2, group, 2))
    in_rows[pair, core, :, pl.ds(0, inward_cols)] = in_ref[...].astype(jnp.bfloat16)
    in_rows[pair, core, :, pl.ds(inward_cols, 128)] = gain_ref[...]
    meet_spread(near)
    pass_rows_start(in_rows, send_in, come_in, near)
    for t in range(slices):
        columns = pl.ds(t * ff_cols, ff_cols)
        low_gate_up[t, :, pl.ds(0, ff_cols)] = gate_up_ref[:, columns].astype(jnp.bfloat16)
        low_gate_up[t, :, pl.ds(ff_cols, ff_cols)] = gate_up_ref[
            :, pl.ds(FF + t * ff_cols, ff_cols)
        ].astype(jnp.bfloat16)
        low_down[t] = down_ref[:, columns].astype(jnp.bfloat16)

    feeds = ((low_gate_up, feed_gate_up), (low_down, feed_down))

    def feed_copy(k, d, owner, target):
        low, feed = feeds[k]
        return remote(
            low.at[target],
            feed.at[pl.ds(pl.multiple_of(owner * depth, depth), depth), :],
            send_feed.at[k, d], come_feed.at[k, d], "fsdp", target,
        )

    for d in range(1, slices):
        for k in range(2):
            feed_copy(k, d, f, f ^ d).start()
    mine = pl.ds(pl.multiple_of(f * depth, depth), depth)
    for low, feed in feeds:
        feed[mine, :] = low[f]
    pass_rows_finish(in_rows, send_in, come_in, pass_in, passed_in, near)
    for d in range(1, slices):
        for k in range(2):
            feed_copy(k, d, f ^ d, f ^ d).wait()


def share_weights(w_inward, gain_columns, w_gate_up, w_down, group, slices):
    depth = w_inward.shape[0]
    ff_cols = FF // slices
    width = w_inward.shape[1] + 128
    sems = [pltpu.SemaphoreType.DMA((2, slices))] * 2 + [pltpu.SemaphoreType.DMA((group,))] * 4
    return pl.pallas_call(
        share_kernel,
        in_specs=[VMEM] * 4,
        out_specs=[VMEM] * 3,
        out_shape=[
            jax.ShapeDtypeStruct((slices * depth, 2 * ff_cols), jnp.bfloat16),
            jax.ShapeDtypeStruct((slices * depth, ff_cols), jnp.bfloat16),
            jax.ShapeDtypeStruct((group // 2, 2, depth, width), jnp.bfloat16),
        ],
        scratch_shapes=[
            pltpu.VMEM((slices, depth, 2 * ff_cols), jnp.bfloat16),
            pltpu.VMEM((slices, depth, ff_cols), jnp.bfloat16),
        ]
        + sems,
        compiler_params=pltpu.CompilerParams(
            vmem_limit_bytes=48 << 20, collective_id=2, has_side_effects=True
        ),
    )(w_inward, gain_columns, w_gate_up, w_down)


def block_order():
    slices = lax.axis_size("fsdp")
    if slices != 4:
        return list(range(1, slices))
    core = lax.rem(lax.axis_index("seq"), 2)
    return [2 - core, 1 + core, 3]


def gather_blocks(source, place, send, come):
    f, slices = lax.axis_index("fsdp"), lax.axis_size("fsdp")
    order = block_order()
    square = slices == 4
    near = [1, 2] if square else order

    def direct(d, owner, holder):
        return remote(source, place(owner, holder), send.at[d], come.at[d], "fsdp", f ^ d)

    def relay(owner, holder):
        return remote(
            place(order[0], 0), place(owner, holder), send.at[3], come.at[3], "fsdp", f ^ order[1]
        )

    def start():
        for d in near:
            direct(d, 0, d).start()

    def take(turn):
        if square and turn == 2:
            relay(3, 0).wait_recv()
        else:
            direct(order[turn], order[turn], 0).wait_recv()
        if square and turn == 0:
            relay(order[0], order[1]).start()

    def finish():
        for d in near:
            direct(d, 0, d).wait_send()
        if square:
            relay(order[0], order[1]).wait_send()

    return order, start, take, finish


def spread_copies(rows, full, send, come, forward, passed):
    s, f = lax.axis_index("seq"), lax.axis_index("fsdp")
    core = lax.rem(s, 2)
    order, begin, take, sent = gather_blocks(
        rows.at[:, core], lambda owner, holder: full.at[:, core, f ^ owner], send, come
    )

    def second(d, half):
        block = full.at[:, half, f ^ d]
        return remote(block, block, forward.at[d], passed.at[d], "seq", s ^ 1)

    def local():
        full[:, :, f] = rows[...]

    def early():
        take(0)
        second(order[0], core).start()

    def finish():
        for turn, d in enumerate(order[1:]):
            take(turn + 1)
            second(d, core).start()
        sent()
        for d in range(1, lax.axis_size("fsdp")):
            second(d, core).wait_send()
            second(d, 1 - core).wait_recv()

    return begin, local, early, finish


def meet_spread(extra=()):
    barrier = pltpu.get_barrier_semaphore()
    s, f = lax.axis_index("seq"), lax.axis_index("fsdp")
    near = sorted({1, *extra})
    slices = lax.axis_size("fsdp")
    for d in near:
        pl.semaphore_signal(
            barrier, inc=1, device_id={"seq": s ^ d}, device_id_type=pl.DeviceIdType.MESH
        )
    for d in range(1, slices):
        pl.semaphore_signal(
            barrier, inc=1, device_id={"fsdp": f ^ d}, device_id_type=pl.DeviceIdType.MESH
        )
    pl.semaphore_wait(barrier, len(near) + slices - 1)


def spread_kernel(
    rows, out_ref, full, out_rows, send, come, forward, passed,
    send_out, come_out, pass_out, passed_out,
):
    near = list(range(2, lax.axis_size("seq"), 2))
    pair, core = core_pair(lax.axis_index("seq"))
    meet_spread(near)
    start, local, early, finish = spread_copies(rows, full, send, come, forward, passed)
    start()
    out_rows[pair, core] = out_ref[...].astype(jnp.bfloat16)
    pass_rows_start(out_rows, send_out, come_out, near)
    local()
    early()
    pass_rows_finish(out_rows, send_out, come_out, pass_out, passed_out, near)
    finish()


def spread_rows(rows, w_outward, slices):
    pairs, two, depth, width = rows.shape
    full, out_rows = pl.pallas_call(
        spread_kernel,
        in_specs=[VMEM] * 2,
        out_specs=[VMEM] * 2,
        out_shape=[
            jax.ShapeDtypeStruct((pairs, two, slices, depth, width), rows.dtype),
            jax.ShapeDtypeStruct((pairs, two, depth, w_outward.shape[1]), rows.dtype),
        ],
        scratch_shapes=[pltpu.SemaphoreType.DMA((slices,))] * 4
        + [pltpu.SemaphoreType.DMA((2 * pairs,))] * 4,
        compiler_params=pltpu.CompilerParams(
            vmem_limit_bytes=48 << 20, collective_id=3, has_side_effects=True
        ),
    )(rows, w_outward)
    return full.reshape(pairs * two * slices * depth, width), out_rows


def forward_kernel(
    query_ref, kv_ref, out_rows, kv_all, mixed_ref, logs, out_full,
    queries, largest, total, mixed,
    send_kv, come_kv, pass_kv, passed_kv, send_rows, come_rows, pass_rows, passed_rows,
):
    group, s = lax.axis_size("seq"), lax.axis_index("seq")
    place, core = core_pair(s)
    local = query_ref.shape[0]
    per_head = HEADS // KV_HEADS
    width, pair = per_head * HEAD_DIM, 2 * HEAD_DIM
    near = list(range(2, group, 2))
    meet_spread(range(1, group))
    spread_start, spread_local, spread_early, spread_finish = spread_copies(
        out_rows, out_full, send_rows, come_rows, pass_rows, passed_rows
    )

    def kv_copy(d, owner, target):
        chip, half = core_pair(owner)
        return remote(kv_ref, kv_all.at[chip, half], send_kv.at[d], come_kv.at[d], "seq", target)

    def hand_on(chip, half):
        block = kv_all.at[chip, half]
        return remote(block, block, pass_kv.at[chip, half], passed_kv.at[chip, half], "seq", s ^ 1)

    kv_copy(1, s, s ^ 1).start()
    for d in near:

        @pl.when((s ^ d) > s)
        def _():
            kv_copy(d, s, s ^ d).start()

    spread_start()
    kv_all[place, core] = kv_ref[...]
    for h in range(KV_HEADS):
        field = query_ref[:, pl.ds(h * width, width)]
        queries[h] = stack_heads(field, per_head) * jnp.bfloat16(HEAD_DIM**-0.5)
    spread_local()

    def scores_of(h, chip, masked):
        kv = kv_all[chip, :, :, pl.ds(pl.multiple_of(h * pair, pair), pair)]
        kv = kv.reshape(2 * local, pair)
        keys, values = kv[:, :HEAD_DIM], kv[:, HEAD_DIM:]
        if masked:
            return masked_scores(keys, queries[h], local, core * local), values
        return against(keys, queries[h]), values

    def own_chip(h, _):
        scores, values = scores_of(h, place, True)
        new = jnp.max(scores, axis=0, keepdims=True)
        weights = jnp.exp(scores - new)
        largest[h] = new
        total[h] = jnp.sum(weights, axis=0, keepdims=True)
        mixed[h] = outer(values, weights.astype(jnp.bfloat16))
        return 0

    kv_copy(1, s ^ 1, s ^ 1).wait_recv()
    lax.fori_loop(0, KV_HEADS, own_chip, 0)

    def earlier_chip(turn, _):
        chip = place - 1 - turn

        @pl.when(chip == 0)
        def _():
            spread_early()

        owner = 2 * chip + core
        kv_copy(owner ^ s, owner, owner).wait_recv()
        hand_on(chip, core).start()
        hand_on(chip, 1 - core).wait_recv()

        def head(h, _):
            scores, values = scores_of(h, chip, False)
            new = jnp.maximum(largest[h], jnp.max(scores, axis=0, keepdims=True))
            fade = jnp.exp(largest[h] - new)
            weights = jnp.exp(scores - new)
            largest[h] = new
            total[h] = total[h] * fade + jnp.sum(weights, axis=0, keepdims=True)
            mixed[h] = mixed[h] * fade + outer(values, weights.astype(jnp.bfloat16))
            return 0

        lax.fori_loop(0, KV_HEADS, head, 0)
        return 0

    lax.fori_loop(0, place, earlier_chip, 0)

    @pl.when(place == 0)
    def _():
        spread_early()

    for h in range(KV_HEADS):
        logs[h] = largest[h] + jnp.log(total[h])
        mixed_ref[:, pl.ds(h * width, width)] = unstack_heads(
            (mixed[h] / total[h]).T, per_head
        ).astype(mixed_ref.dtype)
    kv_copy(1, s, s ^ 1).wait_send()
    for d in near:

        @pl.when((s ^ d) > s)
        def _():
            kv_copy(d, s, s ^ d).wait_send()

    def handed(chip, _):
        hand_on(chip, core).wait_send()
        return 0

    lax.fori_loop(0, place, handed, 0)
    spread_finish()


def backward_kernel(
    grad_ref, query_ref, mixed_ref, logs, kv_all, branch_ref, normed_ref,
    cosine_ref, sine_ref, cosine_rows, sine_rows,
    inward_grad, inward_slices, attended_all, branch_all, normed_all, kv_grad,
    queries, grads, inner, query_sum, parts, part_come, final_come,
    send_part, come_part, send_final, come_final, send_slice, come_slice,
    send_mixed, come_mixed, send_normed, come_normed,
):
    group, s = lax.axis_size("seq"), lax.axis_index("seq")
    place, core = core_pair(s)
    local = query_ref.shape[0]
    per_head = HEADS // KV_HEADS
    width, pair = per_head * HEAD_DIM, 2 * HEAD_DIM
    scale = HEAD_DIM**-0.5
    slices, f = lax.axis_size("fsdp"), lax.axis_index("fsdp")
    share = branch_all.shape[2]
    meet_spread(range(1, group))

    def slice_copy(d, target):
        columns = pl.ds(pl.multiple_of(target * share, 128), share)
        return remote(
            branch_ref.at[:, columns], branch_all.at[d], send_slice.at[d], come_slice.at[d],
            "fsdp", target,
        )

    gathers = [
        gather_blocks(mixed_ref, lambda owner, holder: attended_all.at[owner ^ holder],
                      send_mixed, come_mixed),
        gather_blocks(normed_ref, lambda owner, holder: normed_all.at[owner ^ holder],
                      send_normed, come_normed),
    ]

    def gathers_early():
        for _, _, take, _ in gathers:
            take(0)

    def part_copy(chip, half):
        return remote(
            parts.at[chip, half], part_come.at[chip], send_part.at[chip], come_part.at[chip],
            "seq", s ^ 1,
        )

    def final_copy(chip, sender):
        return remote(
            parts.at[chip, core], final_come.at[sender], send_final.at[chip], come_final.at[sender],
            "seq", 2 * chip + core,
        )

    for d in range(1, slices):
        slice_copy(d, f ^ d).start()
    for _, begin, _, _ in gathers:
        begin()
    normed_all[0] = normed_ref[...]
    attended_all[0] = mixed_ref[...]
    branch_all[0] = branch_ref[:, pl.ds(pl.multiple_of(f * share, 128), share)]
    for h in range(KV_HEADS):
        columns = pl.ds(h * width, width)
        queries[h] = stack_heads(query_ref[:, columns], per_head) * jnp.bfloat16(scale)
        grad = stack_heads(grad_ref[:, columns], per_head)
        grads[h] = grad
        product = grad.astype(jnp.float32) * stack_heads(mixed_ref[:, columns], per_head).astype(
            jnp.float32
        )
        inner[h] = jnp.sum(product.T, axis=0, keepdims=True)
    query_sum[...] = jnp.zeros_like(query_sum)

    def head_grads(h, chip, masked):
        columns = pl.ds(pl.multiple_of(h * pair, pair), pair)
        kv = kv_all[chip, :, :, columns].reshape(2 * local, pair)
        keys, values = kv[:, :HEAD_DIM], kv[:, HEAD_DIM:]
        if masked:
            scores = masked_scores(keys, queries[h], local, core * local)
        else:
            scores = against(keys, queries[h])
        shares = jnp.exp(scores - logs[h])
        share_grad = against(values, grads[h])
        score_grad = (shares * (share_grad - inner[h])).astype(jnp.bfloat16)
        value_grad = dot(shares.astype(jnp.bfloat16), grads[h])
        key_grad = dot(score_grad, queries[h])
        part = jnp.concatenate([key_grad, value_grad], axis=1).astype(jnp.bfloat16)
        parts[chip, :, :, columns] = part.reshape(2, local, pair)
        query_sum[h] += outer(keys, score_grad)
        return 0

    def finish_chip(chip):
        part_copy(chip, core).wait_recv()
        parts[chip, core] = (
            parts[chip, core].astype(jnp.float32) + part_come[chip].astype(jnp.float32)
        ).astype(jnp.bfloat16)
        final_copy(chip, place).start()

    def earlier_chip(chip, _):
        @pl.when(chip == place - 1)
        def _():
            gathers_early()

        lax.fori_loop(0, KV_HEADS, lambda h, c: head_grads(h, chip, False), 0)
        part_copy(chip, 1 - core).start()

        @pl.when(chip > 0)
        def _():
            finish_chip(chip - 1)

        return 0

    lax.fori_loop(0, place, earlier_chip, 0)
    lax.fori_loop(0, KV_HEADS, lambda h, c: head_grads(h, place, True), 0)

    @pl.when(core == 1)
    def _():
        part_copy(place, 0).start()

    @pl.when(place == 0)
    def _():
        gathers_early()

    @pl.when(place > 0)
    def _():
        finish_chip(place - 1)

    half = HEAD_DIM // 2
    for h in range(KV_HEADS):
        total = query_sum[h] * scale
        one, two = total[:half], total[half:]
        turned = jnp.concatenate(
            [
                one * cosine_ref[...] + two * sine_ref[...],
                two * cosine_ref[...] - one * sine_ref[...],
            ],
            axis=0,
        )
        inward_grad[:, pl.ds(h * width, width)] = unstack_heads(turned.T, per_head).astype(
            jnp.bfloat16
        )
    kv_grad[...] = parts[place, core].astype(jnp.float32)

    @pl.when(core == 0)
    def _():
        part_copy(place, 0).wait_recv()
        kv_grad[...] += part_come[place].astype(jnp.float32)

    def later_chip(chip, _):
        final_copy(place, chip).wait_recv()
        kv_grad[...] += final_come[chip].astype(jnp.float32)
        return 0

    lax.fori_loop(place + 1, group // 2, later_chip, 0)
    key_grads, value_grads = [], []
    for h in range(KV_HEADS):
        field = kv_grad[:, pl.ds(h * pair, pair)]
        one, two = field[:, :half], field[:, half:HEAD_DIM]
        key_grads.append(one * cosine_rows[...] + two * sine_rows[...])
        key_grads.append(two * cosine_rows[...] - one * sine_rows[...])
        value_grads.append(field[:, HEAD_DIM:])
    inward_grad[:, pl.ds(HEADS * HEAD_DIM, 2 * KV_HEADS * HEAD_DIM)] = jnp.concatenate(
        key_grads + value_grads, axis=1
    ).astype(jnp.bfloat16)
    part_cols = inward_slices.shape[2]
    for t in range(slices):
        inward_slices[t] = inward_grad[:, pl.ds(t * part_cols, part_cols)]

    def sent(chip, _):
        part_copy(chip, 1 - core).wait_send()
        final_copy(chip, place).wait_send()
        return 0

    lax.fori_loop(0, place, sent, 0)

    @pl.when(core == 1)
    def _():
        part_copy(place, 0).wait_send()

    for d in range(1, slices):
        slice_copy(d, f ^ d).wait()
    for order, _, take, finish in gathers:
        for turn in range(1, len(order)):
            take(turn)
        finish()


def attend_forward(query, kv, out_rows, group, slices):
    local, width = query.shape
    per_head = HEADS // KV_HEADS
    columns = per_head * local
    pairs_seq, _, depth, _ = out_rows.shape
    tiles = KV_HEADS * group * columns * local
    return pl.pallas_call(
        forward_kernel,
        in_specs=[VMEM] * 3,
        out_specs=[VMEM] * 4,
        out_shape=[
            jax.ShapeDtypeStruct((group // 2, 2, local, kv.shape[1]), jnp.bfloat16),
            jax.ShapeDtypeStruct((local, width), jnp.bfloat16),
            jax.ShapeDtypeStruct((KV_HEADS, 1, columns), jnp.float32),
            jax.ShapeDtypeStruct(
                (pairs_seq, 2, slices, depth, out_rows.shape[3]), jnp.bfloat16
            ),
        ],
        scratch_shapes=[
            pltpu.VMEM((KV_HEADS, columns, HEAD_DIM), jnp.bfloat16),
            pltpu.VMEM((KV_HEADS, 1, columns), jnp.float32),
            pltpu.VMEM((KV_HEADS, 1, columns), jnp.float32),
            pltpu.VMEM((KV_HEADS, HEAD_DIM, columns), jnp.float32),
        ]
        + [pltpu.SemaphoreType.DMA((group,))] * 2
        + [pltpu.SemaphoreType.DMA((group // 2, 2))] * 2
        + [pltpu.SemaphoreType.DMA((slices,))] * 4,
        compiler_params=pltpu.CompilerParams(
            vmem_limit_bytes=56 << 20, collective_id=0, has_side_effects=True
        ),
        cost_estimate=pl.CostEstimate(
            flops=tiles * HEAD_DIM * 80, bytes_accessed=20 << 20, transcendentals=tiles
        ),
    )(query, kv, out_rows)


def attend_backward(
    grads, query, mixed, logs, kv_all, branch, normed, cosine, sine, group, slices
):
    local, features = branch.shape
    per_head = HEADS // KV_HEADS
    columns = per_head * local
    kv_cols = kv_all.shape[3]
    inward_cols = features + kv_cols
    tiles = KV_HEADS * group * columns * local
    gathered = jax.ShapeDtypeStruct((slices, local, features), jnp.bfloat16)
    stacked = pltpu.VMEM((KV_HEADS, columns, HEAD_DIM), jnp.bfloat16)
    one_half = pltpu.VMEM((group // 2, local, kv_cols), jnp.bfloat16)
    return pl.pallas_call(
        backward_kernel,
        in_specs=[VMEM] * 11,
        out_specs=[VMEM] * 5,
        out_shape=[
            jax.ShapeDtypeStruct((local, inward_cols), jnp.bfloat16),
            jax.ShapeDtypeStruct((slices, local, inward_cols // slices), jnp.bfloat16),
            gathered,
            jax.ShapeDtypeStruct((slices, local, features // slices), jnp.bfloat16),
            gathered,
        ],
        scratch_shapes=[
            pltpu.VMEM((local, kv_cols), jnp.float32),
            stacked,
            stacked,
            pltpu.VMEM((KV_HEADS, 1, columns), jnp.float32),
            pltpu.VMEM((KV_HEADS, HEAD_DIM, columns), jnp.float32),
            pltpu.VMEM((group // 2, 2, local, kv_cols), jnp.bfloat16),
            one_half,
            one_half,
        ]
        + [pltpu.SemaphoreType.DMA((group // 2,))] * 4
        + [pltpu.SemaphoreType.DMA((slices,))] * 6,
        compiler_params=pltpu.CompilerParams(
            vmem_limit_bytes=60 << 20, collective_id=1, has_side_effects=True
        ),
        cost_estimate=pl.CostEstimate(
            flops=tiles * HEAD_DIM * 80, bytes_accessed=20 << 20, transcendentals=tiles
        ),
    )(
        grads, query, mixed, logs, kv_all, branch, normed,
        jnp.tile(cosine.T, (1, per_head)), jnp.tile(sine.T, (1, per_head)), cosine, sine,
    )


def meet_slices():
    slices, f = lax.axis_size("fsdp"), lax.axis_index("fsdp")
    barrier = pltpu.get_barrier_semaphore()
    for d in range(1, slices):
        pl.semaphore_signal(
            barrier, inc=1, device_id={"fsdp": f ^ d}, device_id_type=pl.DeviceIdType.MESH
        )
    pl.semaphore_wait(barrier, slices - 1)


def row_copy(stage, target, sem, r):
    width = stage.shape[0]
    rows = pl.ds(pl.multiple_of(r * width, width), width)
    return pltpu.make_async_copy(stage, target.at[rows, :], sem)


def grad_rows(field, grads, target, stage, sems):
    width = stage.shape[1]
    steps = target.shape[0] // width

    def step(r, _):
        columns = pl.ds(pl.multiple_of(r * width, width), width)
        slot = lax.rem(r, 2)
        left = field[:, :, columns].reshape(grads[0].shape[0], width)

        @pl.when(r > 1)
        def _():
            row_copy(stage.at[slot], target, sems.at[slot], r - 2).wait()

        for k, grad in enumerate(grads):
            units = grad.shape[1]
            stage[slot, :, pl.ds(k * units, units)] = outer(left, grad[...]).astype(jnp.bfloat16)
        row_copy(stage.at[slot], target, sems.at[slot], r).start()
        return 0

    lax.fori_loop(0, steps, step, 0)
    for r in (steps - 2, steps - 1):
        row_copy(stage.at[r % 2], target, sems.at[r % 2], r).wait()


def feed_first_kernel(
    x_ref, dy_ref, gate_up_ref, x_all, gate_all, up_all, hidden, down_grad_out,
    gate_sum, up_sum, grad_stage, send_x, come_x, grad_sem, *, strip
):
    slices, f = lax.axis_size("fsdp"), lax.axis_index("fsdp")
    local = x_ref.shape[0]
    meet_slices()

    order, begin, take, sent = gather_blocks(
        x_ref, lambda owner, holder: x_all.at[owner ^ holder], send_x, come_x
    )
    begin()
    x_all[0] = x_ref[...]

    def token_block(turn, d):
        for i in range(slices - 1):

            @pl.when(turn == i + 1)
            def _():
                take(i)

        x = x_all[d]
        units = hidden.shape[1]
        gate_sum[...] = dot(x, gate_up_ref[:, pl.ds(0, units)])
        up_sum[...] = dot(x, gate_up_ref[:, pl.ds(units, units)])

        def part(i, _):
            rows = pl.ds(pl.multiple_of(i * strip, strip), strip)
            place = pl.ds(pl.multiple_of(d * local + i * strip, strip), strip)
            gate, up = gate_sum[rows, :], up_sum[rows, :]
            hidden[place, :] = (gate / (1.0 + jnp.exp(-gate)) * up).astype(jnp.bfloat16)
            gate_all[place, :] = gate.astype(jnp.bfloat16)
            up_all[place, :] = up.astype(jnp.bfloat16)
            return 0

        lax.fori_loop(0, local // strip, part, 0)
        following = 0
        for i in reversed(range(slices - 1)):
            following = jnp.where(turn == i, order[i], following)
        return following

    lax.fori_loop(0, slices, token_block, jnp.int32(0))
    grad_rows(dy_ref, [hidden], down_grad_out, grad_stage, grad_sem)
    sent()


def feed_second_kernel(
    x_ref, dy_ref, gate_all, up_all, hidden, gate_up_ref, down_ref,
    back_ref, out_parts, gate_up_grad_out,
    gate_grad, up_grad, hidden_sum, back_send, back_come, out_stage, grad_stage,
    send_back, come_back, out_sem, grad_sem, *, strip
):
    slices, f = lax.axis_size("fsdp"), lax.axis_index("fsdp")
    local = back_ref.shape[0]
    meet_slices()

    square = slices == 4
    order = block_order()
    first, second = (order[1], order[0]) if square else (None, None)
    turns = [3, second, first, 0] if square else list(range(slices - 1, -1, -1))

    def back_copy(d, target, landing):
        return remote(
            back_send.at[d], back_come.at[landing - 1], send_back.at[d], come_back.at[landing],
            "fsdp", f ^ target,
        )

    def out_copy(slot, d):
        return pltpu.make_async_copy(out_stage.at[slot], out_parts.at[d], out_sem.at[slot])

    def token_block(turn, carry):
        d, before = carry
        place = pl.ds(pl.multiple_of(d * local, local), local)
        hidden_sum[...] = dot(dy_ref[d], down_ref[...])

        def part(i, _):
            rows = pl.ds(pl.multiple_of(i * strip, strip), strip)
            here = pl.ds(pl.multiple_of(d * local + i * strip, strip), strip)
            gate = gate_all[here, :].astype(jnp.float32)
            up = up_all[here, :].astype(jnp.float32)
            sigmoid = 1.0 / (1.0 + jnp.exp(-gate))
            grad = hidden_sum[rows, :]
            gate_grad[here, :] = (
                grad * up * sigmoid * (1.0 + gate * (1.0 - sigmoid))
            ).astype(jnp.bfloat16)
            up_grad[here, :] = (grad * gate * sigmoid).astype(jnp.bfloat16)
            return 0

        lax.fori_loop(0, local // strip, part, 0)
        units = hidden.shape[1]
        back = against(gate_grad[place, :], gate_up_ref[:, pl.ds(0, units)])
        back = back + against(up_grad[place, :], gate_up_ref[:, pl.ds(units, units)])
        back_send[d] = back.astype(jnp.bfloat16)
        if square:

            @pl.when(turn == 0)
            def _():
                back_copy(3, first, 3).start()

            @pl.when(turn == 2)
            def _():
                back_copy(3, first, 3).wait_recv()
                back_send[second] = (
                    back_send[second].astype(jnp.float32) + back_come[2].astype(jnp.float32)
                ).astype(jnp.bfloat16)
                back_copy(second, second, second).start()
                back_copy(first, first, first).start()

        else:

            @pl.when(d > 0)
            def _():
                back_copy(d, d, d).start()

        @pl.when(turn > 1)
        def _():
            out_copy(lax.rem(turn, 2), before).wait()

        out_stage[lax.rem(turn, 2)] = against(hidden[place, :], down_ref[...]).astype(jnp.bfloat16)
        out_copy(lax.rem(turn, 2), d).start()
        following = 0
        for i in reversed(range(slices - 1)):
            following = jnp.where(turn == i, turns[i + 1], following)
        return following, d

    lax.fori_loop(0, slices, token_block, (jnp.int32(turns[0]), jnp.int32(0)))
    out_copy(0, 0).wait()
    out_copy(1, 0).wait()
    grad_rows(x_ref, [gate_grad, up_grad], gate_up_grad_out, grad_stage, grad_sem)
    if square:
        back_copy(3, first, 3).wait_send()
    for d in (1, 2) if square else range(1, slices):
        back_copy(d, d, d).wait()
    home = [back_send[0]] + [back_come[d - 1] for d in ((1, 2) if square else range(1, slices))]
    back_ref[...] = functools.reduce(jnp.add, [p.astype(jnp.float32) for p in home])


ANY = pl.BlockSpec(memory_space=pl.ANY)


def feed_first(x, upstream_all, gate_up_slice):
    slices, local, width = upstream_all.shape
    ff_cols = gate_up_slice.shape[1] // 2
    tokens = slices * local
    units = jax.ShapeDtypeStruct((tokens, ff_cols), jnp.bfloat16)
    high = pltpu.VMEM((local, ff_cols), jnp.float32)
    sems = pltpu.SemaphoreType.DMA((slices,))
    return pl.pallas_call(
        functools.partial(feed_first_kernel, strip=32),
        in_specs=[VMEM] * 3,
        out_specs=[VMEM] * 4 + [ANY],
        out_shape=[
            jax.ShapeDtypeStruct((slices, local, width), jnp.bfloat16),
            units,
            units,
            units,
            jax.ShapeDtypeStruct((width, ff_cols), jnp.bfloat16),
        ],
        scratch_shapes=[high, high, pltpu.VMEM((2, 256, ff_cols), jnp.bfloat16)]
        + [sems] * 2
        + [pltpu.SemaphoreType.DMA((2,))],
        compiler_params=pltpu.CompilerParams(
            vmem_limit_bytes=60 << 20, collective_id=4, has_side_effects=True
        ),
        cost_estimate=pl.CostEstimate(
            flops=10 * tokens * width * ff_cols, bytes_accessed=30 << 20, transcendentals=0
        ),
    )(x, upstream_all, gate_up_slice)


def feed_second(
    x_all, upstream_all, gate_all, up_all, hidden, gate_up_slice, down_slice
):
    slices, local, width = upstream_all.shape
    ff_cols = gate_up_slice.shape[1] // 2
    tokens = slices * local
    blocks = pltpu.VMEM((slices, local, width), jnp.bfloat16)
    low = pltpu.VMEM((tokens, ff_cols), jnp.bfloat16)
    sems = pltpu.SemaphoreType.DMA((slices,))
    return pl.pallas_call(
        functools.partial(feed_second_kernel, strip=32),
        in_specs=[VMEM] * 7,
        out_specs=[VMEM] + [ANY] * 2,
        out_shape=[
            jax.ShapeDtypeStruct((local, width), jnp.float32),
            jax.ShapeDtypeStruct((slices, local, width), jnp.bfloat16),
            jax.ShapeDtypeStruct((width, 2 * ff_cols), jnp.bfloat16),
        ],
        scratch_shapes=[low, low, pltpu.VMEM((local, ff_cols), jnp.float32), blocks]
        + [
            pltpu.VMEM((slices - 1, local, width), jnp.bfloat16),
            pltpu.VMEM((2, local, width), jnp.bfloat16),
            pltpu.VMEM((2, 256, 2 * ff_cols), jnp.bfloat16),
        ]
        + [sems] * 2
        + [pltpu.SemaphoreType.DMA((2,)), pltpu.SemaphoreType.DMA((2,))],
        compiler_params=pltpu.CompilerParams(
            vmem_limit_bytes=62 << 20, collective_id=5, has_side_effects=True
        ),
        cost_estimate=pl.CostEstimate(
            flops=20 * tokens * width * ff_cols, bytes_accessed=40 << 20, transcendentals=0
        ),
    )(x_all, upstream_all, gate_all, up_all, hidden, gate_up_slice, down_slice)


def home_kernel(*refs, count, moves, summed):
    slices, f = lax.axis_size("fsdp"), lax.axis_index("fsdp")
    sources, rest = refs[:count], refs[count:]
    results, rest = rest[: -(count + 2)], rest[-(count + 2) :]
    landed, (send, come) = rest[:count], rest[count:]
    depth = sources[0].shape[0] // slices
    meet_slices()

    def copy(k, d):
        rows = pl.ds(pl.multiple_of((f ^ d) * depth, depth), depth)
        return remote(
            sources[k].at[rows, :], landed[k].at[d], send.at[k, d], come.at[k, d], "fsdp", f ^ d
        )

    for k in range(count):
        for d in range(1, slices):
            copy(k, d).start()
    for k in range(count):
        landed[k][0] = sources[k][pl.ds(pl.multiple_of(f * depth, depth), depth), :]
    for k in range(count):
        for d in range(1, slices):
            copy(k, d).wait()
    for t in range(slices):
        for source, first, width, result, base in moves:
            results[result][:, pl.ds(base + t * width, width)] = landed[source][
                f ^ t, :, pl.ds(first, width)
            ]
    if summed:
        source, first = summed
        results[-1][...] = functools.reduce(
            jnp.add,
            [landed[source][d, :, pl.ds(first, 128)].astype(jnp.float32) for d in range(slices)],
        )


def bring_home(sources, moves, widths, summed, slices, number):
    depth = sources[0].shape[0] // slices
    shapes = [jax.ShapeDtypeStruct((depth, width), jnp.bfloat16) for width in widths]
    if summed:
        shapes.append(jax.ShapeDtypeStruct((depth, 128), jnp.float32))
    return pl.pallas_call(
        functools.partial(home_kernel, count=len(sources), moves=moves, summed=summed),
        in_specs=[VMEM] * len(sources),
        out_specs=[VMEM] * len(shapes),
        out_shape=shapes,
        scratch_shapes=[pltpu.VMEM((slices, depth, s.shape[1]), jnp.bfloat16) for s in sources]
        + [pltpu.SemaphoreType.DMA((len(sources), slices))] * 2,
        compiler_params=pltpu.CompilerParams(
            vmem_limit_bytes=32 << 20, collective_id=number, has_side_effects=True
        ),
        cost_estimate=pl.CostEstimate(flops=10 << 30, bytes_accessed=4 << 20, transcendentals=0),
    )(*sources)


def swap(piece, axis, offset):
    size = lax.axis_size(axis)
    return lax.ppermute(piece, axis, [(i, i ^ offset) for i in range(size)])


def gather_swap(piece, axis):
    return [piece] + [swap(piece, axis, d) for d in range(1, lax.axis_size(axis))]


def exchange_swap(stack, axis):
    me = lax.axis_index(axis)
    pieces = [
        lax.dynamic_index_in_dim(stack, me ^ d, 0, keepdims=False)
        for d in range(lax.axis_size(axis))
    ]
    return [pieces[0]] + [swap(p, axis, d) for d, p in enumerate(pieces) if d]


def reduce_swap(parts, axis):
    total = parts[0].astype(jnp.float32)
    for d in range(1, len(parts)):
        total = total + swap(parts[d], axis, d).astype(jnp.float32)
    return total


def scatter_rows(partial, after=()):
    partial, *_ = lax.optimization_barrier((partial, *after))
    return lax.psum_scatter(partial, "seq", scatter_dimension=0, tiled=True)


def adam_update(weight, first, second, grad, rate, decay):
    first_new = beta_first * first + (1.0 - beta_first) * grad
    second_new = beta_second * second + (1.0 - beta_second) * grad * grad
    first_hat = first_new / (1.0 - beta_first**STEP)
    second_hat = second_new / (1.0 - beta_second**STEP)
    weight_new = weight - rate * (
        first_hat / (jnp.sqrt(second_hat) + adam_epsilon) + decay * weight
    )
    return (first_new, second_new, weight_new)


def body(
    inputs,
    cotangent,
    w_inward,
    w_outward,
    w_gate_up,
    w_down,
    gains,
    first_inward,
    first_outward,
    first_gate_up,
    first_down,
    first_gains,
    second_inward,
    second_outward,
    second_gate_up,
    second_down,
    second_gains,
):
    rows = inputs[0].astype(jnp.float32)
    upstream = cotangent[0]
    local = rows.shape[0]
    group = lax.axis_size("seq")
    slices = lax.axis_size("fsdp")
    kv_width = KV_HEADS * HEAD_DIM
    inward_cols = D + 2 * kv_width
    ff_cols = FF // slices
    depth = w_inward.shape[0]
    position = (lax.axis_index("seq") * local + jnp.arange(local)).astype(jnp.float32)

    low_gains = jnp.pad(jnp.transpose(gains.astype(jnp.bfloat16)), ((0, 0), (0, 126)))
    feed_gate_up, feed_down, in_rows = share_weights(
        w_inward, low_gains, w_gate_up, w_down, group, slices
    )
    gate_up_slice = lax.all_gather(feed_gate_up, "seq", axis=0, tiled=True)
    inward_gains, out_rows = spread_rows(in_rows, w_outward, slices)
    inward_full = inward_gains[:, :inward_cols]
    gain_first = inward_gains[:, inward_cols].astype(jnp.float32)
    gain_second = inward_gains[:, inward_cols + 1].astype(jnp.float32)

    scale_first = rms_scale(rows)
    normed = (rows * scale_first * gain_first).astype(jnp.bfloat16)
    mixed = dot(normed, inward_full)
    query = rotate(mixed[:, :D].reshape(local, HEADS, HEAD_DIM), position, 1.0).astype(jnp.bfloat16)
    key = rotate(
        mixed[:, D : D + kv_width].reshape(local, KV_HEADS, HEAD_DIM), position, 1.0
    ).astype(jnp.bfloat16)
    value = mixed[:, D + kv_width :].reshape(local, KV_HEADS, HEAD_DIM).astype(jnp.bfloat16)
    kv = jnp.concatenate([key, value], axis=-1).reshape(local, 2 * kv_width)
    query = query.reshape(local, D)
    kv_all, attended, logs, outward_full = attend_forward(query, kv, out_rows, group, slices)
    outward_full = outward_full.reshape(D, D)
    upstream_late, _ = lax.optimization_barrier((upstream, inward_gains))
    upstream_blocks = gather_swap(upstream_late, "fsdp")
    attended, upstream_blocks = lax.optimization_barrier((attended, upstream_blocks))
    down_slice = lax.all_gather(feed_down, "seq", axis=0, tiled=True)
    upstream_all = jnp.stack(upstream_blocks)
    middle = rows + dot(attended, outward_full)
    scale_second = rms_scale(middle)
    normed_second = (middle * scale_second * gain_second).astype(jnp.bfloat16)

    def add_up(parts):
        return functools.reduce(jnp.add, [p.astype(jnp.float32) for p in parts])

    normed_all, gate_all, up_all, hidden, down_partial = feed_first(
        normed_second, upstream_all, gate_up_slice
    )
    normed_second_grad, out_parts, gate_up_partial = feed_second(
        normed_all, upstream_all, gate_all, up_all, hidden, gate_up_slice, down_slice
    )
    down_mine = scatter_rows(down_partial)
    gate_up_mine = scatter_rows(gate_up_partial)
    middle_back, gain_second_grad = norm_back(middle, scale_second, gain_second, normed_second_grad)
    middle_grad = upstream.astype(jnp.float32) + middle_back
    branch_low = middle_grad.astype(jnp.bfloat16)
    attended_grad = against(branch_low, outward_full).astype(jnp.bfloat16)
    exponent = jnp.arange(HEAD_DIM // 2).astype(jnp.float32) * (-2.0 / HEAD_DIM)
    angle = position[:, None] * jnp.power(rope_base, exponent)[None, :]
    inward_grad, inward_slices, attended_all, branch_all, first_all = attend_backward(
        attended_grad, query, attended, logs, kv_all, branch_low, normed,
        jnp.cos(angle), jnp.sin(angle), group, slices,
    )
    out_parts = [out_parts[0]] + [swap(out_parts[d], "fsdp", d) for d in range(1, slices)]
    inward_grad, inward_slices, attended_all, branch_all, first_all, down_mine, out_parts = (
        lax.optimization_barrier(
            (inward_grad, inward_slices, attended_all, branch_all, first_all, down_mine, out_parts)
        )
    )
    result = middle + add_up(out_parts)
    inward_grad_blocks = exchange_swap(inward_slices, "fsdp")
    outward_mine = scatter_rows(
        outer(attended_all.reshape(-1, D), branch_all.reshape(-1, D // slices)).astype(jnp.bfloat16)
    )

    normed_grad = against(inward_grad, inward_full)
    rows_back, gain_first_grad = norm_back(rows, scale_first, gain_first, normed_grad)
    input_grad = middle_grad + rows_back

    inward_grad_blocks, gain_first_grad, down_mine, gate_up_mine = lax.optimization_barrier(
        (inward_grad_blocks, gain_first_grad, down_mine, gate_up_mine)
    )
    gain_grads = jnp.stack([gain_first_grad, gain_second_grad], axis=1)
    gain_grads = jnp.pad(gain_grads.astype(jnp.bfloat16), ((0, 0), (0, 126)))
    inward_partial = outer(first_all.reshape(-1, D), jnp.concatenate(inward_grad_blocks, axis=0))
    inward_partial = inward_partial.astype(jnp.bfloat16)
    slice_cols = inward_partial.shape[1]
    inward_mine = scatter_rows(jnp.concatenate([inward_partial, gain_grads], axis=1))
    gate_up_sum, down_sum = bring_home(
        [gate_up_mine, down_mine],
        [(0, 0, ff_cols, 0, 0), (0, ff_cols, ff_cols, 0, FF), (1, 0, ff_cols, 1, 0)],
        [2 * FF, FF], None, slices, 6,
    )
    inward_sum, outward_sum, gains_sum = bring_home(
        [inward_mine, outward_mine],
        [(0, 0, slice_cols, 0, 0), (1, 0, D // slices, 1, 0)],
        [inward_cols, D], (0, slice_cols), slices, 7,
    )
    gate_up_sum, down_sum, inward_sum, outward_sum = [
        field.astype(jnp.float32) for field in (gate_up_sum, down_sum, inward_sum, outward_sum)
    ]
    gains_sum = jnp.transpose(gains_sum[:, :2])
    first_inward_new, second_inward_new, inward_new = adam_update(
        w_inward, first_inward, second_inward, inward_sum, 0.02, weight_decay
    )
    first_outward_new, second_outward_new, outward_new = adam_update(
        w_outward, first_outward, second_outward, outward_sum, 0.15, weight_decay
    )
    first_gate_up_new, second_gate_up_new, gate_up_new = adam_update(
        w_gate_up, first_gate_up, second_gate_up, gate_up_sum, 0.02, weight_decay
    )
    first_down_new, second_down_new, down_new = adam_update(
        w_down, first_down, second_down, down_sum, 0.015, weight_decay
    )
    first_gains_new, second_gains_new, gains_new = adam_update(
        gains, first_gains, second_gains, gains_sum, 0.6, 0.0
    )
    return (
        result[None].astype(jnp.bfloat16),
        input_grad[None],
        first_inward_new,
        second_inward_new,
        inward_new,
        first_outward_new,
        second_outward_new,
        outward_new,
        first_gate_up_new,
        second_gate_up_new,
        gate_up_new,
        first_down_new,
        second_down_new,
        down_new,
        first_gains_new,
        second_gains_new,
        gains_new,
    )


def solution(mesh):
    in_specs = (
        P("fsdp", "seq", None),
        P("fsdp", "seq", None),
        P(("seq", "fsdp"), None),
        P(("seq", "fsdp"), None),
        P(("seq", "fsdp"), None),
        P(("seq", "fsdp"), None),
        P(None, ("seq", "fsdp")),
        P(("seq", "fsdp"), None),
        P(("seq", "fsdp"), None),
        P(("seq", "fsdp"), None),
        P(("seq", "fsdp"), None),
        P(None, ("seq", "fsdp")),
        P(("seq", "fsdp"), None),
        P(("seq", "fsdp"), None),
        P(("seq", "fsdp"), None),
        P(("seq", "fsdp"), None),
        P(None, ("seq", "fsdp")),
    )
    out_specs = (
        P("fsdp", "seq", None),
        P("fsdp", "seq", None),
        P(("seq", "fsdp"), None),
        P(("seq", "fsdp"), None),
        P(("seq", "fsdp"), None),
        P(("seq", "fsdp"), None),
        P(("seq", "fsdp"), None),
        P(("seq", "fsdp"), None),
        P(("seq", "fsdp"), None),
        P(("seq", "fsdp"), None),
        P(("seq", "fsdp"), None),
        P(("seq", "fsdp"), None),
        P(("seq", "fsdp"), None),
        P(("seq", "fsdp"), None),
        P(None, ("seq", "fsdp")),
        P(None, ("seq", "fsdp")),
        P(None, ("seq", "fsdp")),
    )
    return jax.shard_map(body, mesh=mesh, in_specs=in_specs, out_specs=out_specs, check_vma=False)
```

```python
import functools

import jax
import jax.numpy as jnp
from jax import lax
from jax.experimental import pallas as pl
from jax.experimental.pallas import tpu as pltpu
from jax.sharding import PartitionSpec as P

D = 2048
FF = 5632
HEADS = 32
KV_HEADS = 4
HEAD_DIM = 64
STEP = 10


epsilon = 1e-05
adam_epsilon = 1e-08
beta_first = 0.9
beta_second = 0.95
rope_base = 10000.0
weight_decay = 0.1
masked_value = -1e30


def rotate(field, position, sign):
    half = field.shape[-1] // 2
    exponent = jnp.arange(half).astype(jnp.float32) * (-2.0 / field.shape[-1])
    frequency = jnp.power(rope_base, exponent)
    angle = position[:, None] * frequency[None, :]
    cosine = jnp.cos(angle)[:, None, :]
    sine = sign * jnp.sin(angle)[:, None, :]
    first = field[..., :half]
    second = field[..., half:]
    return jnp.concatenate(
        [first * cosine - second * sine, second * cosine + first * sine], axis=-1
    )


def rms_scale(rows):
    return lax.rsqrt(jnp.mean(rows * rows, axis=-1, keepdims=True) + epsilon)


def norm_back(rows, scale_rows, gain, grad):
    weighted = grad * gain
    row_grad = scale_rows * weighted - rows * scale_rows**3 * jnp.mean(
        weighted * rows, axis=-1, keepdims=True
    )
    gain_grad = jnp.sum(grad * rows * scale_rows, axis=0)
    return (row_grad, gain_grad)


def dot(left, right):
    return jnp.dot(left, right, preferred_element_type=jnp.float32)


def outer(left, right):
    return lax.dot_general(
        left, right, (((0,), (0,)), ((), ())), preferred_element_type=jnp.float32
    )


def against(left, right):
    return lax.dot_general(
        left, right, (((1,), (1,)), ((), ())), preferred_element_type=jnp.float32
    )


def stack_heads(field, heads):
    return jnp.concatenate(
        [field[:, h * HEAD_DIM : (h + 1) * HEAD_DIM] for h in range(heads)], axis=0
    )


def unstack_heads(field, heads):
    rows = field.shape[0] // heads
    return jnp.concatenate([field[h * rows : (h + 1) * rows] for h in range(heads)], axis=1)


def masked_scores(keys, queries, block, first):
    scores = against(keys, queries)
    key_place = lax.broadcasted_iota(jnp.int32, scores.shape, 0)
    query_place = first + lax.rem(lax.broadcasted_iota(jnp.int32, scores.shape, 1), block)
    return jnp.where(key_place <= query_place, scores, masked_value)


def remote(source, target, send, arrive, axis, device):
    return pltpu.make_async_remote_copy(
        src_ref=source,
        dst_ref=target,
        send_sem=send,
        recv_sem=arrive,
        device_id={axis: device},
        device_id_type=pl.DeviceIdType.MESH,
    )


VMEM = pl.BlockSpec(memory_space=pltpu.VMEM)


def core_pair(index):
    return index // 2, lax.rem(index, 2)


def pass_rows_start(rows, send, come, near):
    s = lax.axis_index("seq")
    for d in [1] + near:
        rows_copy(rows, send, come, d, s, s ^ d).start()


def pass_rows_finish(rows, send, come, forward, passed, near):
    s = lax.axis_index("seq")
    for d in near:
        rows_copy(rows, send, come, d, s ^ d, s ^ d).wait_recv()
        rows_copy(rows, forward, passed, d, s ^ d, s ^ 1).start()
    rows_copy(rows, send, come, 1, s ^ 1, s ^ 1).wait()
    for d in near:
        rows_copy(rows, send, come, d, s, s ^ d).wait_send()
        rows_copy(rows, forward, passed, d, s ^ d, s ^ 1).wait_send()
        rows_copy(rows, forward, passed, d, s ^ 1 ^ d, s ^ 1).wait_recv()


def rows_copy(rows, send, come, d, owner, target):
    place, half = core_pair(owner)
    return remote(rows.at[place, half], rows.at[place, half], send.at[d], come.at[d], "seq", target)


def share_kernel(
    in_ref, gain_ref, gate_up_ref, down_ref, feed_gate_up, feed_down, in_rows,
    low_gate_up, low_down, send_feed, come_feed, send_in, come_in, pass_in, passed_in,
):
    group, slices = lax.axis_size("seq"), lax.axis_size("fsdp")
    s, f = lax.axis_index("seq"), lax.axis_index("fsdp")
    pair, core = core_pair(s)
    depth, inward_cols = in_ref.shape
    ff_cols = FF // slices
    near = list(range(2, group, 2))
    in_rows[pair, core, :, pl.ds(0, inward_cols)] = in_ref[...].astype(jnp.bfloat16)
    in_rows[pair, core, :, pl.ds(inward_cols, 128)] = gain_ref[...]
    meet_spread(near)
    pass_rows_start(in_rows, send_in, come_in, near)
    for t in range(slices):
        columns = pl.ds(t * ff_cols, ff_cols)
        low_gate_up[t, :, pl.ds(0, ff_cols)] = gate_up_ref[:, columns].astype(jnp.bfloat16)
        low_gate_up[t, :, pl.ds(ff_cols, ff_cols)] = gate_up_ref[
            :, pl.ds(FF + t * ff_cols, ff_cols)
        ].astype(jnp.bfloat16)
        low_down[t] = down_ref[:, columns].astype(jnp.bfloat16)

    feeds = ((low_gate_up, feed_gate_up), (low_down, feed_down))

    def feed_copy(k, d, owner, target):
        low, feed = feeds[k]
        return remote(
            low.at[target],
            feed.at[pl.ds(pl.multiple_of(owner * depth, depth), depth), :],
            send_feed.at[k, d], come_feed.at[k, d], "fsdp", target,
        )

    for d in range(1, slices):
        for k in range(2):
            feed_copy(k, d, f, f ^ d).start()
    mine = pl.ds(pl.multiple_of(f * depth, depth), depth)
    for low, feed in feeds:
        feed[mine, :] = low[f]
    pass_rows_finish(in_rows, send_in, come_in, pass_in, passed_in, near)
    for d in range(1, slices):
        for k in range(2):
            feed_copy(k, d, f ^ d, f ^ d).wait()


def share_weights(w_inward, gain_columns, w_gate_up, w_down, group, slices):
    depth = w_inward.shape[0]
    ff_cols = FF // slices
    width = w_inward.shape[1] + 128
    sems = [pltpu.SemaphoreType.DMA((2, slices))] * 2 + [pltpu.SemaphoreType.DMA((group,))] * 4
    return pl.pallas_call(
        share_kernel,
        in_specs=[VMEM] * 4,
        out_specs=[VMEM] * 3,
        out_shape=[
            jax.ShapeDtypeStruct((slices * depth, 2 * ff_cols), jnp.bfloat16),
            jax.ShapeDtypeStruct((slices * depth, ff_cols), jnp.bfloat16),
            jax.ShapeDtypeStruct((group // 2, 2, depth, width), jnp.bfloat16),
        ],
        scratch_shapes=[
            pltpu.VMEM((slices, depth, 2 * ff_cols), jnp.bfloat16),
            pltpu.VMEM((slices, depth, ff_cols), jnp.bfloat16),
        ]
        + sems,
        compiler_params=pltpu.CompilerParams(
            vmem_limit_bytes=48 << 20, collective_id=2, has_side_effects=True
        ),
    )(w_inward, gain_columns, w_gate_up, w_down)


def block_order():
    slices = lax.axis_size("fsdp")
    if slices != 4:
        return list(range(1, slices))
    core = lax.rem(lax.axis_index("seq"), 2)
    return [2 - core, 1 + core, 3]


def gather_blocks(source, place, send, come):
    f, slices = lax.axis_index("fsdp"), lax.axis_size("fsdp")
    order = block_order()
    square = slices == 4
    near = [1, 2] if square else order

    def direct(d, owner, holder):
        return remote(source, place(owner, holder), send.at[d], come.at[d], "fsdp", f ^ d)

    def relay(owner, holder):
        return remote(
            place(order[0], 0), place(owner, holder), send.at[3], come.at[3], "fsdp", f ^ order[1]
        )

    def start():
        for d in near:
            direct(d, 0, d).start()

    def take(turn):
        if square and turn == 2:
            relay(3, 0).wait_recv()
        else:
            direct(order[turn], order[turn], 0).wait_recv()
        if square and turn == 0:
            relay(order[0], order[1]).start()

    def finish():
        for d in near:
            direct(d, 0, d).wait_send()
        if square:
            relay(order[0], order[1]).wait_send()

    return order, start, take, finish


def spread_copies(rows, full, send, come, forward, passed):
    s, f = lax.axis_index("seq"), lax.axis_index("fsdp")
    core = lax.rem(s, 2)
    order, begin, take, sent = gather_blocks(
        rows.at[:, core], lambda owner, holder: full.at[:, core, f ^ owner], send, come
    )

    def second(d, half):
        block = full.at[:, half, f ^ d]
        return remote(block, block, forward.at[d], passed.at[d], "seq", s ^ 1)

    def local():
        full[:, :, f] = rows[...]

    def early():
        take(0)
        second(order[0], core).start()

    def finish():
        for turn, d in enumerate(order[1:]):
            take(turn + 1)
            second(d, core).start()
        sent()
        for d in range(1, lax.axis_size("fsdp")):
            second(d, core).wait_send()
            second(d, 1 - core).wait_recv()

    return begin, local, early, finish


def meet_spread(extra=()):
    barrier = pltpu.get_barrier_semaphore()
    s, f = lax.axis_index("seq"), lax.axis_index("fsdp")
    near = sorted({1, *extra})
    slices = lax.axis_size("fsdp")
    for d in near:
        pl.semaphore_signal(
            barrier, inc=1, device_id={"seq": s ^ d}, device_id_type=pl.DeviceIdType.MESH
        )
    for d in range(1, slices):
        pl.semaphore_signal(
            barrier, inc=1, device_id={"fsdp": f ^ d}, device_id_type=pl.DeviceIdType.MESH
        )
    pl.semaphore_wait(barrier, len(near) + slices - 1)


def spread_part(
    rows, out_ref, full, out_rows, send, come, forward, passed,
    send_out, come_out, pass_out, passed_out, follow,
):
    near = list(range(2, lax.axis_size("seq"), 2))
    pair, core = core_pair(lax.axis_index("seq"))
    start, local, early, finish = spread_copies(rows, full, send, come, forward, passed)
    start()
    out_rows[pair, core] = out_ref[...].astype(jnp.bfloat16)
    pass_rows_start(out_rows, send_out, come_out, near)
    local()
    early()
    pass_rows_finish(out_rows, send_out, come_out, pass_out, passed_out, near)
    follow()
    finish()


def projections(x_ref, cosine_ref, sine_ref, full, normed, query, kv, gains):
    depth = full.shape[0] * 2 * full.shape[2] * full.shape[3]
    width, kv_width = HEADS * HEAD_DIM, KV_HEADS * HEAD_DIM

    def weights(first, count):
        return full[:, :, :, :, pl.ds(first, count)].reshape(depth, count)

    def turn(field):
        parts = []
        for i in range(field.shape[1] // 128):
            part = field[:, i * 128 : (i + 1) * 128]
            lane = lax.rem(lax.broadcasted_iota(jnp.int32, part.shape, 1), HEAD_DIM)
            other = jnp.where(
                lane < HEAD_DIM // 2,
                pltpu.roll(part, 128 - HEAD_DIM // 2, 1),
                pltpu.roll(part, HEAD_DIM // 2, 1),
            )
            parts.append(part * cosine_ref[...] + other * sine_ref[...])
        return jnp.concatenate(parts, axis=1)

    def keys_and_values():
        gains[...] = weights(width + 2 * kv_width, 128).astype(jnp.float32).T[:2]
        x = x_ref[...].astype(jnp.float32)
        normed[...] = (x * rms_scale(x) * gains[0:1, :]).astype(jnp.bfloat16)
        mixed = dot(normed[...], weights(width, 2 * kv_width))
        keys, values = turn(mixed[:, :kv_width]), mixed[:, kv_width:]
        kv[...] = jnp.concatenate(
            [
                field[:, h * HEAD_DIM : (h + 1) * HEAD_DIM]
                for h in range(KV_HEADS)
                for field in (keys, values)
            ],
            axis=1,
        ).astype(jnp.bfloat16)

    def queries():
        def query_part(i, _):
            first = pl.multiple_of(i * 512, 512)
            query[:, pl.ds(first, 512)] = turn(dot(normed[...], weights(first, 512))).astype(
                jnp.bfloat16
            )
            return 0

        lax.fori_loop(0, width // 512, query_part, 0)

    return keys_and_values, queries


def forward_kernel(
    in_rows, out_ref, x_ref, cosine_ref, sine_ref, dy_ref,
    in_full, normed, query_ref, gains, kv_all, mixed_ref, logs, out_full, middle, normed_second, dy_all,
    kv_ref, out_rows, queries, largest, total, mixed,
    send_in, come_in, pass_in, passed_in, send_z, come_z, pass_z, passed_z,
    send_kv, come_kv, pass_kv, passed_kv, send_rows, come_rows, pass_rows, passed_rows,
    send_dy, come_dy, own_sem,
):
    group, s = lax.axis_size("seq"), lax.axis_index("seq")
    place, core = core_pair(s)
    local = query_ref.shape[0]
    per_head = HEADS // KV_HEADS
    width, pair = per_head * HEAD_DIM, 2 * HEAD_DIM
    near = list(range(2, group, 2))
    meet_spread(range(1, group))
    find_keys, find_queries = projections(
        x_ref, cosine_ref, sine_ref, in_full, normed, query_ref, kv_ref, gains
    )
    spread_start, spread_local, spread_early, spread_finish = spread_copies(
        out_rows, out_full, send_rows, come_rows, pass_rows, passed_rows
    )

    dy_order, dy_start, dy_take, dy_sent = gather_blocks(
        dy_ref, lambda owner, holder: dy_all.at[owner ^ holder], send_dy, come_dy
    )
    own_dy = pltpu.make_async_copy(dy_ref, dy_all.at[0], own_sem)
    own_dy.start()

    def links_early():
        spread_early()
        dy_start()

    def links_late():
        dy_take(0)

    def kv_copy(d, owner, target):
        chip, half = core_pair(owner)
        return remote(kv_ref, kv_all.at[chip, half], send_kv.at[d], come_kv.at[d], "seq", target)

    def hand_on(chip, half):
        block = kv_all.at[chip, half]
        return remote(block, block, pass_kv.at[chip, half], passed_kv.at[chip, half], "seq", s ^ 1)

    spread_part(
        in_rows, out_ref, in_full, out_rows, send_in, come_in, pass_in, passed_in,
        send_z, come_z, pass_z, passed_z, spread_start,
    )
    find_keys()
    kv_copy(1, s, s ^ 1).start()
    for d in near:

        @pl.when((s ^ d) > s)
        def _():
            kv_copy(d, s, s ^ d).start()

    spread_local()
    find_queries()
    kv_all[place, core] = kv_ref[...]
    for h in range(KV_HEADS):
        field = query_ref[:, pl.ds(h * width, width)]
        queries[h] = stack_heads(field, per_head) * jnp.bfloat16(HEAD_DIM**-0.5)
    links_early()

    def scores_of(h, chip, masked):
        kv = kv_all[chip, :, :, pl.ds(pl.multiple_of(h * pair, pair), pair)]
        kv = kv.reshape(2 * local, pair)
        keys, values = kv[:, :HEAD_DIM], kv[:, HEAD_DIM:]
        if masked:
            return masked_scores(keys, queries[h], local, core * local), values
        return against(keys, queries[h]), values

    def own_chip(h, _):
        scores, values = scores_of(h, place, True)
        new = jnp.max(scores, axis=0, keepdims=True)
        weights = jnp.exp(scores - new)
        largest[h] = new
        total[h] = jnp.sum(weights, axis=0, keepdims=True)
        mixed[h] = outer(values, weights.astype(jnp.bfloat16))
        return 0

    kv_copy(1, s ^ 1, s ^ 1).wait_recv()
    lax.fori_loop(0, KV_HEADS, own_chip, 0)

    @pl.when(place == 0)
    def _():
        links_late()

    def earlier_chip(turn, _):
        chip = place - 1 - turn

        @pl.when(turn == jnp.minimum(place - 1, 1))
        def _():
            links_late()

        owner = 2 * chip + core
        kv_copy(owner ^ s, owner, owner).wait_recv()
        hand_on(chip, core).start()
        hand_on(chip, 1 - core).wait_recv()

        def head(h, _):
            scores, values = scores_of(h, chip, False)
            new = jnp.maximum(largest[h], jnp.max(scores, axis=0, keepdims=True))
            fade = jnp.exp(largest[h] - new)
            weights = jnp.exp(scores - new)
            largest[h] = new
            total[h] = total[h] * fade + jnp.sum(weights, axis=0, keepdims=True)
            mixed[h] = mixed[h] * fade + outer(values, weights.astype(jnp.bfloat16))
            return 0

        lax.fori_loop(0, KV_HEADS, head, 0)
        return 0

    lax.fori_loop(0, place, earlier_chip, 0)

    for h in range(KV_HEADS):
        logs[h] = largest[h] + jnp.log(total[h])
        mixed_ref[:, pl.ds(h * width, width)] = unstack_heads(
            (mixed[h] / total[h]).T, per_head
        ).astype(mixed_ref.dtype)
    kv_copy(1, s, s ^ 1).wait_send()
    for d in near:

        @pl.when((s ^ d) > s)
        def _():
            kv_copy(d, s, s ^ d).wait_send()

    def handed(chip, _):
        hand_on(chip, core).wait_send()
        return 0

    lax.fori_loop(0, place, handed, 0)
    spread_finish()

    depth = out_full.shape[0] * 2 * out_full.shape[2] * out_full.shape[3]

    def middle_part(i, _):
        columns = pl.ds(pl.multiple_of(i * 512, 512), 512)
        weights = out_full[:, :, :, :, columns].reshape(depth, 512)
        middle[:, columns] = x_ref[:, columns].astype(jnp.float32) + dot(mixed_ref[...], weights)
        return 0

    lax.fori_loop(0, middle.shape[1] // 512, middle_part, 0)
    field = middle[...]
    normed_second[...] = (field * rms_scale(field) * gains[1:2, :]).astype(jnp.bfloat16)
    for turn in range(1, len(dy_order)):
        dy_take(turn)
    dy_sent()
    own_dy.wait()


def backward_kernel(
    grad_ref, query_ref, mixed_ref, logs, kv_all, branch_ref,
    cosine_ref, sine_ref, cosine_rows, sine_rows, out_parts,
    inward_grad, inward_slices, attended_all, branch_all, out_come, kv_grad,
    queries, grads, inner, query_sum, parts, part_come, final_come,
    send_part, come_part, send_final, come_final, send_slice, come_slice,
    send_mixed, come_mixed, send_out, come_out,
):
    group, s = lax.axis_size("seq"), lax.axis_index("seq")
    place, core = core_pair(s)
    local = query_ref.shape[0]
    per_head = HEADS // KV_HEADS
    width, pair = per_head * HEAD_DIM, 2 * HEAD_DIM
    scale = HEAD_DIM**-0.5
    slices, f = lax.axis_size("fsdp"), lax.axis_index("fsdp")
    share = branch_all.shape[2]
    meet_spread(range(1, group))

    def slice_copy(d, target):
        columns = pl.ds(pl.multiple_of(target * share, 128), share)
        return remote(
            branch_ref.at[:, columns], branch_all.at[d], send_slice.at[d], come_slice.at[d],
            "fsdp", target,
        )

    gathers = [
        gather_blocks(mixed_ref, lambda owner, holder: attended_all.at[owner ^ holder],
                      send_mixed, come_mixed),
    ]

    def out_copy(d):
        return remote(
            out_parts.at[d], out_come.at[d - 1], send_out.at[d], come_out.at[d], "fsdp", f ^ d
        )

    def gathers_early():
        for _, _, take, _ in gathers:
            take(0)
        for d in range(1, slices):
            out_copy(d).start()

    def part_copy(chip, half):
        return remote(
            parts.at[chip, half], part_come.at[chip], send_part.at[chip], come_part.at[chip],
            "seq", s ^ 1,
        )

    def final_copy(chip, sender):
        return remote(
            parts.at[chip, core], final_come.at[sender], send_final.at[chip], come_final.at[sender],
            "seq", 2 * chip + core,
        )

    for d in range(1, slices):
        slice_copy(d, f ^ d).start()
    for _, begin, _, _ in gathers:
        begin()
    attended_all[0] = mixed_ref[...]
    branch_all[0] = branch_ref[:, pl.ds(pl.multiple_of(f * share, 128), share)]
    for h in range(KV_HEADS):
        columns = pl.ds(h * width, width)
        queries[h] = stack_heads(query_ref[:, columns], per_head) * jnp.bfloat16(scale)
        grad = stack_heads(grad_ref[:, columns], per_head)
        grads[h] = grad
        product = grad.astype(jnp.float32) * stack_heads(mixed_ref[:, columns], per_head).astype(
            jnp.float32
        )
        inner[h] = jnp.sum(product.T, axis=0, keepdims=True)
    query_sum[...] = jnp.zeros_like(query_sum)

    def head_grads(h, chip, masked):
        columns = pl.ds(pl.multiple_of(h * pair, pair), pair)
        kv = kv_all[chip, :, :, columns].reshape(2 * local, pair)
        keys, values = kv[:, :HEAD_DIM], kv[:, HEAD_DIM:]
        if masked:
            scores = masked_scores(keys, queries[h], local, core * local)
        else:
            scores = against(keys, queries[h])
        shares = jnp.exp(scores - logs[h])
        share_grad = against(values, grads[h])
        score_grad = (shares * (share_grad - inner[h])).astype(jnp.bfloat16)
        value_grad = dot(shares.astype(jnp.bfloat16), grads[h])
        key_grad = dot(score_grad, queries[h])
        part = jnp.concatenate([key_grad, value_grad], axis=1).astype(jnp.bfloat16)
        parts[chip, :, :, columns] = part.reshape(2, local, pair)
        query_sum[h] += outer(keys, score_grad)
        return 0

    def finish_chip(chip):
        part_copy(chip, core).wait_recv()
        parts[chip, core] = (
            parts[chip, core].astype(jnp.float32) + part_come[chip].astype(jnp.float32)
        ).astype(jnp.bfloat16)
        final_copy(chip, place).start()

    def earlier_chip(chip, _):
        @pl.when(chip == place - 1)
        def _():
            gathers_early()

        lax.fori_loop(0, KV_HEADS, lambda h, c: head_grads(h, chip, False), 0)
        part_copy(chip, 1 - core).start()

        @pl.when(chip > 0)
        def _():
            finish_chip(chip - 1)

        return 0

    lax.fori_loop(0, place, earlier_chip, 0)
    lax.fori_loop(0, KV_HEADS, lambda h, c: head_grads(h, place, True), 0)

    @pl.when(core == 1)
    def _():
        part_copy(place, 0).start()

    @pl.when(place == 0)
    def _():
        gathers_early()

    @pl.when(place > 0)
    def _():
        finish_chip(place - 1)

    half = HEAD_DIM // 2
    for h in range(KV_HEADS):
        total = query_sum[h] * scale
        one, two = total[:half], total[half:]
        turned = jnp.concatenate(
            [
                one * cosine_ref[...] + two * sine_ref[...],
                two * cosine_ref[...] - one * sine_ref[...],
            ],
            axis=0,
        )
        inward_grad[:, pl.ds(h * width, width)] = unstack_heads(turned.T, per_head).astype(
            jnp.bfloat16
        )
    kv_grad[...] = parts[place, core].astype(jnp.float32)

    @pl.when(core == 0)
    def _():
        part_copy(place, 0).wait_recv()
        kv_grad[...] += part_come[place].astype(jnp.float32)

    def later_chip(chip, _):
        final_copy(place, chip).wait_recv()
        kv_grad[...] += final_come[chip].astype(jnp.float32)
        return 0

    lax.fori_loop(place + 1, group // 2, later_chip, 0)
    key_grads, value_grads = [], []
    for h in range(KV_HEADS):
        field = kv_grad[:, pl.ds(h * pair, pair)]
        one, two = field[:, :half], field[:, half:HEAD_DIM]
        key_grads.append(one * cosine_rows[...] + two * sine_rows[...])
        key_grads.append(two * cosine_rows[...] - one * sine_rows[...])
        value_grads.append(field[:, HEAD_DIM:])
    inward_grad[:, pl.ds(HEADS * HEAD_DIM, 2 * KV_HEADS * HEAD_DIM)] = jnp.concatenate(
        key_grads + value_grads, axis=1
    ).astype(jnp.bfloat16)
    rest = inward_grad.shape[1] - slices * inward_slices.shape[2]
    inward_grad[:, pl.ds(inward_grad.shape[1] - rest, rest)] = jnp.zeros((local, rest), jnp.bfloat16)
    part_cols = inward_slices.shape[2]
    for t in range(slices):
        inward_slices[t] = inward_grad[:, pl.ds(t * part_cols, part_cols)]

    def sent(chip, _):
        part_copy(chip, 1 - core).wait_send()
        final_copy(chip, place).wait_send()
        return 0

    lax.fori_loop(0, place, sent, 0)

    @pl.when(core == 1)
    def _():
        part_copy(place, 0).wait_send()

    for d in range(1, slices):
        out_copy(d).wait()
        slice_copy(d, f ^ d).wait()
    for order, _, take, finish in gathers:
        for turn in range(1, len(order)):
            take(turn)
        finish()


def attend_forward(rows, w_outward, x, cosine, sine, upstream, group, slices):
    local, width = x.shape
    pairs, two, depth, inward_width = rows.shape
    outward_width = w_outward.shape[1]
    kv_cols = 2 * KV_HEADS * HEAD_DIM
    columns = HEADS // KV_HEADS * local
    low = jax.ShapeDtypeStruct((local, width), jnp.bfloat16)
    tiles = KV_HEADS * group * columns * local
    four_slices = [pltpu.SemaphoreType.DMA((slices,))] * 4
    in_full, *results = pl.pallas_call(
        forward_kernel,
        in_specs=[VMEM] * 5 + [ANY],
        out_specs=[VMEM] * 10 + [ANY],
        out_shape=[
            jax.ShapeDtypeStruct((pairs, two, slices, depth, inward_width), jnp.bfloat16),
            low,
            low,
            jax.ShapeDtypeStruct((2, width), jnp.float32),
            jax.ShapeDtypeStruct((pairs, two, local, kv_cols), jnp.bfloat16),
            low,
            jax.ShapeDtypeStruct((KV_HEADS, 1, columns), jnp.float32),
            jax.ShapeDtypeStruct((pairs, two, slices, depth, outward_width), jnp.bfloat16),
            jax.ShapeDtypeStruct((local, width), jnp.float32),
            low,
            jax.ShapeDtypeStruct((slices, local, width), jnp.bfloat16),
        ],
        scratch_shapes=[
            pltpu.VMEM((local, kv_cols), jnp.bfloat16),
            pltpu.VMEM((pairs, two, depth, outward_width), jnp.bfloat16),
            pltpu.VMEM((KV_HEADS, columns, HEAD_DIM), jnp.bfloat16),
            pltpu.VMEM((KV_HEADS, 1, columns), jnp.float32),
            pltpu.VMEM((KV_HEADS, 1, columns), jnp.float32),
            pltpu.VMEM((KV_HEADS, HEAD_DIM, columns), jnp.float32),
        ]
        + four_slices
        + [pltpu.SemaphoreType.DMA((group,))] * 6
        + [pltpu.SemaphoreType.DMA((pairs, 2))] * 2
        + four_slices
        + [pltpu.SemaphoreType.DMA((slices,))] * 2
        + [pltpu.SemaphoreType.DMA],
        compiler_params=pltpu.CompilerParams(
            vmem_limit_bytes=60 << 20, collective_id=0, has_side_effects=True
        ),
        cost_estimate=pl.CostEstimate(
            flops=tiles * HEAD_DIM * 160, bytes_accessed=20 << 20, transcendentals=tiles
        ),
    )(
        rows, w_outward, x, jnp.tile(cosine, (1, 4)),
        jnp.tile(jnp.concatenate([-sine, sine], axis=1), (1, 2)), upstream,
    )
    return in_full.reshape(-1, inward_width), *results


def attend_backward(
    grads, query, mixed, logs, kv_all, branch, cosine, sine, out_parts, group, slices
):
    local, features = branch.shape
    per_head = HEADS // KV_HEADS
    columns = per_head * local
    kv_cols = kv_all.shape[3]
    inward_cols = features + kv_cols
    tiles = KV_HEADS * group * columns * local
    gathered = jax.ShapeDtypeStruct((slices, local, features), jnp.bfloat16)
    stacked = pltpu.VMEM((KV_HEADS, columns, HEAD_DIM), jnp.bfloat16)
    one_half = pltpu.VMEM((group // 2, local, kv_cols), jnp.bfloat16)
    return pl.pallas_call(
        backward_kernel,
        in_specs=[VMEM] * 10 + [ANY],
        out_specs=[VMEM] * 4 + [ANY],
        out_shape=[
            jax.ShapeDtypeStruct((local, inward_cols + 128), jnp.bfloat16),
            jax.ShapeDtypeStruct((slices, local, inward_cols // slices), jnp.bfloat16),
            gathered,
            jax.ShapeDtypeStruct((slices, local, features // slices), jnp.bfloat16),
            jax.ShapeDtypeStruct((slices - 1, local, features), jnp.bfloat16),
        ],
        scratch_shapes=[
            pltpu.VMEM((local, kv_cols), jnp.float32),
            stacked,
            stacked,
            pltpu.VMEM((KV_HEADS, 1, columns), jnp.float32),
            pltpu.VMEM((KV_HEADS, HEAD_DIM, columns), jnp.float32),
            pltpu.VMEM((group // 2, 2, local, kv_cols), jnp.bfloat16),
            one_half,
            one_half,
        ]
        + [pltpu.SemaphoreType.DMA((group // 2,))] * 4
        + [pltpu.SemaphoreType.DMA((slices,))] * 4
        + [pltpu.SemaphoreType.DMA((slices,))] * 2,
        compiler_params=pltpu.CompilerParams(
            vmem_limit_bytes=60 << 20, collective_id=1, has_side_effects=True
        ),
        cost_estimate=pl.CostEstimate(
            flops=tiles * HEAD_DIM * 80, bytes_accessed=20 << 20, transcendentals=tiles
        ),
    )(
        grads, query, mixed, logs, kv_all, branch,
        jnp.tile(cosine.T, (1, per_head)), jnp.tile(sine.T, (1, per_head)), cosine, sine,
        out_parts,
    )


def meet_slices():
    slices, f = lax.axis_size("fsdp"), lax.axis_index("fsdp")
    barrier = pltpu.get_barrier_semaphore()
    for d in range(1, slices):
        pl.semaphore_signal(
            barrier, inc=1, device_id={"fsdp": f ^ d}, device_id_type=pl.DeviceIdType.MESH
        )
    pl.semaphore_wait(barrier, slices - 1)


def row_copy(stage, target, sem, r):
    width = stage.shape[0]
    rows = pl.ds(pl.multiple_of(r * width, width), width)
    return pltpu.make_async_copy(stage, target.at[rows, :], sem)


def grad_rows(field, grads, target, stage, sems):
    width = stage.shape[1]
    steps = target.shape[0] // width

    def step(r, _):
        columns = pl.ds(pl.multiple_of(r * width, width), width)
        slot = lax.rem(r, 2)
        left = field[:, :, columns].reshape(grads[0].shape[0], width)

        @pl.when(r > 1)
        def _():
            row_copy(stage.at[slot], target, sems.at[slot], r - 2).wait()

        for k, grad in enumerate(grads):
            units = grad.shape[1]
            stage[slot, :, pl.ds(k * units, units)] = outer(left, grad[...]).astype(jnp.bfloat16)
        row_copy(stage.at[slot], target, sems.at[slot], r).start()
        return 0

    lax.fori_loop(0, steps, step, 0)
    for r in (steps - 2, steps - 1):
        row_copy(stage.at[r % 2], target, sems.at[r % 2], r).wait()


def feed_first_kernel(
    *refs, slices, strip
):
    (
        dy_ref, x_ref, gate_up_ref, normed_ref,
        x_all, gate_all, up_all, hidden, down_grad_out, normed_near,
        gate_sum, up_sum, grad_stage, dy_all, send_x, come_x, grad_sem, dy_sem,
        send_normed, come_normed, own_sem,
    ) = refs
    f = lax.axis_index("fsdp")
    local = x_ref.shape[0]
    for d in range(slices):
        pltpu.make_async_copy(dy_ref.at[d], dy_all.at[d], dy_sem.at[d]).start()
    meet_slices()

    order, begin, take, sent = gather_blocks(
        x_ref, lambda owner, holder: x_all.at[owner ^ holder], send_x, come_x
    )
    begin()
    x_all[0] = x_ref[...]

    def normed_copy(d):
        return remote(
            normed_ref, normed_near.at[d], send_normed.at[d], come_normed.at[d], "fsdp", f ^ d
        )

    near = (1, 2) if slices == 4 else range(1, slices)
    own_normed = pltpu.make_async_copy(normed_ref, normed_near.at[0], own_sem)
    own_normed.start()

    def token_block(turn, d):
        for i in range(slices - 1):

            @pl.when(turn == i + 1)
            def _():
                take(i)
                if i == slices - 2:
                    for k in near:
                        normed_copy(k).start()

        x = x_all[d]
        units = hidden.shape[1]
        gate_sum[...] = dot(x, gate_up_ref[:, pl.ds(0, units)])
        up_sum[...] = dot(x, gate_up_ref[:, pl.ds(units, units)])

        def part(i, _):
            rows = pl.ds(pl.multiple_of(i * strip, strip), strip)
            place = pl.ds(pl.multiple_of(d * local + i * strip, strip), strip)
            gate, up = gate_sum[rows, :], up_sum[rows, :]
            hidden[place, :] = (gate / (1.0 + jnp.exp(-gate)) * up).astype(jnp.bfloat16)
            gate_all[place, :] = gate.astype(jnp.bfloat16)
            up_all[place, :] = up.astype(jnp.bfloat16)
            return 0

        lax.fori_loop(0, local // strip, part, 0)
        following = 0
        for i in reversed(range(slices - 1)):
            following = jnp.where(turn == i, order[i], following)
        return following

    lax.fori_loop(0, slices, token_block, jnp.int32(0))
    for d in range(slices):
        pltpu.make_async_copy(dy_ref.at[d], dy_all.at[d], dy_sem.at[d]).wait()
    grad_rows(dy_all, [hidden], down_grad_out, grad_stage, grad_sem)
    sent()
    own_normed.wait()
    for d in near:
        normed_copy(d).wait()


def feed_second_kernel(
    *refs, slices, strip
):
    (
        dy_ref, x_ref, gate_all, up_all, hidden, gate_up_ref, down_ref, normed_near,
        back_ref, out_parts, gate_up_grad_out, normed_far,
        dy_all,
        gate_grad, up_grad, hidden_sum, back_send, back_come, out_stage, grad_stage,
        send_back, come_back, out_sem, grad_sem, dy_sem,
        send_normed, come_normed,
    ) = refs
    f = lax.axis_index("fsdp")
    local = back_ref.shape[0]

    def dy_copy(d):
        return pltpu.make_async_copy(dy_ref.at[d], dy_all.at[d], dy_sem.at[d])

    for d in range(slices):
        dy_copy(d).start()
    meet_slices()
    square = slices == 4
    order = block_order()
    first, second = (order[1], order[0]) if square else (None, None)
    turns = [3, second, first, 0] if square else list(range(slices - 1, -1, -1))

    def relay():
        return remote(
            normed_near.at[order[0]], normed_far, send_normed, come_normed, "fsdp", f ^ order[1]
        )

    if square:
        relay().start()
    for d in range(slices):
        dy_copy(d).wait()

    def back_copy(d, target, landing):
        return remote(
            back_send.at[d], back_come.at[landing - 1], send_back.at[d], come_back.at[landing],
            "fsdp", f ^ target,
        )

    def out_copy(slot, d):
        return pltpu.make_async_copy(out_stage.at[slot], out_parts.at[d], out_sem.at[slot])

    def token_block(turn, carry):
        d, before = carry
        place = pl.ds(pl.multiple_of(d * local, local), local)
        hidden_sum[...] = dot(dy_all[d], down_ref[...])

        def part(i, _):
            rows = pl.ds(pl.multiple_of(i * strip, strip), strip)
            here = pl.ds(pl.multiple_of(d * local + i * strip, strip), strip)
            gate = gate_all[here, :].astype(jnp.float32)
            up = up_all[here, :].astype(jnp.float32)
            sigmoid = 1.0 / (1.0 + jnp.exp(-gate))
            grad = hidden_sum[rows, :]
            gate_grad[here, :] = (
                grad * up * sigmoid * (1.0 + gate * (1.0 - sigmoid))
            ).astype(jnp.bfloat16)
            up_grad[here, :] = (grad * gate * sigmoid).astype(jnp.bfloat16)
            return 0

        lax.fori_loop(0, local // strip, part, 0)
        units = hidden.shape[1]
        back = against(gate_grad[place, :], gate_up_ref[:, pl.ds(0, units)])
        back = back + against(up_grad[place, :], gate_up_ref[:, pl.ds(units, units)])
        back_send[d] = back.astype(jnp.bfloat16)
        if square:

            @pl.when(turn == 0)
            def _():
                back_copy(3, first, 3).start()

            @pl.when(turn == 2)
            def _():
                back_copy(3, first, 3).wait_recv()
                back_send[second] = (
                    back_send[second].astype(jnp.float32) + back_come[2].astype(jnp.float32)
                ).astype(jnp.bfloat16)
                back_copy(second, second, second).start()
                back_copy(first, first, first).start()

        else:

            @pl.when(d > 0)
            def _():
                back_copy(d, d, d).start()

        @pl.when(turn > 1)
        def _():
            out_copy(lax.rem(turn, 2), before).wait()

        out_stage[lax.rem(turn, 2)] = against(hidden[place, :], down_ref[...]).astype(jnp.bfloat16)
        out_copy(lax.rem(turn, 2), d).start()
        following = 0
        for i in reversed(range(slices - 1)):
            following = jnp.where(turn == i, turns[i + 1], following)
        return following, d

    lax.fori_loop(0, slices, token_block, (jnp.int32(turns[0]), jnp.int32(0)))
    out_copy(0, 0).wait()
    out_copy(1, 0).wait()
    grad_rows(x_ref, [gate_grad, up_grad], gate_up_grad_out, grad_stage, grad_sem)
    if square:
        relay().wait()
        back_copy(3, first, 3).wait_send()
    for d in (1, 2) if square else range(1, slices):
        back_copy(d, d, d).wait()
    home = [back_send[0]] + [back_come[d - 1] for d in ((1, 2) if square else range(1, slices))]
    back_ref[...] = functools.reduce(jnp.add, [p.astype(jnp.float32) for p in home])


ANY = pl.BlockSpec(memory_space=pl.ANY)


def feed_first(x, upstream_all, gate_up_slice, normed):
    slices, local, width = upstream_all.shape
    ff_cols = gate_up_slice.shape[1] // 2
    tokens = slices * local
    units = jax.ShapeDtypeStruct((tokens, ff_cols), jnp.bfloat16)
    high = pltpu.VMEM((local, ff_cols), jnp.float32)
    sems = pltpu.SemaphoreType.DMA((slices,))
    return pl.pallas_call(
        functools.partial(feed_first_kernel, slices=slices, strip=32),
        in_specs=[ANY] + [VMEM] * 3,
        out_specs=[VMEM] * 4 + [ANY] * 2,
        out_shape=[
            jax.ShapeDtypeStruct((slices, local, width), jnp.bfloat16),
            units,
            units,
            units,
            jax.ShapeDtypeStruct((width, ff_cols), jnp.bfloat16),
            jax.ShapeDtypeStruct((slices, local, width), jnp.bfloat16),
        ],
        scratch_shapes=[
            high,
            high,
            pltpu.VMEM((2, 256, ff_cols), jnp.bfloat16),
            pltpu.VMEM((slices, local, width), jnp.bfloat16),
            sems,
            sems,
            pltpu.SemaphoreType.DMA((2,)),
            sems,
            sems,
            sems,
            pltpu.SemaphoreType.DMA,
        ],
        compiler_params=pltpu.CompilerParams(
            vmem_limit_bytes=60 << 20, collective_id=4, has_side_effects=True
        ),
        cost_estimate=pl.CostEstimate(
            flops=10 * tokens * width * ff_cols, bytes_accessed=30 << 20, transcendentals=0
        ),
    )(upstream_all, x, gate_up_slice, normed)


def feed_second(
    x_all, upstream_all, gate_all, up_all, hidden, gate_up_slice, down_slice, normed_near
):
    slices, local, width = x_all.shape
    ff_cols = gate_up_slice.shape[1] // 2
    tokens = slices * local
    blocks = pltpu.VMEM((slices, local, width), jnp.bfloat16)
    low = pltpu.VMEM((tokens, ff_cols), jnp.bfloat16)
    sems = pltpu.SemaphoreType.DMA((slices,))
    pair = pltpu.SemaphoreType.DMA((2,))
    return pl.pallas_call(
        functools.partial(feed_second_kernel, slices=slices, strip=32),
        in_specs=[ANY] + [VMEM] * 6 + [ANY],
        out_specs=[VMEM] + [ANY] * 3,
        out_shape=[
            jax.ShapeDtypeStruct((local, width), jnp.float32),
            jax.ShapeDtypeStruct((slices, local, width), jnp.bfloat16),
            jax.ShapeDtypeStruct((width, 2 * ff_cols), jnp.bfloat16),
            jax.ShapeDtypeStruct((local, width), jnp.bfloat16),
        ],
        scratch_shapes=[
            blocks,
            low,
            low,
            pltpu.VMEM((local, ff_cols), jnp.float32),
            blocks,
            pltpu.VMEM((slices - 1, local, width), jnp.bfloat16),
            pltpu.VMEM((2, local, width), jnp.bfloat16),
            pltpu.VMEM((2, 256, 2 * ff_cols), jnp.bfloat16),
            sems,
            sems,
            pair,
            pair,
            sems,
            pltpu.SemaphoreType.DMA,
            pltpu.SemaphoreType.DMA,
        ],
        compiler_params=pltpu.CompilerParams(
            vmem_limit_bytes=62 << 20, collective_id=5, has_side_effects=True
        ),
        cost_estimate=pl.CostEstimate(
            flops=20 * tokens * width * ff_cols, bytes_accessed=40 << 20, transcendentals=0
        ),
    )(
        upstream_all, x_all, gate_all, up_all, hidden, gate_up_slice, down_slice,
        normed_near,
    )


def home_kernel(*refs, count, moves, summed):
    slices, f = lax.axis_size("fsdp"), lax.axis_index("fsdp")
    sources, rest = refs[:count], refs[count:]
    results, rest = rest[: -(count + 2)], rest[-(count + 2) :]
    landed, (send, come) = rest[:count], rest[count:]
    depth = sources[0].shape[0] // slices
    meet_slices()

    def copy(k, d):
        rows = pl.ds(pl.multiple_of((f ^ d) * depth, depth), depth)
        return remote(
            sources[k].at[rows, :], landed[k].at[d], send.at[k, d], come.at[k, d], "fsdp", f ^ d
        )

    for k in range(count):
        for d in range(1, slices):
            copy(k, d).start()
    for k in range(count):
        landed[k][0] = sources[k][pl.ds(pl.multiple_of(f * depth, depth), depth), :]
    for k in range(count):
        for d in range(1, slices):
            copy(k, d).wait()
    for t in range(slices):
        for source, first, width, result, base in moves:
            results[result][:, pl.ds(base + t * width, width)] = landed[source][
                f ^ t, :, pl.ds(first, width)
            ]
    if summed:
        source, first = summed
        results[-1][...] = functools.reduce(
            jnp.add,
            [landed[source][d, :, pl.ds(first, 128)].astype(jnp.float32) for d in range(slices)],
        )


def bring_home(sources, moves, widths, summed, slices, number):
    depth = sources[0].shape[0] // slices
    shapes = [jax.ShapeDtypeStruct((depth, width), jnp.bfloat16) for width in widths]
    if summed:
        shapes.append(jax.ShapeDtypeStruct((depth, 128), jnp.float32))
    return pl.pallas_call(
        functools.partial(home_kernel, count=len(sources), moves=moves, summed=summed),
        in_specs=[VMEM] * len(sources),
        out_specs=[VMEM] * len(shapes),
        out_shape=shapes,
        scratch_shapes=[pltpu.VMEM((slices, depth, s.shape[1]), jnp.bfloat16) for s in sources]
        + [pltpu.SemaphoreType.DMA((len(sources), slices))] * 2,
        compiler_params=pltpu.CompilerParams(
            vmem_limit_bytes=32 << 20, collective_id=number, has_side_effects=True
        ),
        cost_estimate=pl.CostEstimate(flops=10 << 30, bytes_accessed=4 << 20, transcendentals=0),
    )(*sources)


def swap(piece, axis, offset):
    size = lax.axis_size(axis)
    return lax.ppermute(piece, axis, [(i, i ^ offset) for i in range(size)])


def gather_swap(piece, axis):
    return [piece] + [swap(piece, axis, d) for d in range(1, lax.axis_size(axis))]


def exchange_swap(stack, axis):
    me = lax.axis_index(axis)
    pieces = [
        lax.dynamic_index_in_dim(stack, me ^ d, 0, keepdims=False)
        for d in range(lax.axis_size(axis))
    ]
    return [pieces[0]] + [swap(p, axis, d) for d, p in enumerate(pieces) if d]


def reduce_swap(parts, axis):
    total = parts[0].astype(jnp.float32)
    for d in range(1, len(parts)):
        total = total + swap(parts[d], axis, d).astype(jnp.float32)
    return total


def scatter_rows(partial, after=()):
    partial, *_ = lax.optimization_barrier((partial, *after))
    return lax.psum_scatter(partial, "seq", scatter_dimension=0, tiled=True)


def adam_update(weight, first, second, grad, rate, decay):
    first_new = beta_first * first + (1.0 - beta_first) * grad
    second_new = beta_second * second + (1.0 - beta_second) * grad * grad
    first_hat = first_new / (1.0 - beta_first**STEP)
    second_hat = second_new / (1.0 - beta_second**STEP)
    weight_new = weight - rate * (
        first_hat / (jnp.sqrt(second_hat) + adam_epsilon) + decay * weight
    )
    return (first_new, second_new, weight_new)


def body(
    inputs,
    cotangent,
    w_inward,
    w_outward,
    w_gate_up,
    w_down,
    gains,
    first_inward,
    first_outward,
    first_gate_up,
    first_down,
    first_gains,
    second_inward,
    second_outward,
    second_gate_up,
    second_down,
    second_gains,
):
    rows = inputs[0].astype(jnp.float32)
    upstream = cotangent[0]
    local = rows.shape[0]
    group = lax.axis_size("seq")
    slices = lax.axis_size("fsdp")
    kv_width = KV_HEADS * HEAD_DIM
    inward_cols = D + 2 * kv_width
    ff_cols = FF // slices
    depth = w_inward.shape[0]
    position = (lax.axis_index("seq") * local + jnp.arange(local)).astype(jnp.float32)

    low_gains = jnp.pad(jnp.transpose(gains.astype(jnp.bfloat16)), ((0, 0), (0, 126)))
    feed_gate_up, feed_down, in_rows = share_weights(
        w_inward, low_gains, w_gate_up, w_down, group, slices
    )
    gate_up_slice = lax.all_gather(feed_gate_up, "seq", axis=0, tiled=True)
    exponent = jnp.arange(HEAD_DIM // 2).astype(jnp.float32) * (-2.0 / HEAD_DIM)
    angle = position[:, None] * jnp.power(rope_base, exponent)[None, :]
    cosine, sine = jnp.cos(angle), jnp.sin(angle)
    (
        inward_gains, normed, query, gains_full, kv_all, attended, logs, outward_full,
        middle, normed_second, upstream_all,
    ) = attend_forward(in_rows, w_outward, inputs[0], cosine, sine, upstream, group, slices)
    gain_first, gain_second = gains_full[0], gains_full[1]
    scale_first = rms_scale(rows)
    scale_second = rms_scale(middle)
    down_slice = lax.all_gather(feed_down, "seq", axis=0, tiled=True)
    outward_full = outward_full.reshape(D, D)
    normed_all, gate_all, up_all, hidden, down_partial, normed_near = feed_first(
        normed_second, upstream_all, gate_up_slice, normed
    )
    normed_second_grad, out_parts, gate_up_partial, normed_far = feed_second(
        normed_all, upstream_all, gate_all, up_all, hidden, gate_up_slice, down_slice,
        normed_near,
    )
    down_mine = scatter_rows(down_partial)
    gate_up_mine = scatter_rows(gate_up_partial)
    middle_back, gain_second_grad = norm_back(middle, scale_second, gain_second, normed_second_grad)
    middle_grad = upstream.astype(jnp.float32) + middle_back
    branch_low = middle_grad.astype(jnp.bfloat16)
    attended_grad = against(branch_low, outward_full).astype(jnp.bfloat16)
    inward_grad, inward_slices, attended_all, branch_all, out_come = attend_backward(
        attended_grad, query, attended, logs, kv_all, branch_low,
        cosine, sine, out_parts, group, slices,
    )
    inward_grad, inward_slices, attended_all, branch_all, down_mine, normed_far = (
        lax.optimization_barrier(
            (inward_grad, inward_slices, attended_all, branch_all, down_mine, normed_far)
        )
    )
    inward_grad_blocks = exchange_swap(inward_slices, "fsdp")
    outward_partial = outer(attended_all.reshape(-1, D), branch_all.reshape(-1, D // slices))
    outward_partial = outward_partial.astype(jnp.bfloat16)
    normed_grad = against(inward_grad, inward_gains)
    rows_back, gain_first_grad = norm_back(rows, scale_first, gain_first, normed_grad)
    input_grad = middle_grad + rows_back

    inward_grad_blocks, gain_first_grad = lax.optimization_barrier(
        (inward_grad_blocks, gain_first_grad)
    )
    gain_grads = jnp.stack([gain_first_grad, gain_second_grad], axis=1)
    gain_grads = jnp.pad(gain_grads.astype(jnp.bfloat16), ((0, 0), (0, 126)))
    if slices == 4:
        inward_partial = outer(
            normed_near[:3].reshape(-1, D), jnp.concatenate(inward_grad_blocks[:3], axis=0)
        ) + outer(normed_far, inward_grad_blocks[3])
    else:
        inward_partial = outer(
            normed_near.reshape(-1, D), jnp.concatenate(inward_grad_blocks, axis=0)
        )
    inward_partial = inward_partial.astype(jnp.bfloat16)
    slice_cols = inward_partial.shape[1]
    inward_partial, gate_up_mine = lax.optimization_barrier(
        (
            jnp.concatenate([inward_partial, gain_grads, outward_partial], axis=1),
            gate_up_mine,
        )
    )
    inward_mine = scatter_rows(inward_partial)
    result = middle + functools.reduce(
        jnp.add,
        [p.astype(jnp.float32) for p in [out_parts[0]] + [out_come[d] for d in range(slices - 1)]],
    )
    gate_up_sum, down_sum = bring_home(
        [gate_up_mine, down_mine],
        [(0, 0, ff_cols, 0, 0), (0, ff_cols, ff_cols, 0, FF), (1, 0, ff_cols, 1, 0)],
        [2 * FF, FF], None, slices, 6,
    )
    inward_sum, outward_sum, gains_sum = bring_home(
        [inward_mine],
        [(0, 0, slice_cols, 0, 0), (0, slice_cols + 128, D // slices, 1, 0)],
        [inward_cols, D], (0, slice_cols), slices, 7,
    )
    gate_up_sum, down_sum, inward_sum, outward_sum = [
        field.astype(jnp.float32) for field in (gate_up_sum, down_sum, inward_sum, outward_sum)
    ]
    gains_sum = jnp.transpose(gains_sum[:, :2])
    first_inward_new, second_inward_new, inward_new = adam_update(
        w_inward, first_inward, second_inward, inward_sum, 0.02, weight_decay
    )
    first_outward_new, second_outward_new, outward_new = adam_update(
        w_outward, first_outward, second_outward, outward_sum, 0.15, weight_decay
    )
    first_gate_up_new, second_gate_up_new, gate_up_new = adam_update(
        w_gate_up, first_gate_up, second_gate_up, gate_up_sum, 0.02, weight_decay
    )
    first_down_new, second_down_new, down_new = adam_update(
        w_down, first_down, second_down, down_sum, 0.015, weight_decay
    )
    first_gains_new, second_gains_new, gains_new = adam_update(
        gains, first_gains, second_gains, gains_sum, 0.6, 0.0
    )
    return (
        result[None].astype(jnp.bfloat16),
        input_grad[None],
        first_inward_new,
        second_inward_new,
        inward_new,
        first_outward_new,
        second_outward_new,
        outward_new,
        first_gate_up_new,
        second_gate_up_new,
        gate_up_new,
        first_down_new,
        second_down_new,
        down_new,
        first_gains_new,
        second_gains_new,
        gains_new,
    )


def solution(mesh):
    in_specs = (
        P("fsdp", "seq", None),
        P("fsdp", "seq", None),
        P(("seq", "fsdp"), None),
        P(("seq", "fsdp"), None),
        P(("seq", "fsdp"), None),
        P(("seq", "fsdp"), None),
        P(None, ("seq", "fsdp")),
        P(("seq", "fsdp"), None),
        P(("seq", "fsdp"), None),
        P(("seq", "fsdp"), None),
        P(("seq", "fsdp"), None),
        P(None, ("seq", "fsdp")),
        P(("seq", "fsdp"), None),
        P(("seq", "fsdp"), None),
        P(("seq", "fsdp"), None),
        P(("seq", "fsdp"), None),
        P(None, ("seq", "fsdp")),
    )
    out_specs = (
        P("fsdp", "seq", None),
        P("fsdp", "seq", None),
        P(("seq", "fsdp"), None),
        P(("seq", "fsdp"), None),
        P(("seq", "fsdp"), None),
        P(("seq", "fsdp"), None),
        P(("seq", "fsdp"), None),
        P(("seq", "fsdp"), None),
        P(("seq", "fsdp"), None),
        P(("seq", "fsdp"), None),
        P(("seq", "fsdp"), None),
        P(("seq", "fsdp"), None),
        P(("seq", "fsdp"), None),
        P(("seq", "fsdp"), None),
        P(None, ("seq", "fsdp")),
        P(None, ("seq", "fsdp")),
        P(None, ("seq", "fsdp")),
    )
    return jax.shard_map(body, mesh=mesh, in_specs=in_specs, out_specs=out_specs, check_vma=False)
```

```python
import functools

import jax
import jax.numpy as jnp
from jax import lax
from jax.experimental import pallas as pl
from jax.experimental.pallas import tpu as pltpu
from jax.sharding import PartitionSpec as P

D = 2048
FF = 5632
HEADS = 32
KV_HEADS = 4
HEAD_DIM = 64
STEP = 10


epsilon = 1e-05
adam_epsilon = 1e-08
beta_first = 0.9
beta_second = 0.95
rope_base = 10000.0
weight_decay = 0.1
masked_value = -1e30


def rotate(field, position, sign):
    half = field.shape[-1] // 2
    exponent = jnp.arange(half).astype(jnp.float32) * (-2.0 / field.shape[-1])
    frequency = jnp.power(rope_base, exponent)
    angle = position[:, None] * frequency[None, :]
    cosine = jnp.cos(angle)[:, None, :]
    sine = sign * jnp.sin(angle)[:, None, :]
    first = field[..., :half]
    second = field[..., half:]
    return jnp.concatenate(
        [first * cosine - second * sine, second * cosine + first * sine], axis=-1
    )


def rms_scale(rows):
    return lax.rsqrt(jnp.mean(rows * rows, axis=-1, keepdims=True) + epsilon)


def norm_back(rows, scale_rows, gain, grad):
    weighted = grad * gain
    row_grad = scale_rows * weighted - rows * scale_rows**3 * jnp.mean(
        weighted * rows, axis=-1, keepdims=True
    )
    gain_grad = jnp.sum(grad * rows * scale_rows, axis=0)
    return (row_grad, gain_grad)


def dot(left, right):
    return jnp.dot(left, right, preferred_element_type=jnp.float32)


def outer(left, right):
    return lax.dot_general(
        left, right, (((0,), (0,)), ((), ())), preferred_element_type=jnp.float32
    )


def against(left, right):
    return lax.dot_general(
        left, right, (((1,), (1,)), ((), ())), preferred_element_type=jnp.float32
    )


def stack_heads(field, heads):
    return jnp.concatenate(
        [field[:, h * HEAD_DIM : (h + 1) * HEAD_DIM] for h in range(heads)], axis=0
    )


def unstack_heads(field, heads):
    rows = field.shape[0] // heads
    return jnp.concatenate([field[h * rows : (h + 1) * rows] for h in range(heads)], axis=1)


def masked_scores(keys, queries, block, first):
    scores = against(keys, queries)
    key_place = lax.broadcasted_iota(jnp.int32, scores.shape, 0)
    query_place = first + lax.rem(lax.broadcasted_iota(jnp.int32, scores.shape, 1), block)
    return jnp.where(key_place <= query_place, scores, masked_value)


def remote(source, target, send, arrive, axis, device):
    return pltpu.make_async_remote_copy(
        src_ref=source,
        dst_ref=target,
        send_sem=send,
        recv_sem=arrive,
        device_id={axis: device},
        device_id_type=pl.DeviceIdType.MESH,
    )


VMEM = pl.BlockSpec(memory_space=pltpu.VMEM)


def core_pair(index):
    return index // 2, lax.rem(index, 2)


def pass_rows_start(rows, send, come, near):
    s = lax.axis_index("seq")
    for d in [1] + near:
        rows_copy(rows, send, come, d, s, s ^ d).start()


def pass_rows_finish(rows, send, come, forward, passed, near):
    s = lax.axis_index("seq")
    for d in near:
        rows_copy(rows, send, come, d, s ^ d, s ^ d).wait_recv()
        rows_copy(rows, forward, passed, d, s ^ d, s ^ 1).start()
    rows_copy(rows, send, come, 1, s ^ 1, s ^ 1).wait()
    for d in near:
        rows_copy(rows, send, come, d, s, s ^ d).wait_send()
        rows_copy(rows, forward, passed, d, s ^ d, s ^ 1).wait_send()
        rows_copy(rows, forward, passed, d, s ^ 1 ^ d, s ^ 1).wait_recv()


def rows_copy(rows, send, come, d, owner, target):
    place, half = core_pair(owner)
    return remote(rows.at[place, half], rows.at[place, half], send.at[d], come.at[d], "seq", target)


def share_kernel(
    in_ref, gain_ref, gate_up_ref, down_ref, feed_gate_up, feed_down, in_rows,
    low_gate_up, low_down, send_feed, come_feed, send_in, come_in, pass_in, passed_in,
):
    group, slices = lax.axis_size("seq"), lax.axis_size("fsdp")
    s, f = lax.axis_index("seq"), lax.axis_index("fsdp")
    pair, core = core_pair(s)
    depth, inward_cols = in_ref.shape
    ff_cols = FF // slices
    near = list(range(2, group, 2))
    in_rows[pair, core, :, pl.ds(0, inward_cols)] = in_ref[...].astype(jnp.bfloat16)
    in_rows[pair, core, :, pl.ds(inward_cols, 128)] = gain_ref[...]
    meet_spread(near)
    pass_rows_start(in_rows, send_in, come_in, near)
    for t in range(slices):
        columns = pl.ds(t * ff_cols, ff_cols)
        low_gate_up[t, :, pl.ds(0, ff_cols)] = gate_up_ref[:, columns].astype(jnp.bfloat16)
        low_gate_up[t, :, pl.ds(ff_cols, ff_cols)] = gate_up_ref[
            :, pl.ds(FF + t * ff_cols, ff_cols)
        ].astype(jnp.bfloat16)
        low_down[t] = down_ref[:, columns].astype(jnp.bfloat16)

    feeds = ((low_gate_up, feed_gate_up), (low_down, feed_down))

    def feed_copy(k, d, owner, target):
        low, feed = feeds[k]
        return remote(
            low.at[target],
            feed.at[pl.ds(pl.multiple_of(owner * depth, depth), depth), :],
            send_feed.at[k, d], come_feed.at[k, d], "fsdp", target,
        )

    for d in range(1, slices):
        for k in range(2):
            feed_copy(k, d, f, f ^ d).start()
    mine = pl.ds(pl.multiple_of(f * depth, depth), depth)
    for low, feed in feeds:
        feed[mine, :] = low[f]
    pass_rows_finish(in_rows, send_in, come_in, pass_in, passed_in, near)
    for d in range(1, slices):
        for k in range(2):
            feed_copy(k, d, f ^ d, f ^ d).wait()


def share_weights(w_inward, gain_columns, w_gate_up, w_down, group, slices):
    depth = w_inward.shape[0]
    ff_cols = FF // slices
    width = w_inward.shape[1] + 128
    sems = [pltpu.SemaphoreType.DMA((2, slices))] * 2 + [pltpu.SemaphoreType.DMA((group,))] * 4
    return pl.pallas_call(
        share_kernel,
        in_specs=[VMEM] * 4,
        out_specs=[VMEM] * 3,
        out_shape=[
            jax.ShapeDtypeStruct((slices * depth, 2 * ff_cols), jnp.bfloat16),
            jax.ShapeDtypeStruct((slices * depth, ff_cols), jnp.bfloat16),
            jax.ShapeDtypeStruct((group // 2, 2, depth, width), jnp.bfloat16),
        ],
        scratch_shapes=[
            pltpu.VMEM((slices, depth, 2 * ff_cols), jnp.bfloat16),
            pltpu.VMEM((slices, depth, ff_cols), jnp.bfloat16),
        ]
        + sems,
        compiler_params=pltpu.CompilerParams(
            vmem_limit_bytes=48 << 20, collective_id=2, has_side_effects=True
        ),
    )(w_inward, gain_columns, w_gate_up, w_down)


def block_order():
    slices = lax.axis_size("fsdp")
    if slices != 4:
        return list(range(1, slices))
    core = lax.rem(lax.axis_index("seq"), 2)
    return [2 - core, 1 + core, 3]


def gather_blocks(source, place, send, come):
    f, slices = lax.axis_index("fsdp"), lax.axis_size("fsdp")
    order = block_order()
    square = slices == 4
    near = [1, 2] if square else order

    def direct(d, owner, holder):
        return remote(source, place(owner, holder), send.at[d], come.at[d], "fsdp", f ^ d)

    def relay(owner, holder):
        return remote(
            place(order[0], 0), place(owner, holder), send.at[3], come.at[3], "fsdp", f ^ order[1]
        )

    def start():
        for d in near:
            direct(d, 0, d).start()

    def take(turn):
        if square and turn == 2:
            relay(3, 0).wait_recv()
        else:
            direct(order[turn], order[turn], 0).wait_recv()
        if square and turn == 0:
            relay(order[0], order[1]).start()

    def finish():
        for d in near:
            direct(d, 0, d).wait_send()
        if square:
            relay(order[0], order[1]).wait_send()

    return order, start, take, finish


def spread_copies(rows, full, send, come, forward, passed):
    s, f = lax.axis_index("seq"), lax.axis_index("fsdp")
    core = lax.rem(s, 2)
    order, begin, take, sent = gather_blocks(
        rows.at[:, core], lambda owner, holder: full.at[:, core, f ^ owner], send, come
    )

    def second(d, half):
        block = full.at[:, half, f ^ d]
        return remote(block, block, forward.at[d], passed.at[d], "seq", s ^ 1)

    def local():
        full[:, :, f] = rows[...]

    def early():
        take(0)
        second(order[0], core).start()

    def finish():
        for turn, d in enumerate(order[1:]):
            take(turn + 1)
            second(d, core).start()
        sent()
        for d in range(1, lax.axis_size("fsdp")):
            second(d, core).wait_send()
            second(d, 1 - core).wait_recv()

    return begin, local, early, finish


def meet_spread(extra=()):
    barrier = pltpu.get_barrier_semaphore()
    s, f = lax.axis_index("seq"), lax.axis_index("fsdp")
    near = sorted({1, *extra})
    slices = lax.axis_size("fsdp")
    for d in near:
        pl.semaphore_signal(
            barrier, inc=1, device_id={"seq": s ^ d}, device_id_type=pl.DeviceIdType.MESH
        )
    for d in range(1, slices):
        pl.semaphore_signal(
            barrier, inc=1, device_id={"fsdp": f ^ d}, device_id_type=pl.DeviceIdType.MESH
        )
    pl.semaphore_wait(barrier, len(near) + slices - 1)


def spread_part(
    rows, out_ref, full, out_rows, send, come, forward, passed,
    send_out, come_out, pass_out, passed_out, follow,
):
    near = list(range(2, lax.axis_size("seq"), 2))
    pair, core = core_pair(lax.axis_index("seq"))
    start, local, early, finish = spread_copies(rows, full, send, come, forward, passed)
    start()
    out_rows[pair, core] = out_ref[...].astype(jnp.bfloat16)
    pass_rows_start(out_rows, send_out, come_out, near)
    local()
    early()
    pass_rows_finish(out_rows, send_out, come_out, pass_out, passed_out, near)
    follow()
    finish()


def projections(x_ref, cosine_ref, sine_ref, full, normed, query, kv, gains):
    depth = full.shape[0] * 2 * full.shape[2] * full.shape[3]
    width, kv_width = HEADS * HEAD_DIM, KV_HEADS * HEAD_DIM

    def weights(first, count):
        return full[:, :, :, :, pl.ds(first, count)].reshape(depth, count)

    def turn(field):
        parts = []
        for i in range(field.shape[1] // 128):
            part = field[:, i * 128 : (i + 1) * 128]
            lane = lax.rem(lax.broadcasted_iota(jnp.int32, part.shape, 1), HEAD_DIM)
            other = jnp.where(
                lane < HEAD_DIM // 2,
                pltpu.roll(part, 128 - HEAD_DIM // 2, 1),
                pltpu.roll(part, HEAD_DIM // 2, 1),
            )
            parts.append(part * cosine_ref[...] + other * sine_ref[...])
        return jnp.concatenate(parts, axis=1)

    def keys_and_values():
        gains[...] = weights(width + 2 * kv_width, 128).astype(jnp.float32).T[:2]
        x = x_ref[...].astype(jnp.float32)
        normed[...] = (x * rms_scale(x) * gains[0:1, :]).astype(jnp.bfloat16)
        mixed = dot(normed[...], weights(width, 2 * kv_width))
        keys, values = turn(mixed[:, :kv_width]), mixed[:, kv_width:]
        kv[...] = jnp.concatenate(
            [
                field[:, h * HEAD_DIM : (h + 1) * HEAD_DIM]
                for h in range(KV_HEADS)
                for field in (keys, values)
            ],
            axis=1,
        ).astype(jnp.bfloat16)

    def queries():
        def query_part(i, _):
            first = pl.multiple_of(i * 512, 512)
            query[:, pl.ds(first, 512)] = turn(dot(normed[...], weights(first, 512))).astype(
                jnp.bfloat16
            )
            return 0

        lax.fori_loop(0, width // 512, query_part, 0)

    return keys_and_values, queries


def forward_kernel(
    in_rows, out_ref, x_ref, cosine_ref, sine_ref, dy_ref,
    in_full, normed, query_ref, gains, kv_all, mixed_ref, logs, out_full, middle, normed_second, dy_all, normed_near,
    kv_ref, out_rows, queries, largest, total, mixed,
    send_in, come_in, pass_in, passed_in, send_z, come_z, pass_z, passed_z,
    send_kv, come_kv, pass_kv, passed_kv, send_rows, come_rows, pass_rows, passed_rows,
    send_dy, come_dy, send_normed, come_normed, own_sem,
):
    group, s = lax.axis_size("seq"), lax.axis_index("seq")
    place, core = core_pair(s)
    local = query_ref.shape[0]
    per_head = HEADS // KV_HEADS
    width, pair = per_head * HEAD_DIM, 2 * HEAD_DIM
    near = list(range(2, group, 2))
    meet_spread(range(1, group))
    find_keys, find_queries = projections(
        x_ref, cosine_ref, sine_ref, in_full, normed, query_ref, kv_ref, gains
    )
    spread_start, spread_local, spread_early, spread_finish = spread_copies(
        out_rows, out_full, send_rows, come_rows, pass_rows, passed_rows
    )

    dy_order, dy_start, dy_take, dy_sent = gather_blocks(
        dy_ref, lambda owner, holder: dy_all.at[owner ^ holder], send_dy, come_dy
    )
    slices, f = lax.axis_size("fsdp"), lax.axis_index("fsdp")
    square = slices == 4

    def normed_copy(d):
        slot = 1 if square else d
        return remote(
            normed, normed_near.at[slot], send_normed.at[slot], come_normed.at[slot], "fsdp", f ^ d
        )

    near_normed = dy_order[:1] if square else range(1, slices)
    own_dy = pltpu.make_async_copy(dy_ref, dy_all.at[0], own_sem.at[0])
    own_dy.start()

    def links_early():
        spread_early()
        dy_start()

    def links_late():
        dy_take(0)
        for d in near_normed:
            normed_copy(d).start()

    def kv_copy(d, owner, target):
        chip, half = core_pair(owner)
        return remote(kv_ref, kv_all.at[chip, half], send_kv.at[d], come_kv.at[d], "seq", target)

    def hand_on(chip, half):
        block = kv_all.at[chip, half]
        return remote(block, block, pass_kv.at[chip, half], passed_kv.at[chip, half], "seq", s ^ 1)

    spread_part(
        in_rows, out_ref, in_full, out_rows, send_in, come_in, pass_in, passed_in,
        send_z, come_z, pass_z, passed_z, spread_start,
    )
    find_keys()
    kv_copy(1, s, s ^ 1).start()
    for d in near:

        @pl.when((s ^ d) > s)
        def _():
            kv_copy(d, s, s ^ d).start()

    spread_local()
    find_queries()
    kv_all[place, core] = kv_ref[...]
    for h in range(KV_HEADS):
        field = query_ref[:, pl.ds(h * width, width)]
        queries[h] = stack_heads(field, per_head) * jnp.bfloat16(HEAD_DIM**-0.5)
    links_early()

    def scores_of(h, chip, masked):
        kv = kv_all[chip, :, :, pl.ds(pl.multiple_of(h * pair, pair), pair)]
        kv = kv.reshape(2 * local, pair)
        keys, values = kv[:, :HEAD_DIM], kv[:, HEAD_DIM:]
        if masked:
            return masked_scores(keys, queries[h], local, core * local), values
        return against(keys, queries[h]), values

    def own_chip(h, _):
        scores, values = scores_of(h, place, True)
        new = jnp.max(scores, axis=0, keepdims=True)
        weights = jnp.exp(scores - new)
        largest[h] = new
        total[h] = jnp.sum(weights, axis=0, keepdims=True)
        mixed[h] = outer(values, weights.astype(jnp.bfloat16))
        return 0

    kv_copy(1, s ^ 1, s ^ 1).wait_recv()
    lax.fori_loop(0, KV_HEADS, own_chip, 0)

    @pl.when(place == 0)
    def _():
        links_late()

    def earlier_chip(turn, _):
        chip = place - 1 - turn

        @pl.when(turn == jnp.minimum(place - 1, 1))
        def _():
            links_late()

        owner = 2 * chip + core
        kv_copy(owner ^ s, owner, owner).wait_recv()
        hand_on(chip, core).start()
        hand_on(chip, 1 - core).wait_recv()

        def head(h, _):
            scores, values = scores_of(h, chip, False)
            new = jnp.maximum(largest[h], jnp.max(scores, axis=0, keepdims=True))
            fade = jnp.exp(largest[h] - new)
            weights = jnp.exp(scores - new)
            largest[h] = new
            total[h] = total[h] * fade + jnp.sum(weights, axis=0, keepdims=True)
            mixed[h] = mixed[h] * fade + outer(values, weights.astype(jnp.bfloat16))
            return 0

        lax.fori_loop(0, KV_HEADS, head, 0)
        return 0

    lax.fori_loop(0, place, earlier_chip, 0)

    for h in range(KV_HEADS):
        logs[h] = largest[h] + jnp.log(total[h])
        mixed_ref[:, pl.ds(h * width, width)] = unstack_heads(
            (mixed[h] / total[h]).T, per_head
        ).astype(mixed_ref.dtype)
    kv_copy(1, s, s ^ 1).wait_send()
    for d in near:

        @pl.when((s ^ d) > s)
        def _():
            kv_copy(d, s, s ^ d).wait_send()

    def handed(chip, _):
        hand_on(chip, core).wait_send()
        return 0

    lax.fori_loop(0, place, handed, 0)
    spread_finish()

    depth = out_full.shape[0] * 2 * out_full.shape[2] * out_full.shape[3]

    def middle_part(i, _):
        columns = pl.ds(pl.multiple_of(i * 512, 512), 512)
        weights = out_full[:, :, :, :, columns].reshape(depth, 512)
        middle[:, columns] = x_ref[:, columns].astype(jnp.float32) + dot(mixed_ref[...], weights)
        return 0

    lax.fori_loop(0, middle.shape[1] // 512, middle_part, 0)
    field = middle[...]
    normed_second[...] = (field * rms_scale(field) * gains[1:2, :]).astype(jnp.bfloat16)
    own_normed = pltpu.make_async_copy(normed, normed_near.at[0], own_sem.at[1])
    own_normed.start()
    for turn in range(1, len(dy_order)):
        dy_take(turn)
    dy_sent()
    for d in near_normed:
        normed_copy(d).wait()
    own_dy.wait()
    own_normed.wait()


def backward_kernel(
    grad_ref, query_ref, mixed_ref, logs, kv_all, branch_ref,
    cosine_ref, sine_ref, cosine_rows, sine_rows, out_parts,
    inward_grad, inward_slices, attended_all, branch_all, out_come, kv_grad,
    queries, grads, inner, query_sum, parts, part_come, final_come,
    send_part, come_part, send_final, come_final, send_slice, come_slice,
    send_mixed, come_mixed, send_out, come_out,
):
    group, s = lax.axis_size("seq"), lax.axis_index("seq")
    place, core = core_pair(s)
    local = query_ref.shape[0]
    per_head = HEADS // KV_HEADS
    width, pair = per_head * HEAD_DIM, 2 * HEAD_DIM
    scale = HEAD_DIM**-0.5
    slices, f = lax.axis_size("fsdp"), lax.axis_index("fsdp")
    share = branch_all.shape[2]
    meet_spread(range(1, group))

    def slice_copy(d, target):
        columns = pl.ds(pl.multiple_of(target * share, 128), share)
        return remote(
            branch_ref.at[:, columns], branch_all.at[d], send_slice.at[d], come_slice.at[d],
            "fsdp", target,
        )

    gathers = [
        gather_blocks(mixed_ref, lambda owner, holder: attended_all.at[owner ^ holder],
                      send_mixed, come_mixed),
    ]

    def out_copy(d):
        return remote(
            out_parts.at[d], out_come.at[d - 1], send_out.at[d], come_out.at[d], "fsdp", f ^ d
        )

    def gathers_early():
        for _, _, take, _ in gathers:
            take(0)

    def part_copy(chip, half):
        return remote(
            parts.at[chip, half], part_come.at[chip], send_part.at[chip], come_part.at[chip],
            "seq", s ^ 1,
        )

    def final_copy(chip, sender):
        return remote(
            parts.at[chip, core], final_come.at[sender], send_final.at[chip], come_final.at[sender],
            "seq", 2 * chip + core,
        )

    for d in range(1, slices):
        slice_copy(d, f ^ d).start()
    for _, begin, _, _ in gathers:
        begin()
    for d in range(1, slices):
        out_copy(d).start()
    attended_all[0] = mixed_ref[...]
    branch_all[0] = branch_ref[:, pl.ds(pl.multiple_of(f * share, 128), share)]
    for h in range(KV_HEADS):
        columns = pl.ds(h * width, width)
        queries[h] = stack_heads(query_ref[:, columns], per_head) * jnp.bfloat16(scale)
        grad = stack_heads(grad_ref[:, columns], per_head)
        grads[h] = grad
        product = grad.astype(jnp.float32) * stack_heads(mixed_ref[:, columns], per_head).astype(
            jnp.float32
        )
        inner[h] = jnp.sum(product.T, axis=0, keepdims=True)
    query_sum[...] = jnp.zeros_like(query_sum)

    def head_grads(h, chip, masked):
        columns = pl.ds(pl.multiple_of(h * pair, pair), pair)
        kv = kv_all[chip, :, :, columns].reshape(2 * local, pair)
        keys, values = kv[:, :HEAD_DIM], kv[:, HEAD_DIM:]
        if masked:
            scores = masked_scores(keys, queries[h], local, core * local)
        else:
            scores = against(keys, queries[h])
        shares = jnp.exp(scores - logs[h])
        share_grad = against(values, grads[h])
        score_grad = (shares * (share_grad - inner[h])).astype(jnp.bfloat16)
        value_grad = dot(shares.astype(jnp.bfloat16), grads[h])
        key_grad = dot(score_grad, queries[h])
        part = jnp.concatenate([key_grad, value_grad], axis=1).astype(jnp.bfloat16)
        parts[chip, :, :, columns] = part.reshape(2, local, pair)
        query_sum[h] += outer(keys, score_grad)
        return 0

    def finish_chip(chip):
        part_copy(chip, core).wait_recv()
        parts[chip, core] = (
            parts[chip, core].astype(jnp.float32) + part_come[chip].astype(jnp.float32)
        ).astype(jnp.bfloat16)
        final_copy(chip, place).start()

    def earlier_chip(chip, _):
        @pl.when(chip == place - 1)
        def _():
            gathers_early()

        lax.fori_loop(0, KV_HEADS, lambda h, c: head_grads(h, chip, False), 0)
        part_copy(chip, 1 - core).start()

        @pl.when(chip > 0)
        def _():
            finish_chip(chip - 1)

        return 0

    lax.fori_loop(0, place, earlier_chip, 0)

    @pl.when(place > 0)
    def _():
        finish_chip(place - 1)

    lax.fori_loop(0, KV_HEADS, lambda h, c: head_grads(h, place, True), 0)

    @pl.when(core == 1)
    def _():
        part_copy(place, 0).start()

    @pl.when(place == 0)
    def _():
        gathers_early()

    half = HEAD_DIM // 2
    for h in range(KV_HEADS):
        total = query_sum[h] * scale
        one, two = total[:half], total[half:]
        turned = jnp.concatenate(
            [
                one * cosine_ref[...] + two * sine_ref[...],
                two * cosine_ref[...] - one * sine_ref[...],
            ],
            axis=0,
        )
        inward_grad[:, pl.ds(h * width, width)] = unstack_heads(turned.T, per_head).astype(
            jnp.bfloat16
        )
    kv_grad[...] = parts[place, core].astype(jnp.float32)

    @pl.when(core == 0)
    def _():
        part_copy(place, 0).wait_recv()
        kv_grad[...] += part_come[place].astype(jnp.float32)

    def later_chip(chip, _):
        final_copy(place, chip).wait_recv()
        kv_grad[...] += final_come[chip].astype(jnp.float32)
        return 0

    lax.fori_loop(place + 1, group // 2, later_chip, 0)
    key_grads, value_grads = [], []
    for h in range(KV_HEADS):
        field = kv_grad[:, pl.ds(h * pair, pair)]
        one, two = field[:, :half], field[:, half:HEAD_DIM]
        key_grads.append(one * cosine_rows[...] + two * sine_rows[...])
        key_grads.append(two * cosine_rows[...] - one * sine_rows[...])
        value_grads.append(field[:, HEAD_DIM:])
    inward_grad[:, pl.ds(HEADS * HEAD_DIM, 2 * KV_HEADS * HEAD_DIM)] = jnp.concatenate(
        key_grads + value_grads, axis=1
    ).astype(jnp.bfloat16)
    rest = inward_grad.shape[1] - slices * inward_slices.shape[2]
    inward_grad[:, pl.ds(inward_grad.shape[1] - rest, rest)] = jnp.zeros((local, rest), jnp.bfloat16)
    part_cols = inward_slices.shape[2]
    for t in range(slices):
        inward_slices[t] = inward_grad[:, pl.ds(t * part_cols, part_cols)]

    def sent(chip, _):
        part_copy(chip, 1 - core).wait_send()
        final_copy(chip, place).wait_send()
        return 0

    lax.fori_loop(0, place, sent, 0)

    @pl.when(core == 1)
    def _():
        part_copy(place, 0).wait_send()

    for d in range(1, slices):
        out_copy(d).wait()
        slice_copy(d, f ^ d).wait()
    for order, _, take, finish in gathers:
        for turn in range(1, len(order)):
            take(turn)
        finish()


def attend_forward(rows, w_outward, x, cosine, sine, upstream, group, slices):
    local, width = x.shape
    pairs, two, depth, inward_width = rows.shape
    outward_width = w_outward.shape[1]
    kv_cols = 2 * KV_HEADS * HEAD_DIM
    columns = HEADS // KV_HEADS * local
    low = jax.ShapeDtypeStruct((local, width), jnp.bfloat16)
    tiles = KV_HEADS * group * columns * local
    four_slices = [pltpu.SemaphoreType.DMA((slices,))] * 4
    in_full, *results = pl.pallas_call(
        forward_kernel,
        in_specs=[VMEM] * 5 + [ANY],
        out_specs=[VMEM] * 10 + [ANY] * 2,
        out_shape=[
            jax.ShapeDtypeStruct((pairs, two, slices, depth, inward_width), jnp.bfloat16),
            low,
            low,
            jax.ShapeDtypeStruct((2, width), jnp.float32),
            jax.ShapeDtypeStruct((pairs, two, local, kv_cols), jnp.bfloat16),
            low,
            jax.ShapeDtypeStruct((KV_HEADS, 1, columns), jnp.float32),
            jax.ShapeDtypeStruct((pairs, two, slices, depth, outward_width), jnp.bfloat16),
            jax.ShapeDtypeStruct((local, width), jnp.float32),
            low,
            jax.ShapeDtypeStruct((slices, local, width), jnp.bfloat16),
            jax.ShapeDtypeStruct((2 if slices == 4 else slices, local, width), jnp.bfloat16),
        ],
        scratch_shapes=[
            pltpu.VMEM((local, kv_cols), jnp.bfloat16),
            pltpu.VMEM((pairs, two, depth, outward_width), jnp.bfloat16),
            pltpu.VMEM((KV_HEADS, columns, HEAD_DIM), jnp.bfloat16),
            pltpu.VMEM((KV_HEADS, 1, columns), jnp.float32),
            pltpu.VMEM((KV_HEADS, 1, columns), jnp.float32),
            pltpu.VMEM((KV_HEADS, HEAD_DIM, columns), jnp.float32),
        ]
        + four_slices
        + [pltpu.SemaphoreType.DMA((group,))] * 6
        + [pltpu.SemaphoreType.DMA((pairs, 2))] * 2
        + four_slices
        + four_slices
        + [pltpu.SemaphoreType.DMA((2,))],
        compiler_params=pltpu.CompilerParams(
            vmem_limit_bytes=60 << 20, collective_id=0, has_side_effects=True
        ),
        cost_estimate=pl.CostEstimate(
            flops=tiles * HEAD_DIM * 160, bytes_accessed=20 << 20, transcendentals=tiles
        ),
    )(
        rows, w_outward, x, jnp.tile(cosine, (1, 4)),
        jnp.tile(jnp.concatenate([-sine, sine], axis=1), (1, 2)), upstream,
    )
    return in_full.reshape(-1, inward_width), *results


def attend_backward(
    grads, query, mixed, logs, kv_all, branch, cosine, sine, out_parts, group, slices
):
    local, features = branch.shape
    per_head = HEADS // KV_HEADS
    columns = per_head * local
    kv_cols = kv_all.shape[3]
    inward_cols = features + kv_cols
    tiles = KV_HEADS * group * columns * local
    gathered = jax.ShapeDtypeStruct((slices, local, features), jnp.bfloat16)
    stacked = pltpu.VMEM((KV_HEADS, columns, HEAD_DIM), jnp.bfloat16)
    one_half = pltpu.VMEM((group // 2, local, kv_cols), jnp.bfloat16)
    return pl.pallas_call(
        backward_kernel,
        in_specs=[VMEM] * 10 + [ANY],
        out_specs=[VMEM] * 4 + [ANY],
        out_shape=[
            jax.ShapeDtypeStruct((local, inward_cols + 128), jnp.bfloat16),
            jax.ShapeDtypeStruct((slices, local, inward_cols // slices), jnp.bfloat16),
            gathered,
            jax.ShapeDtypeStruct((slices, local, features // slices), jnp.bfloat16),
            jax.ShapeDtypeStruct((slices - 1, local, features), jnp.bfloat16),
        ],
        scratch_shapes=[
            pltpu.VMEM((local, kv_cols), jnp.float32),
            stacked,
            stacked,
            pltpu.VMEM((KV_HEADS, 1, columns), jnp.float32),
            pltpu.VMEM((KV_HEADS, HEAD_DIM, columns), jnp.float32),
            pltpu.VMEM((group // 2, 2, local, kv_cols), jnp.bfloat16),
            one_half,
            one_half,
        ]
        + [pltpu.SemaphoreType.DMA((group // 2,))] * 4
        + [pltpu.SemaphoreType.DMA((slices,))] * 4
        + [pltpu.SemaphoreType.DMA((slices,))] * 2,
        compiler_params=pltpu.CompilerParams(
            vmem_limit_bytes=60 << 20, collective_id=1, has_side_effects=True
        ),
        cost_estimate=pl.CostEstimate(
            flops=tiles * HEAD_DIM * 80, bytes_accessed=20 << 20, transcendentals=tiles
        ),
    )(
        grads, query, mixed, logs, kv_all, branch,
        jnp.tile(cosine.T, (1, per_head)), jnp.tile(sine.T, (1, per_head)), cosine, sine,
        out_parts,
    )


def meet_slices():
    slices, f = lax.axis_size("fsdp"), lax.axis_index("fsdp")
    barrier = pltpu.get_barrier_semaphore()
    for d in range(1, slices):
        pl.semaphore_signal(
            barrier, inc=1, device_id={"fsdp": f ^ d}, device_id_type=pl.DeviceIdType.MESH
        )
    pl.semaphore_wait(barrier, slices - 1)


def row_copy(stage, target, sem, r):
    width = stage.shape[0]
    rows = pl.ds(pl.multiple_of(r * width, width), width)
    return pltpu.make_async_copy(stage, target.at[rows, :], sem)


def grad_rows(field, grads, target, stage, sems):
    width = stage.shape[1]
    steps = target.shape[0] // width

    def step(r, _):
        columns = pl.ds(pl.multiple_of(r * width, width), width)
        slot = lax.rem(r, 2)
        left = field[:, :, columns].reshape(grads[0].shape[0], width)

        @pl.when(r > 1)
        def _():
            row_copy(stage.at[slot], target, sems.at[slot], r - 2).wait()

        for k, grad in enumerate(grads):
            units = grad.shape[1]
            stage[slot, :, pl.ds(k * units, units)] = outer(left, grad[...]).astype(jnp.bfloat16)
        row_copy(stage.at[slot], target, sems.at[slot], r).start()
        return 0

    lax.fori_loop(0, steps, step, 0)
    for r in (steps - 2, steps - 1):
        row_copy(stage.at[r % 2], target, sems.at[r % 2], r).wait()


def feed_first_kernel(
    *refs, slices, strip
):
    (
        dy_ref, x_ref, gate_up_ref, normed_ref,
        x_all, gate_all, up_all, hidden, down_grad_out, normed_other,
        gate_sum, up_sum, grad_stage, dy_all, send_x, come_x, grad_sem, dy_sem,
        send_normed, come_normed,
    ) = refs
    f = lax.axis_index("fsdp")
    local = x_ref.shape[0]
    for d in range(slices):
        pltpu.make_async_copy(dy_ref.at[d], dy_all.at[d], dy_sem.at[d]).start()
    meet_slices()

    order, begin, take, sent = gather_blocks(
        x_ref, lambda owner, holder: x_all.at[owner ^ holder], send_x, come_x
    )
    begin()
    x_all[0] = x_ref[...]

    square = slices == 4

    def normed_copy():
        return remote(normed_ref, normed_other, send_normed, come_normed, "fsdp", f ^ order[1])

    def token_block(turn, d):
        for i in range(slices - 1):

            @pl.when(turn == i + 1)
            def _():
                take(i)
                if square and i == 2:
                    normed_copy().start()

        x = x_all[d]
        units = hidden.shape[1]
        gate_sum[...] = dot(x, gate_up_ref[:, pl.ds(0, units)])
        up_sum[...] = dot(x, gate_up_ref[:, pl.ds(units, units)])

        def part(i, _):
            rows = pl.ds(pl.multiple_of(i * strip, strip), strip)
            place = pl.ds(pl.multiple_of(d * local + i * strip, strip), strip)
            gate, up = gate_sum[rows, :], up_sum[rows, :]
            hidden[place, :] = (gate / (1.0 + jnp.exp(-gate)) * up).astype(jnp.bfloat16)
            gate_all[place, :] = gate.astype(jnp.bfloat16)
            up_all[place, :] = up.astype(jnp.bfloat16)
            return 0

        lax.fori_loop(0, local // strip, part, 0)
        following = 0
        for i in reversed(range(slices - 1)):
            following = jnp.where(turn == i, order[i], following)
        return following

    lax.fori_loop(0, slices, token_block, jnp.int32(0))
    for d in range(slices):
        pltpu.make_async_copy(dy_ref.at[d], dy_all.at[d], dy_sem.at[d]).wait()
    grad_rows(dy_all, [hidden], down_grad_out, grad_stage, grad_sem)
    sent()
    if square:
        normed_copy().wait()


def feed_second_kernel(
    *refs, slices, strip
):
    (
        dy_ref, x_ref, gate_all, up_all, hidden, gate_up_ref, down_ref, normed_near,
        back_ref, out_parts, gate_up_grad_out, normed_far,
        dy_all,
        gate_grad, up_grad, hidden_sum, back_send, back_come, out_stage, grad_stage,
        send_back, come_back, out_sem, grad_sem, dy_sem,
        send_normed, come_normed,
    ) = refs
    f = lax.axis_index("fsdp")
    local = back_ref.shape[0]

    def dy_copy(d):
        return pltpu.make_async_copy(dy_ref.at[d], dy_all.at[d], dy_sem.at[d])

    for d in range(slices):
        dy_copy(d).start()
    meet_slices()
    square = slices == 4
    order = block_order()
    first, second = (order[1], order[0]) if square else (None, None)
    turns = [3, second, first, 0] if square else list(range(slices - 1, -1, -1))

    def relay():
        return remote(
            normed_near.at[1], normed_far, send_normed, come_normed, "fsdp", f ^ order[1]
        )

    if square:
        relay().start()
    for d in range(slices):
        dy_copy(d).wait()

    def back_copy(d, target, landing):
        return remote(
            back_send.at[d], back_come.at[landing - 1], send_back.at[d], come_back.at[landing],
            "fsdp", f ^ target,
        )

    def out_copy(slot, d):
        return pltpu.make_async_copy(out_stage.at[slot], out_parts.at[d], out_sem.at[slot])

    def token_block(turn, carry):
        d, before = carry
        place = pl.ds(pl.multiple_of(d * local, local), local)
        hidden_sum[...] = dot(dy_all[d], down_ref[...])

        def part(i, _):
            rows = pl.ds(pl.multiple_of(i * strip, strip), strip)
            here = pl.ds(pl.multiple_of(d * local + i * strip, strip), strip)
            gate = gate_all[here, :].astype(jnp.float32)
            up = up_all[here, :].astype(jnp.float32)
            sigmoid = 1.0 / (1.0 + jnp.exp(-gate))
            grad = hidden_sum[rows, :]
            gate_grad[here, :] = (
                grad * up * sigmoid * (1.0 + gate * (1.0 - sigmoid))
            ).astype(jnp.bfloat16)
            up_grad[here, :] = (grad * gate * sigmoid).astype(jnp.bfloat16)
            return 0

        lax.fori_loop(0, local // strip, part, 0)
        units = hidden.shape[1]
        back = against(gate_grad[place, :], gate_up_ref[:, pl.ds(0, units)])
        back = back + against(up_grad[place, :], gate_up_ref[:, pl.ds(units, units)])
        back_send[d] = back.astype(jnp.bfloat16)
        if square:

            @pl.when(turn == 0)
            def _():
                back_copy(3, first, 3).start()

            @pl.when(turn == 2)
            def _():
                back_copy(3, first, 3).wait_recv()
                back_send[second] = (
                    back_send[second].astype(jnp.float32) + back_come[2].astype(jnp.float32)
                ).astype(jnp.bfloat16)
                back_copy(second, second, second).start()
                back_copy(first, first, first).start()

        else:

            @pl.when(d > 0)
            def _():
                back_copy(d, d, d).start()

        @pl.when(turn > 1)
        def _():
            out_copy(lax.rem(turn, 2), before).wait()

        out_stage[lax.rem(turn, 2)] = against(hidden[place, :], down_ref[...]).astype(jnp.bfloat16)
        out_copy(lax.rem(turn, 2), d).start()
        following = 0
        for i in reversed(range(slices - 1)):
            following = jnp.where(turn == i, turns[i + 1], following)
        return following, d

    lax.fori_loop(0, slices, token_block, (jnp.int32(turns[0]), jnp.int32(0)))
    out_copy(0, 0).wait()
    out_copy(1, 0).wait()
    grad_rows(x_ref, [gate_grad, up_grad], gate_up_grad_out, grad_stage, grad_sem)
    if square:
        relay().wait()
        back_copy(3, first, 3).wait_send()
    for d in (1, 2) if square else range(1, slices):
        back_copy(d, d, d).wait()
    home = [back_send[0]] + [back_come[d - 1] for d in ((1, 2) if square else range(1, slices))]
    back_ref[...] = functools.reduce(jnp.add, [p.astype(jnp.float32) for p in home])


ANY = pl.BlockSpec(memory_space=pl.ANY)


def feed_first(x, upstream_all, gate_up_slice, normed):
    slices, local, width = upstream_all.shape
    ff_cols = gate_up_slice.shape[1] // 2
    tokens = slices * local
    units = jax.ShapeDtypeStruct((tokens, ff_cols), jnp.bfloat16)
    high = pltpu.VMEM((local, ff_cols), jnp.float32)
    sems = pltpu.SemaphoreType.DMA((slices,))
    return pl.pallas_call(
        functools.partial(feed_first_kernel, slices=slices, strip=32),
        in_specs=[ANY] + [VMEM] * 3,
        out_specs=[VMEM] * 4 + [ANY] * 2,
        out_shape=[
            jax.ShapeDtypeStruct((slices, local, width), jnp.bfloat16),
            units,
            units,
            units,
            jax.ShapeDtypeStruct((width, ff_cols), jnp.bfloat16),
            jax.ShapeDtypeStruct((local, width), jnp.bfloat16),
        ],
        scratch_shapes=[
            high,
            high,
            pltpu.VMEM((2, 256, ff_cols), jnp.bfloat16),
            pltpu.VMEM((slices, local, width), jnp.bfloat16),
            sems,
            sems,
            pltpu.SemaphoreType.DMA((2,)),
            sems,
            pltpu.SemaphoreType.DMA,
            pltpu.SemaphoreType.DMA,
        ],
        compiler_params=pltpu.CompilerParams(
            vmem_limit_bytes=60 << 20, collective_id=4, has_side_effects=True
        ),
        cost_estimate=pl.CostEstimate(
            flops=10 * tokens * width * ff_cols, bytes_accessed=30 << 20, transcendentals=0
        ),
    )(upstream_all, x, gate_up_slice, normed)


def feed_second(
    x_all, upstream_all, gate_all, up_all, hidden, gate_up_slice, down_slice, normed_near
):
    slices, local, width = x_all.shape
    ff_cols = gate_up_slice.shape[1] // 2
    tokens = slices * local
    blocks = pltpu.VMEM((slices, local, width), jnp.bfloat16)
    low = pltpu.VMEM((tokens, ff_cols), jnp.bfloat16)
    sems = pltpu.SemaphoreType.DMA((slices,))
    pair = pltpu.SemaphoreType.DMA((2,))
    return pl.pallas_call(
        functools.partial(feed_second_kernel, slices=slices, strip=32),
        in_specs=[ANY] + [VMEM] * 6 + [ANY],
        out_specs=[VMEM] + [ANY] * 3,
        out_shape=[
            jax.ShapeDtypeStruct((local, width), jnp.float32),
            jax.ShapeDtypeStruct((slices, local, width), jnp.bfloat16),
            jax.ShapeDtypeStruct((width, 2 * ff_cols), jnp.bfloat16),
            jax.ShapeDtypeStruct((local, width), jnp.bfloat16),
        ],
        scratch_shapes=[
            blocks,
            low,
            low,
            pltpu.VMEM((local, ff_cols), jnp.float32),
            blocks,
            pltpu.VMEM((slices - 1, local, width), jnp.bfloat16),
            pltpu.VMEM((2, local, width), jnp.bfloat16),
            pltpu.VMEM((2, 256, 2 * ff_cols), jnp.bfloat16),
            sems,
            sems,
            pair,
            pair,
            sems,
            pltpu.SemaphoreType.DMA,
            pltpu.SemaphoreType.DMA,
        ],
        compiler_params=pltpu.CompilerParams(
            vmem_limit_bytes=62 << 20, collective_id=5, has_side_effects=True
        ),
        cost_estimate=pl.CostEstimate(
            flops=20 * tokens * width * ff_cols, bytes_accessed=40 << 20, transcendentals=0
        ),
    )(
        upstream_all, x_all, gate_all, up_all, hidden, gate_up_slice, down_slice,
        normed_near,
    )


def home_kernel(*refs, count, results, moves, gains):
    slices, f = lax.axis_size("fsdp"), lax.axis_index("fsdp")
    group, s = lax.axis_size("seq"), lax.axis_index("seq")
    inputs, refs = refs[: count + gains], refs[count + gains :]
    outputs, refs = refs[: results + gains], refs[results + gains :]
    landed, refs = refs[:count], refs[count:]
    send, come = refs[:2]
    depth = inputs[0].shape[0] // slices
    if gains:
        meet_spread(range(1, group))
    else:
        meet_slices()

    def copy(k, d):
        rows = pl.ds(pl.multiple_of((f ^ d) * depth, depth), depth)
        return remote(
            inputs[k].at[rows, :], landed[k].at[d], send.at[k, d], come.at[k, d], "fsdp", f ^ d
        )

    if gains:
        seq_come, tiles, tile_come, seq_send, seq_sem, tile_send, tile_sem = refs[2:]

        def seq_copy(d):
            return remote(
                inputs[count].at[s ^ d], seq_come.at[d], seq_send.at[d], seq_sem.at[d], "seq", s ^ d
            )

        def tile_copy(d):
            return remote(
                tiles.at[f ^ d], tile_come.at[d], tile_send.at[d], tile_sem.at[d], "fsdp", f ^ d
            )

        for d in range(1, group):
            seq_copy(d).start()
    for k in range(count):
        for d in range(1, slices):
            copy(k, d).start()
    for k in range(count):
        landed[k][0] = inputs[k][pl.ds(pl.multiple_of(f * depth, depth), depth), :]
    if gains:
        seq_come[0] = inputs[count][s]
        for d in range(1, group):
            seq_copy(d).wait()
        total = functools.reduce(jnp.add, [seq_come[d] for d in range(group)])
        part = total.shape[1] // slices
        tiles[...] = jnp.zeros_like(tiles)
        for t in range(slices):
            tiles[t, :, pl.ds(0, part)] = total[:, t * part : (t + 1) * part]
        for d in range(1, slices):
            tile_copy(d).start()
        tile_come[0] = tiles[f]
    for k in range(count):
        for d in range(1, slices):
            copy(k, d).wait()
    for t in range(slices):
        for source, first, width, result, base in moves:
            outputs[result][:, pl.ds(base + t * width, width)] = landed[source][
                f ^ t, :, pl.ds(first, width)
            ]
    if gains:
        for d in range(1, slices):
            tile_copy(d).wait()
        outputs[results][...] = functools.reduce(jnp.add, [tile_come[d] for d in range(slices)])


def bring_home(sources, moves, widths, gains, group, slices, number):
    depth = sources[0].shape[0] // slices
    shapes = [jax.ShapeDtypeStruct((depth, width), jnp.bfloat16) for width in widths]
    scratch = [pltpu.VMEM((slices, depth, s.shape[1]), jnp.bfloat16) for s in sources]
    scratch += [pltpu.SemaphoreType.DMA((len(sources), slices))] * 2
    extra = []
    if gains is not None:
        extra = [gains]
        shapes.append(jax.ShapeDtypeStruct((8, 128), jnp.float32))
        scratch += [
            pltpu.VMEM(gains.shape, jnp.float32),
            pltpu.VMEM((slices, 8, 128), jnp.float32),
            pltpu.VMEM((slices, 8, 128), jnp.float32),
        ]
        scratch += [pltpu.SemaphoreType.DMA((group,))] * 2
        scratch += [pltpu.SemaphoreType.DMA((slices,))] * 2
    return pl.pallas_call(
        functools.partial(
            home_kernel, count=len(sources), results=len(widths), moves=moves, gains=len(extra)
        ),
        in_specs=[VMEM] * (len(sources) + len(extra)),
        out_specs=[VMEM] * len(shapes),
        out_shape=shapes,
        scratch_shapes=scratch,
        compiler_params=pltpu.CompilerParams(
            vmem_limit_bytes=32 << 20, collective_id=number, has_side_effects=True
        ),
        cost_estimate=pl.CostEstimate(flops=10 << 30, bytes_accessed=4 << 20, transcendentals=0),
    )(*sources, *extra)


def swap(piece, axis, offset):
    size = lax.axis_size(axis)
    return lax.ppermute(piece, axis, [(i, i ^ offset) for i in range(size)])


def gather_swap(piece, axis):
    return [piece] + [swap(piece, axis, d) for d in range(1, lax.axis_size(axis))]


def exchange_swap(stack, axis):
    me = lax.axis_index(axis)
    pieces = [
        lax.dynamic_index_in_dim(stack, me ^ d, 0, keepdims=False)
        for d in range(lax.axis_size(axis))
    ]
    return [pieces[0]] + [swap(p, axis, d) for d, p in enumerate(pieces) if d]


def reduce_swap(parts, axis):
    total = parts[0].astype(jnp.float32)
    for d in range(1, len(parts)):
        total = total + swap(parts[d], axis, d).astype(jnp.float32)
    return total


def scatter_rows(partial, after=()):
    partial, *_ = lax.optimization_barrier((partial, *after))
    return lax.psum_scatter(partial, "seq", scatter_dimension=0, tiled=True)


def adam_update(weight, first, second, grad, rate, decay):
    first_new = beta_first * first + (1.0 - beta_first) * grad
    second_new = beta_second * second + (1.0 - beta_second) * grad * grad
    first_hat = first_new / (1.0 - beta_first**STEP)
    second_hat = second_new / (1.0 - beta_second**STEP)
    weight_new = weight - rate * (
        first_hat / (jnp.sqrt(second_hat) + adam_epsilon) + decay * weight
    )
    return (first_new, second_new, weight_new)


def body(
    inputs,
    cotangent,
    w_inward,
    w_outward,
    w_gate_up,
    w_down,
    gains,
    first_inward,
    first_outward,
    first_gate_up,
    first_down,
    first_gains,
    second_inward,
    second_outward,
    second_gate_up,
    second_down,
    second_gains,
):
    rows = inputs[0].astype(jnp.float32)
    upstream = cotangent[0]
    local = rows.shape[0]
    group = lax.axis_size("seq")
    slices = lax.axis_size("fsdp")
    kv_width = KV_HEADS * HEAD_DIM
    inward_cols = D + 2 * kv_width
    ff_cols = FF // slices
    depth = w_inward.shape[0]
    position = (lax.axis_index("seq") * local + jnp.arange(local)).astype(jnp.float32)

    low_gains = jnp.pad(jnp.transpose(gains.astype(jnp.bfloat16)), ((0, 0), (0, 126)))
    feed_gate_up, feed_down, in_rows = share_weights(
        w_inward, low_gains, w_gate_up, w_down, group, slices
    )
    gate_up_slice = lax.all_gather(feed_gate_up, "seq", axis=0, tiled=True)
    exponent = jnp.arange(HEAD_DIM // 2).astype(jnp.float32) * (-2.0 / HEAD_DIM)
    angle = position[:, None] * jnp.power(rope_base, exponent)[None, :]
    cosine, sine = jnp.cos(angle), jnp.sin(angle)
    (
        inward_gains, normed, query, gains_full, kv_all, attended, logs, outward_full,
        middle, normed_second, upstream_all, normed_near,
    ) = attend_forward(in_rows, w_outward, inputs[0], cosine, sine, upstream, group, slices)
    gain_first, gain_second = gains_full[0], gains_full[1]
    scale_first = rms_scale(rows)
    scale_second = rms_scale(middle)
    down_slice = lax.all_gather(feed_down, "seq", axis=0, tiled=True)
    outward_full = outward_full.reshape(D, D)
    normed_all, gate_all, up_all, hidden, down_partial, normed_other = feed_first(
        normed_second, upstream_all, gate_up_slice, normed
    )
    normed_second_grad, out_parts, gate_up_partial, normed_far = feed_second(
        normed_all, upstream_all, gate_all, up_all, hidden, gate_up_slice, down_slice,
        normed_near,
    )
    down_mine = scatter_rows(down_partial)
    gate_up_mine = scatter_rows(gate_up_partial)
    middle_back, gain_second_grad = norm_back(middle, scale_second, gain_second, normed_second_grad)
    middle_grad = upstream.astype(jnp.float32) + middle_back
    branch_low = middle_grad.astype(jnp.bfloat16)
    attended_grad = against(branch_low, outward_full).astype(jnp.bfloat16)
    inward_grad, inward_slices, attended_all, branch_all, out_come = attend_backward(
        attended_grad, query, attended, logs, kv_all, branch_low,
        cosine, sine, out_parts, group, slices,
    )
    inward_grad, inward_slices, attended_all, branch_all, down_mine, normed_far = (
        lax.optimization_barrier(
            (inward_grad, inward_slices, attended_all, branch_all, down_mine, normed_far)
        )
    )
    inward_grad_blocks = exchange_swap(inward_slices, "fsdp")
    outward_partial = outer(attended_all.reshape(-1, D), branch_all.reshape(-1, D // slices))
    outward_partial = outward_partial.astype(jnp.bfloat16)

    if slices == 4:
        own, one, two, far = inward_grad_blocks
        even = lax.rem(lax.axis_index("seq"), 2) == 0
        near_blocks = jnp.concatenate([own, jnp.where(even, two, one)], axis=0)
        inward_partial = (
            outer(normed_near.reshape(-1, D), near_blocks)
            + outer(normed_other, jnp.where(even, one, two))
            + outer(normed_far, far)
        )
    else:
        inward_partial = outer(
            normed_near.reshape(-1, D), jnp.concatenate(inward_grad_blocks, axis=0)
        )
    inward_partial = inward_partial.astype(jnp.bfloat16)
    slice_cols = inward_partial.shape[1]
    inward_partial, gate_up_mine, inward_grad = lax.optimization_barrier(
        (jnp.concatenate([inward_partial, outward_partial], axis=1), gate_up_mine, inward_grad)
    )
    inward_mine = scatter_rows(inward_partial)
    normed_grad = against(inward_grad, inward_gains)
    rows_back, gain_first_grad = norm_back(rows, scale_first, gain_first, normed_grad)
    input_grad = middle_grad + rows_back
    gain_grads = jnp.stack([gain_first_grad, gain_second_grad]).reshape(2, group, D // group)
    gain_grads = jnp.pad(gain_grads.transpose(1, 0, 2), ((0, 0), (0, 6), (0, 0)))
    result = middle + functools.reduce(
        jnp.add,
        [p.astype(jnp.float32) for p in [out_parts[0]] + [out_come[d] for d in range(slices - 1)]],
    )
    gate_up_sum, down_sum, gains_sum = bring_home(
        [gate_up_mine, down_mine],
        [(0, 0, ff_cols, 0, 0), (0, ff_cols, ff_cols, 0, FF), (1, 0, ff_cols, 1, 0)],
        [2 * FF, FF], gain_grads, group, slices, 6,
    )
    inward_sum, outward_sum = bring_home(
        [inward_mine],
        [(0, 0, slice_cols, 0, 0), (0, slice_cols, D // slices, 1, 0)],
        [inward_cols, D], None, group, slices, 7,
    )
    gate_up_sum, down_sum, inward_sum, outward_sum = [
        field.astype(jnp.float32) for field in (gate_up_sum, down_sum, inward_sum, outward_sum)
    ]
    gains_sum = gains_sum[:2, :depth]
    first_inward_new, second_inward_new, inward_new = adam_update(
        w_inward, first_inward, second_inward, inward_sum, 0.02, weight_decay
    )
    first_outward_new, second_outward_new, outward_new = adam_update(
        w_outward, first_outward, second_outward, outward_sum, 0.15, weight_decay
    )
    first_gate_up_new, second_gate_up_new, gate_up_new = adam_update(
        w_gate_up, first_gate_up, second_gate_up, gate_up_sum, 0.02, weight_decay
    )
    first_down_new, second_down_new, down_new = adam_update(
        w_down, first_down, second_down, down_sum, 0.015, weight_decay
    )
    first_gains_new, second_gains_new, gains_new = adam_update(
        gains, first_gains, second_gains, gains_sum, 0.6, 0.0
    )
    return (
        result[None].astype(jnp.bfloat16),
        input_grad[None],
        first_inward_new,
        second_inward_new,
        inward_new,
        first_outward_new,
        second_outward_new,
        outward_new,
        first_gate_up_new,
        second_gate_up_new,
        gate_up_new,
        first_down_new,
        second_down_new,
        down_new,
        first_gains_new,
        second_gains_new,
        gains_new,
    )


def solution(mesh):
    in_specs = (
        P("fsdp", "seq", None),
        P("fsdp", "seq", None),
        P(("seq", "fsdp"), None),
        P(("seq", "fsdp"), None),
        P(("seq", "fsdp"), None),
        P(("seq", "fsdp"), None),
        P(None, ("seq", "fsdp")),
        P(("seq", "fsdp"), None),
        P(("seq", "fsdp"), None),
        P(("seq", "fsdp"), None),
        P(("seq", "fsdp"), None),
        P(None, ("seq", "fsdp")),
        P(("seq", "fsdp"), None),
        P(("seq", "fsdp"), None),
        P(("seq", "fsdp"), None),
        P(("seq", "fsdp"), None),
        P(None, ("seq", "fsdp")),
    )
    out_specs = (
        P("fsdp", "seq", None),
        P("fsdp", "seq", None),
        P(("seq", "fsdp"), None),
        P(("seq", "fsdp"), None),
        P(("seq", "fsdp"), None),
        P(("seq", "fsdp"), None),
        P(("seq", "fsdp"), None),
        P(("seq", "fsdp"), None),
        P(("seq", "fsdp"), None),
        P(("seq", "fsdp"), None),
        P(("seq", "fsdp"), None),
        P(("seq", "fsdp"), None),
        P(("seq", "fsdp"), None),
        P(("seq", "fsdp"), None),
        P(None, ("seq", "fsdp")),
        P(None, ("seq", "fsdp")),
        P(None, ("seq", "fsdp")),
    )
    return jax.shard_map(body, mesh=mesh, in_specs=in_specs, out_specs=out_specs, check_vma=False)
```

```python
import functools

import jax
import jax.numpy as jnp
from jax import lax
from jax.experimental import pallas as pl
from jax.experimental.pallas import tpu as pltpu
from jax.sharding import PartitionSpec as P

D = 2048
FF = 5632
HEADS = 32
KV_HEADS = 4
HEAD_DIM = 64
STEP = 10


epsilon = 1e-05
adam_epsilon = 1e-08
beta_first = 0.9
beta_second = 0.95
rope_base = 10000.0
weight_decay = 0.1
masked_value = -1e30


def rotate(field, position, sign):
    half = field.shape[-1] // 2
    exponent = jnp.arange(half).astype(jnp.float32) * (-2.0 / field.shape[-1])
    frequency = jnp.power(rope_base, exponent)
    angle = position[:, None] * frequency[None, :]
    cosine = jnp.cos(angle)[:, None, :]
    sine = sign * jnp.sin(angle)[:, None, :]
    first = field[..., :half]
    second = field[..., half:]
    return jnp.concatenate(
        [first * cosine - second * sine, second * cosine + first * sine], axis=-1
    )


def rms_scale(rows):
    return lax.rsqrt(jnp.mean(rows * rows, axis=-1, keepdims=True) + epsilon)


def norm_back(rows, scale_rows, gain, grad):
    weighted = grad * gain
    row_grad = scale_rows * weighted - rows * scale_rows**3 * jnp.mean(
        weighted * rows, axis=-1, keepdims=True
    )
    gain_grad = jnp.sum(grad * rows * scale_rows, axis=0)
    return (row_grad, gain_grad)


def dot(left, right):
    return jnp.dot(left, right, preferred_element_type=jnp.float32)


def outer(left, right):
    return lax.dot_general(
        left, right, (((0,), (0,)), ((), ())), preferred_element_type=jnp.float32
    )


def against(left, right):
    return lax.dot_general(
        left, right, (((1,), (1,)), ((), ())), preferred_element_type=jnp.float32
    )


def stack_heads(field, heads):
    return jnp.concatenate(
        [field[:, h * HEAD_DIM : (h + 1) * HEAD_DIM] for h in range(heads)], axis=0
    )


def unstack_heads(field, heads):
    rows = field.shape[0] // heads
    return jnp.concatenate([field[h * rows : (h + 1) * rows] for h in range(heads)], axis=1)


def masked_scores(keys, queries, block, first):
    scores = against(keys, queries)
    key_place = lax.broadcasted_iota(jnp.int32, scores.shape, 0)
    query_place = first + lax.rem(lax.broadcasted_iota(jnp.int32, scores.shape, 1), block)
    return jnp.where(key_place <= query_place, scores, masked_value)


def remote(source, target, send, arrive, axis, device):
    return pltpu.make_async_remote_copy(
        src_ref=source,
        dst_ref=target,
        send_sem=send,
        recv_sem=arrive,
        device_id={axis: device},
        device_id_type=pl.DeviceIdType.MESH,
    )


VMEM = pl.BlockSpec(memory_space=pltpu.VMEM)


def core_pair(index):
    return index // 2, lax.rem(index, 2)


def pass_rows_start(rows, send, come, near):
    s = lax.axis_index("seq")
    for d in [1] + near:
        rows_copy(rows, send, come, d, s, s ^ d).start()


def pass_rows_finish(rows, send, come, forward, passed, near):
    s = lax.axis_index("seq")
    for d in near:
        rows_copy(rows, send, come, d, s ^ d, s ^ d).wait_recv()
        rows_copy(rows, forward, passed, d, s ^ d, s ^ 1).start()
    rows_copy(rows, send, come, 1, s ^ 1, s ^ 1).wait()
    for d in near:
        rows_copy(rows, send, come, d, s, s ^ d).wait_send()
        rows_copy(rows, forward, passed, d, s ^ d, s ^ 1).wait_send()
        rows_copy(rows, forward, passed, d, s ^ 1 ^ d, s ^ 1).wait_recv()


def rows_copy(rows, send, come, d, owner, target):
    place, half = core_pair(owner)
    return remote(rows.at[place, half], rows.at[place, half], send.at[d], come.at[d], "seq", target)


def share_kernel(
    in_ref, gain_ref, gate_up_ref, down_ref, feed_gate_up, feed_down, in_rows,
    low_gate_up, low_down, send_feed, come_feed, send_in, come_in, pass_in, passed_in,
):
    group, slices = lax.axis_size("seq"), lax.axis_size("fsdp")
    s, f = lax.axis_index("seq"), lax.axis_index("fsdp")
    pair, core = core_pair(s)
    depth, inward_cols = in_ref.shape
    ff_cols = FF // slices
    near = list(range(2, group, 2))
    in_rows[pair, core, :, pl.ds(0, inward_cols)] = in_ref[...].astype(jnp.bfloat16)
    in_rows[pair, core, :, pl.ds(inward_cols, 128)] = gain_ref[...]
    meet_spread(near)
    pass_rows_start(in_rows, send_in, come_in, near)
    feeds = ((low_gate_up, feed_gate_up), (low_down, feed_down))

    def feed_copy(k, d, owner, target):
        low, feed = feeds[k]
        return remote(
            low.at[target],
            feed.at[pl.ds(pl.multiple_of(owner * depth, depth), depth), :],
            send_feed.at[k, d], come_feed.at[k, d], "fsdp", target,
        )

    for t in range(slices):
        columns = pl.ds(t * ff_cols, ff_cols)
        low_gate_up[t, :, pl.ds(0, ff_cols)] = gate_up_ref[:, columns].astype(jnp.bfloat16)
        low_gate_up[t, :, pl.ds(ff_cols, ff_cols)] = gate_up_ref[
            :, pl.ds(FF + t * ff_cols, ff_cols)
        ].astype(jnp.bfloat16)
        low_down[t] = down_ref[:, columns].astype(jnp.bfloat16)

        @pl.when(f != t)
        def _():
            for k in range(2):
                feed_copy(k, f ^ t, f, t).start()

    mine = pl.ds(pl.multiple_of(f * depth, depth), depth)
    for low, feed in feeds:
        feed[mine, :] = low[f]
    pass_rows_finish(in_rows, send_in, come_in, pass_in, passed_in, near)
    for d in range(1, slices):
        for k in range(2):
            feed_copy(k, d, f ^ d, f ^ d).wait()


def share_weights(w_inward, gain_columns, w_gate_up, w_down, group, slices):
    depth = w_inward.shape[0]
    ff_cols = FF // slices
    width = w_inward.shape[1] + 128
    sems = [pltpu.SemaphoreType.DMA((2, slices))] * 2 + [pltpu.SemaphoreType.DMA((group,))] * 4
    return pl.pallas_call(
        share_kernel,
        in_specs=[VMEM] * 4,
        out_specs=[VMEM] * 3,
        out_shape=[
            jax.ShapeDtypeStruct((slices * depth, 2 * ff_cols), jnp.bfloat16),
            jax.ShapeDtypeStruct((slices * depth, ff_cols), jnp.bfloat16),
            jax.ShapeDtypeStruct((group // 2, 2, depth, width), jnp.bfloat16),
        ],
        scratch_shapes=[
            pltpu.VMEM((slices, depth, 2 * ff_cols), jnp.bfloat16),
            pltpu.VMEM((slices, depth, ff_cols), jnp.bfloat16),
        ]
        + sems,
        compiler_params=pltpu.CompilerParams(
            vmem_limit_bytes=48 << 20, collective_id=2, has_side_effects=True
        ),
    )(w_inward, gain_columns, w_gate_up, w_down)


def block_order():
    slices = lax.axis_size("fsdp")
    if slices != 4:
        return list(range(1, slices))
    core = lax.rem(lax.axis_index("seq"), 2)
    return [2 - core, 1 + core, 3]


def gather_blocks(source, place, send, come):
    f, slices = lax.axis_index("fsdp"), lax.axis_size("fsdp")
    order = block_order()
    square = slices == 4
    near = [1, 2] if square else order

    def direct(d, owner, holder):
        return remote(source, place(owner, holder), send.at[d], come.at[d], "fsdp", f ^ d)

    def relay(owner, holder):
        return remote(
            place(order[0], 0), place(owner, holder), send.at[3], come.at[3], "fsdp", f ^ order[1]
        )

    def start():
        for d in near:
            direct(d, 0, d).start()

    def take(turn):
        if square and turn == 2:
            relay(3, 0).wait_recv()
        else:
            direct(order[turn], order[turn], 0).wait_recv()
        if square and turn == 0:
            relay(order[0], order[1]).start()

    def finish():
        for d in near:
            direct(d, 0, d).wait_send()
        if square:
            relay(order[0], order[1]).wait_send()

    return order, start, take, finish


def spread_copies(rows, full, send, come, forward, passed):
    s, f = lax.axis_index("seq"), lax.axis_index("fsdp")
    core = lax.rem(s, 2)
    order, begin, take, sent = gather_blocks(
        rows.at[:, core], lambda owner, holder: full.at[:, core, f ^ owner], send, come
    )

    def second(d, half):
        block = full.at[:, half, f ^ d]
        return remote(block, block, forward.at[d], passed.at[d], "seq", s ^ 1)

    def local():
        full[:, :, f] = rows[...]

    def early():
        take(0)
        second(order[0], core).start()

    def finish():
        for turn, d in enumerate(order[1:]):
            take(turn + 1)
            second(d, core).start()
        sent()
        for d in range(1, lax.axis_size("fsdp")):
            second(d, core).wait_send()
            second(d, 1 - core).wait_recv()

    return begin, local, early, finish


def meet_spread(extra=()):
    barrier = pltpu.get_barrier_semaphore()
    s, f = lax.axis_index("seq"), lax.axis_index("fsdp")
    near = sorted({1, *extra})
    slices = lax.axis_size("fsdp")
    for d in near:
        pl.semaphore_signal(
            barrier, inc=1, device_id={"seq": s ^ d}, device_id_type=pl.DeviceIdType.MESH
        )
    for d in range(1, slices):
        pl.semaphore_signal(
            barrier, inc=1, device_id={"fsdp": f ^ d}, device_id_type=pl.DeviceIdType.MESH
        )
    pl.semaphore_wait(barrier, len(near) + slices - 1)


def spread_part(
    rows, out_ref, full, out_rows, send, come, forward, passed,
    send_out, come_out, pass_out, passed_out, follow,
):
    near = list(range(2, lax.axis_size("seq"), 2))
    pair, core = core_pair(lax.axis_index("seq"))
    start, local, early, finish = spread_copies(rows, full, send, come, forward, passed)
    start()
    out_rows[pair, core] = out_ref[...].astype(jnp.bfloat16)
    pass_rows_start(out_rows, send_out, come_out, near)
    local()
    early()
    pass_rows_finish(out_rows, send_out, come_out, pass_out, passed_out, near)
    follow()
    finish()


def projections(x_ref, cosine_ref, sine_ref, full, normed, query, kv, gains):
    depth = full.shape[0] * 2 * full.shape[2] * full.shape[3]
    width, kv_width = HEADS * HEAD_DIM, KV_HEADS * HEAD_DIM

    def weights(first, count):
        return full[:, :, :, :, pl.ds(first, count)].reshape(depth, count)

    def turn(field):
        parts = []
        for i in range(field.shape[1] // 128):
            part = field[:, i * 128 : (i + 1) * 128]
            lane = lax.rem(lax.broadcasted_iota(jnp.int32, part.shape, 1), HEAD_DIM)
            other = jnp.where(
                lane < HEAD_DIM // 2,
                pltpu.roll(part, 128 - HEAD_DIM // 2, 1),
                pltpu.roll(part, HEAD_DIM // 2, 1),
            )
            parts.append(part * cosine_ref[...] + other * sine_ref[...])
        return jnp.concatenate(parts, axis=1)

    def keys_and_values():
        gains[...] = weights(width + 2 * kv_width, 128).astype(jnp.float32).T[:2]
        x = x_ref[...].astype(jnp.float32)
        normed[...] = (x * rms_scale(x) * gains[0:1, :]).astype(jnp.bfloat16)
        mixed = dot(normed[...], weights(width, 2 * kv_width))
        keys, values = turn(mixed[:, :kv_width]), mixed[:, kv_width:]
        kv[...] = jnp.concatenate(
            [
                field[:, h * HEAD_DIM : (h + 1) * HEAD_DIM]
                for h in range(KV_HEADS)
                for field in (keys, values)
            ],
            axis=1,
        ).astype(jnp.bfloat16)

    def queries():
        def query_part(i, _):
            first = pl.multiple_of(i * 512, 512)
            query[:, pl.ds(first, 512)] = turn(dot(normed[...], weights(first, 512))).astype(
                jnp.bfloat16
            )
            return 0

        lax.fori_loop(0, width // 512, query_part, 0)

    return keys_and_values, queries


def forward_kernel(
    in_rows, out_ref, x_ref, cosine_ref, sine_ref, dy_ref,
    in_full, normed, query_ref, gains, kv_all, mixed_ref, logs, out_full, middle, normed_second, dy_all, normed_near,
    kv_ref, out_rows, queries, largest, total, mixed,
    send_in, come_in, pass_in, passed_in, send_z, come_z, pass_z, passed_z,
    send_kv, come_kv, pass_kv, passed_kv, send_rows, come_rows, pass_rows, passed_rows,
    send_dy, come_dy, send_normed, come_normed, own_sem,
):
    group, s = lax.axis_size("seq"), lax.axis_index("seq")
    place, core = core_pair(s)
    local = query_ref.shape[0]
    per_head = HEADS // KV_HEADS
    width, pair = per_head * HEAD_DIM, 2 * HEAD_DIM
    near = list(range(2, group, 2))
    meet_spread(range(1, group))
    find_keys, find_queries = projections(
        x_ref, cosine_ref, sine_ref, in_full, normed, query_ref, kv_ref, gains
    )
    spread_start, spread_local, spread_early, spread_finish = spread_copies(
        out_rows, out_full, send_rows, come_rows, pass_rows, passed_rows
    )

    dy_order, dy_start, dy_take, dy_sent = gather_blocks(
        dy_ref, lambda owner, holder: dy_all.at[owner ^ holder], send_dy, come_dy
    )
    slices, f = lax.axis_size("fsdp"), lax.axis_index("fsdp")
    square = slices == 4

    def normed_copy(d):
        slot = 1 if square else d
        return remote(
            normed, normed_near.at[slot], send_normed.at[slot], come_normed.at[slot], "fsdp", f ^ d
        )

    near_normed = dy_order[:1] if square else range(1, slices)
    own_dy = pltpu.make_async_copy(dy_ref, dy_all.at[0], own_sem.at[0])
    own_dy.start()

    def links_early():
        spread_early()
        dy_start()

    def links_late():
        dy_take(0)
        for d in near_normed:
            normed_copy(d).start()

    def kv_copy(d, owner, target):
        chip, half = core_pair(owner)
        return remote(kv_ref, kv_all.at[chip, half], send_kv.at[d], come_kv.at[d], "seq", target)

    def hand_on(chip, half):
        block = kv_all.at[chip, half]
        return remote(block, block, pass_kv.at[chip, half], passed_kv.at[chip, half], "seq", s ^ 1)

    spread_part(
        in_rows, out_ref, in_full, out_rows, send_in, come_in, pass_in, passed_in,
        send_z, come_z, pass_z, passed_z, spread_start,
    )
    find_keys()
    kv_copy(1, s, s ^ 1).start()
    for d in near:

        @pl.when((s ^ d) > s)
        def _():
            kv_copy(d, s, s ^ d).start()

    spread_local()
    find_queries()
    kv_all[place, core] = kv_ref[...]
    for h in range(KV_HEADS):
        field = query_ref[:, pl.ds(h * width, width)]
        queries[h] = stack_heads(field, per_head) * jnp.bfloat16(HEAD_DIM**-0.5)
    links_early()

    def scores_of(h, chip, masked):
        kv = kv_all[chip, :, :, pl.ds(pl.multiple_of(h * pair, pair), pair)]
        kv = kv.reshape(2 * local, pair)
        keys, values = kv[:, :HEAD_DIM], kv[:, HEAD_DIM:]
        if masked:
            return masked_scores(keys, queries[h], local, core * local), values
        return against(keys, queries[h]), values

    def keep(heads, states):
        for h, (new, new_total, new_mixed) in zip(heads, states):
            largest[h], total[h], mixed[h] = new, new_total, new_mixed

    def own_head(h):
        scores, values = scores_of(h, place, True)
        new = jnp.max(scores, axis=0, keepdims=True)
        weights = jnp.exp(scores - new)
        return (
            new,
            jnp.sum(weights, axis=0, keepdims=True),
            outer(values, weights.astype(jnp.bfloat16)),
        )

    def own_chip(i, _):
        heads = (2 * i, 2 * i + 1)
        keep(heads, [own_head(h) for h in heads])
        return 0

    kv_copy(1, s ^ 1, s ^ 1).wait_recv()
    lax.fori_loop(0, KV_HEADS // 2, own_chip, 0)

    @pl.when(place == 0)
    def _():
        links_late()

    def earlier_chip(turn, _):
        chip = place - 1 - turn

        @pl.when(turn == 0)
        def _():
            links_late()

        owner = 2 * chip + core
        kv_copy(owner ^ s, owner, owner).wait_recv()
        hand_on(chip, core).start()
        hand_on(chip, 1 - core).wait_recv()

        def head(h):
            scores, values = scores_of(h, chip, False)
            old = largest[h]
            new = jnp.maximum(old, jnp.max(scores, axis=0, keepdims=True))
            fade = jnp.exp(old - new)
            weights = jnp.exp(scores - new)
            return (
                new,
                total[h] * fade + jnp.sum(weights, axis=0, keepdims=True),
                mixed[h] * fade + outer(values, weights.astype(jnp.bfloat16)),
            )

        def two_heads(i, _):
            heads = (2 * i, 2 * i + 1)
            keep(heads, [head(h) for h in heads])
            return 0

        lax.fori_loop(0, KV_HEADS // 2, two_heads, 0)
        return 0

    lax.fori_loop(0, place, earlier_chip, 0)

    for h in range(KV_HEADS):
        logs[h] = largest[h] + jnp.log(total[h])
        mixed_ref[:, pl.ds(h * width, width)] = unstack_heads(
            (mixed[h] / total[h]).T, per_head
        ).astype(mixed_ref.dtype)
    kv_copy(1, s, s ^ 1).wait_send()
    for d in near:

        @pl.when((s ^ d) > s)
        def _():
            kv_copy(d, s, s ^ d).wait_send()

    def handed(chip, _):
        hand_on(chip, core).wait_send()
        return 0

    lax.fori_loop(0, place, handed, 0)
    spread_finish()

    depth = out_full.shape[0] * 2 * out_full.shape[2] * out_full.shape[3]

    def middle_part(i, _):
        columns = pl.ds(pl.multiple_of(i * 512, 512), 512)
        weights = out_full[:, :, :, :, columns].reshape(depth, 512)
        middle[:, columns] = x_ref[:, columns].astype(jnp.float32) + dot(mixed_ref[...], weights)
        return 0

    lax.fori_loop(0, middle.shape[1] // 512, middle_part, 0)
    field = middle[...]
    normed_second[...] = (field * rms_scale(field) * gains[1:2, :]).astype(jnp.bfloat16)
    own_normed = pltpu.make_async_copy(normed, normed_near.at[0], own_sem.at[1])
    own_normed.start()
    for turn in range(1, len(dy_order)):
        dy_take(turn)
    dy_sent()
    for d in near_normed:
        normed_copy(d).wait()
    own_dy.wait()
    own_normed.wait()


def backward_kernel(
    grad_ref, query_ref, mixed_ref, logs, kv_all, branch_ref,
    cosine_ref, sine_ref, cosine_rows, sine_rows, out_parts,
    inward_grad, inward_slices, attended_all, branch_all, out_come, kv_grad,
    queries, grads, inner, query_sum, parts, part_come, final_come,
    send_part, come_part, send_final, come_final, send_slice, come_slice,
    send_mixed, come_mixed, send_out, come_out,
):
    group, s = lax.axis_size("seq"), lax.axis_index("seq")
    place, core = core_pair(s)
    local = query_ref.shape[0]
    per_head = HEADS // KV_HEADS
    width, pair = per_head * HEAD_DIM, 2 * HEAD_DIM
    scale = HEAD_DIM**-0.5
    slices, f = lax.axis_size("fsdp"), lax.axis_index("fsdp")
    share = branch_all.shape[2]
    meet_spread(range(1, group))

    def slice_copy(d, target):
        columns = pl.ds(pl.multiple_of(target * share, 128), share)
        return remote(
            branch_ref.at[:, columns], branch_all.at[d], send_slice.at[d], come_slice.at[d],
            "fsdp", target,
        )

    gathers = [
        gather_blocks(mixed_ref, lambda owner, holder: attended_all.at[owner ^ holder],
                      send_mixed, come_mixed),
    ]

    def out_copy(d):
        return remote(
            out_parts.at[d], out_come.at[d - 1], send_out.at[d], come_out.at[d], "fsdp", f ^ d
        )

    def gathers_early():
        for _, _, take, _ in gathers:
            take(0)

    def part_copy(chip, half):
        return remote(
            parts.at[chip, half], part_come.at[chip], send_part.at[chip], come_part.at[chip],
            "seq", s ^ 1,
        )

    def final_copy(chip, sender):
        return remote(
            parts.at[chip, core], final_come.at[sender], send_final.at[chip], come_final.at[sender],
            "seq", 2 * chip + core,
        )

    for d in range(1, slices):
        slice_copy(d, f ^ d).start()
    for _, begin, _, _ in gathers:
        begin()
    for d in range(1, slices):
        out_copy(d).start()
    attended_all[0] = mixed_ref[...]
    branch_all[0] = branch_ref[:, pl.ds(pl.multiple_of(f * share, 128), share)]
    for h in range(KV_HEADS):
        columns = pl.ds(h * width, width)
        queries[h] = stack_heads(query_ref[:, columns], per_head) * jnp.bfloat16(scale)
        grad = stack_heads(grad_ref[:, columns], per_head)
        grads[h] = grad
        product = grad.astype(jnp.float32) * stack_heads(mixed_ref[:, columns], per_head).astype(
            jnp.float32
        )
        inner[h] = jnp.sum(product.T, axis=0, keepdims=True)
    query_sum[...] = jnp.zeros_like(query_sum)

    def head_grads(h, chip, masked):
        columns = pl.ds(pl.multiple_of(h * pair, pair), pair)
        kv = kv_all[chip, :, :, columns].reshape(2 * local, pair)
        keys, values = kv[:, :HEAD_DIM], kv[:, HEAD_DIM:]
        if masked:
            scores = masked_scores(keys, queries[h], local, core * local)
        else:
            scores = against(keys, queries[h])
        shares = jnp.exp(scores - logs[h])
        share_grad = against(values, grads[h])
        score_grad = (shares * (share_grad - inner[h])).astype(jnp.bfloat16)
        value_grad = dot(shares.astype(jnp.bfloat16), grads[h])
        key_grad = dot(score_grad, queries[h])
        part = jnp.concatenate([key_grad, value_grad], axis=1).astype(jnp.bfloat16)
        return columns, part.reshape(2, local, pair), query_sum[h] + outer(keys, score_grad)

    def all_heads(chip, masked):
        def two_heads(i, _):
            heads = (2 * i, 2 * i + 1)
            done = [head_grads(h, chip, masked) for h in heads]
            for h, (columns, part, total) in zip(heads, done):
                parts[chip, :, :, columns] = part
                query_sum[h] = total
            return 0

        lax.fori_loop(0, KV_HEADS // 2, two_heads, 0)

    def finish_chip(chip):
        part_copy(chip, core).wait_recv()
        parts[chip, core] = (
            parts[chip, core].astype(jnp.float32) + part_come[chip].astype(jnp.float32)
        ).astype(jnp.bfloat16)
        final_copy(chip, place).start()

    def earlier_chip(chip, _):
        @pl.when(chip == place - 1)
        def _():
            gathers_early()

        all_heads(chip, False)
        part_copy(chip, 1 - core).start()

        @pl.when(chip > 0)
        def _():
            finish_chip(chip - 1)

        return 0

    lax.fori_loop(0, place, earlier_chip, 0)

    @pl.when(place > 0)
    def _():
        finish_chip(place - 1)

    all_heads(place, True)

    @pl.when(core == 1)
    def _():
        part_copy(place, 0).start()

    @pl.when(place == 0)
    def _():
        gathers_early()

    half = HEAD_DIM // 2
    for h in range(KV_HEADS):
        total = query_sum[h] * scale
        one, two = total[:half], total[half:]
        turned = jnp.concatenate(
            [
                one * cosine_ref[...] + two * sine_ref[...],
                two * cosine_ref[...] - one * sine_ref[...],
            ],
            axis=0,
        )
        inward_grad[:, pl.ds(h * width, width)] = unstack_heads(turned.T, per_head).astype(
            jnp.bfloat16
        )
    kv_grad[...] = parts[place, core].astype(jnp.float32)

    @pl.when(core == 0)
    def _():
        part_copy(place, 0).wait_recv()
        kv_grad[...] += part_come[place].astype(jnp.float32)

    def later_chip(chip, _):
        final_copy(place, chip).wait_recv()
        kv_grad[...] += final_come[chip].astype(jnp.float32)
        return 0

    lax.fori_loop(place + 1, group // 2, later_chip, 0)
    key_grads, value_grads = [], []
    for h in range(KV_HEADS):
        field = kv_grad[:, pl.ds(h * pair, pair)]
        one, two = field[:, :half], field[:, half:HEAD_DIM]
        key_grads.append(one * cosine_rows[...] + two * sine_rows[...])
        key_grads.append(two * cosine_rows[...] - one * sine_rows[...])
        value_grads.append(field[:, HEAD_DIM:])
    inward_grad[:, pl.ds(HEADS * HEAD_DIM, 2 * KV_HEADS * HEAD_DIM)] = jnp.concatenate(
        key_grads + value_grads, axis=1
    ).astype(jnp.bfloat16)
    rest = inward_grad.shape[1] - slices * inward_slices.shape[2]
    inward_grad[:, pl.ds(inward_grad.shape[1] - rest, rest)] = jnp.zeros((local, rest), jnp.bfloat16)
    part_cols = inward_slices.shape[2]
    for t in range(slices):
        inward_slices[t] = inward_grad[:, pl.ds(t * part_cols, part_cols)]

    def sent(chip, _):
        part_copy(chip, 1 - core).wait_send()
        final_copy(chip, place).wait_send()
        return 0

    lax.fori_loop(0, place, sent, 0)

    @pl.when(core == 1)
    def _():
        part_copy(place, 0).wait_send()

    for d in range(1, slices):
        out_copy(d).wait()
        slice_copy(d, f ^ d).wait()
    for order, _, take, finish in gathers:
        for turn in range(1, len(order)):
            take(turn)
        finish()


def attend_forward(rows, w_outward, x, cosine, sine, upstream, group, slices):
    local, width = x.shape
    pairs, two, depth, inward_width = rows.shape
    outward_width = w_outward.shape[1]
    kv_cols = 2 * KV_HEADS * HEAD_DIM
    columns = HEADS // KV_HEADS * local
    low = jax.ShapeDtypeStruct((local, width), jnp.bfloat16)
    tiles = KV_HEADS * group * columns * local
    four_slices = [pltpu.SemaphoreType.DMA((slices,))] * 4
    in_full, *results = pl.pallas_call(
        forward_kernel,
        in_specs=[VMEM] * 5 + [ANY],
        out_specs=[VMEM] * 10 + [ANY] * 2,
        out_shape=[
            jax.ShapeDtypeStruct((pairs, two, slices, depth, inward_width), jnp.bfloat16),
            low,
            low,
            jax.ShapeDtypeStruct((2, width), jnp.float32),
            jax.ShapeDtypeStruct((pairs, two, local, kv_cols), jnp.bfloat16),
            low,
            jax.ShapeDtypeStruct((KV_HEADS, 1, columns), jnp.float32),
            jax.ShapeDtypeStruct((pairs, two, slices, depth, outward_width), jnp.bfloat16),
            jax.ShapeDtypeStruct((local, width), jnp.float32),
            low,
            jax.ShapeDtypeStruct((slices, local, width), jnp.bfloat16),
            jax.ShapeDtypeStruct((2 if slices == 4 else slices, local, width), jnp.bfloat16),
        ],
        scratch_shapes=[
            pltpu.VMEM((local, kv_cols), jnp.bfloat16),
            pltpu.VMEM((pairs, two, depth, outward_width), jnp.bfloat16),
            pltpu.VMEM((KV_HEADS, columns, HEAD_DIM), jnp.bfloat16),
            pltpu.VMEM((KV_HEADS, 1, columns), jnp.float32),
            pltpu.VMEM((KV_HEADS, 1, columns), jnp.float32),
            pltpu.VMEM((KV_HEADS, HEAD_DIM, columns), jnp.float32),
        ]
        + four_slices
        + [pltpu.SemaphoreType.DMA((group,))] * 6
        + [pltpu.SemaphoreType.DMA((pairs, 2))] * 2
        + four_slices
        + four_slices
        + [pltpu.SemaphoreType.DMA((2,))],
        compiler_params=pltpu.CompilerParams(
            vmem_limit_bytes=60 << 20, collective_id=0, has_side_effects=True
        ),
        cost_estimate=pl.CostEstimate(
            flops=tiles * HEAD_DIM * 160, bytes_accessed=20 << 20, transcendentals=tiles
        ),
    )(
        rows, w_outward, x, jnp.tile(cosine, (1, 4)),
        jnp.tile(jnp.concatenate([-sine, sine], axis=1), (1, 2)), upstream,
    )
    return in_full.reshape(-1, inward_width), *results


def attend_backward(
    grads, query, mixed, logs, kv_all, branch, cosine, sine, out_parts, group, slices
):
    local, features = branch.shape
    per_head = HEADS // KV_HEADS
    columns = per_head * local
    kv_cols = kv_all.shape[3]
    inward_cols = features + kv_cols
    tiles = KV_HEADS * group * columns * local
    gathered = jax.ShapeDtypeStruct((slices, local, features), jnp.bfloat16)
    stacked = pltpu.VMEM((KV_HEADS, columns, HEAD_DIM), jnp.bfloat16)
    one_half = pltpu.VMEM((group // 2, local, kv_cols), jnp.bfloat16)
    return pl.pallas_call(
        backward_kernel,
        in_specs=[VMEM] * 10 + [ANY],
        out_specs=[VMEM] * 4 + [ANY],
        out_shape=[
            jax.ShapeDtypeStruct((local, inward_cols + 128), jnp.bfloat16),
            jax.ShapeDtypeStruct((slices, local, inward_cols // slices), jnp.bfloat16),
            gathered,
            jax.ShapeDtypeStruct((slices, local, features // slices), jnp.bfloat16),
            jax.ShapeDtypeStruct((slices - 1, local, features), jnp.bfloat16),
        ],
        scratch_shapes=[
            pltpu.VMEM((local, kv_cols), jnp.float32),
            stacked,
            stacked,
            pltpu.VMEM((KV_HEADS, 1, columns), jnp.float32),
            pltpu.VMEM((KV_HEADS, HEAD_DIM, columns), jnp.float32),
            pltpu.VMEM((group // 2, 2, local, kv_cols), jnp.bfloat16),
            one_half,
            one_half,
        ]
        + [pltpu.SemaphoreType.DMA((group // 2,))] * 4
        + [pltpu.SemaphoreType.DMA((slices,))] * 4
        + [pltpu.SemaphoreType.DMA((slices,))] * 2,
        compiler_params=pltpu.CompilerParams(
            vmem_limit_bytes=60 << 20, collective_id=1, has_side_effects=True
        ),
        cost_estimate=pl.CostEstimate(
            flops=tiles * HEAD_DIM * 80, bytes_accessed=20 << 20, transcendentals=tiles
        ),
    )(
        grads, query, mixed, logs, kv_all, branch,
        jnp.tile(cosine.T, (1, per_head)), jnp.tile(sine.T, (1, per_head)), cosine, sine,
        out_parts,
    )


def meet_slices():
    slices, f = lax.axis_size("fsdp"), lax.axis_index("fsdp")
    barrier = pltpu.get_barrier_semaphore()
    for d in range(1, slices):
        pl.semaphore_signal(
            barrier, inc=1, device_id={"fsdp": f ^ d}, device_id_type=pl.DeviceIdType.MESH
        )
    pl.semaphore_wait(barrier, slices - 1)


def row_copy(stage, target, sem, r):
    width = stage.shape[0]
    rows = pl.ds(pl.multiple_of(r * width, width), width)
    return pltpu.make_async_copy(stage, target.at[rows, :], sem)


def grad_rows(field, grads, target, stage, sems):
    width = stage.shape[1]
    steps = target.shape[0] // width

    def step(r, _):
        columns = pl.ds(pl.multiple_of(r * width, width), width)
        slot = lax.rem(r, 2)
        left = field[:, :, columns].reshape(grads[0].shape[0], width)

        @pl.when(r > 1)
        def _():
            row_copy(stage.at[slot], target, sems.at[slot], r - 2).wait()

        for k, grad in enumerate(grads):
            units = grad.shape[1]
            stage[slot, :, pl.ds(k * units, units)] = outer(left, grad[...]).astype(jnp.bfloat16)
        row_copy(stage.at[slot], target, sems.at[slot], r).start()
        return 0

    lax.fori_loop(0, steps, step, 0)
    for r in (steps - 2, steps - 1):
        row_copy(stage.at[r % 2], target, sems.at[r % 2], r).wait()


def feed_first_kernel(
    *refs, slices, strip
):
    (
        dy_ref, x_ref, gate_up_ref, normed_ref,
        x_all, gate_all, up_all, hidden, down_grad_out, normed_other,
        gate_sum, up_sum, grad_stage, dy_all, send_x, come_x, grad_sem, dy_sem,
        send_normed, come_normed,
    ) = refs
    f = lax.axis_index("fsdp")
    local = x_ref.shape[0]
    for d in range(slices):
        pltpu.make_async_copy(dy_ref.at[d], dy_all.at[d], dy_sem.at[d]).start()
    meet_slices()

    order, begin, take, sent = gather_blocks(
        x_ref, lambda owner, holder: x_all.at[owner ^ holder], send_x, come_x
    )
    begin()
    x_all[0] = x_ref[...]

    square = slices == 4

    def normed_copy():
        return remote(normed_ref, normed_other, send_normed, come_normed, "fsdp", f ^ order[1])

    def token_block(turn, d):
        for i in range(slices - 1):

            @pl.when(turn == i + 1)
            def _():
                take(i)
                if square and i == 2:
                    normed_copy().start()

        x = x_all[d]
        units = hidden.shape[1]
        gate_sum[...] = dot(x, gate_up_ref[:, pl.ds(0, units)])
        up_sum[...] = dot(x, gate_up_ref[:, pl.ds(units, units)])

        def part(i, _):
            rows = pl.ds(pl.multiple_of(i * strip, strip), strip)
            place = pl.ds(pl.multiple_of(d * local + i * strip, strip), strip)
            gate, up = gate_sum[rows, :], up_sum[rows, :]
            hidden[place, :] = (gate / (1.0 + jnp.exp(-gate)) * up).astype(jnp.bfloat16)
            gate_all[place, :] = gate.astype(jnp.bfloat16)
            up_all[place, :] = up.astype(jnp.bfloat16)
            return 0

        lax.fori_loop(0, local // strip, part, 0)
        following = 0
        for i in reversed(range(slices - 1)):
            following = jnp.where(turn == i, order[i], following)
        return following

    lax.fori_loop(0, slices, token_block, jnp.int32(0))
    for d in range(slices):
        pltpu.make_async_copy(dy_ref.at[d], dy_all.at[d], dy_sem.at[d]).wait()
    grad_rows(dy_all, [hidden], down_grad_out, grad_stage, grad_sem)
    sent()
    if square:
        normed_copy().wait()


def feed_second_kernel(
    *refs, slices, strip
):
    (
        dy_ref, x_ref, gate_all, up_all, hidden, gate_up_ref, down_ref, normed_near,
        back_ref, out_parts, gate_up_grad_out, normed_far,
        dy_all,
        gate_grad, up_grad, hidden_sum, back_send, back_come, out_stage, grad_stage,
        send_back, come_back, out_sem, grad_sem, dy_sem,
        send_normed, come_normed,
    ) = refs
    f = lax.axis_index("fsdp")
    local = back_ref.shape[0]

    def dy_copy(d):
        return pltpu.make_async_copy(dy_ref.at[d], dy_all.at[d], dy_sem.at[d])

    for d in range(slices):
        dy_copy(d).start()
    meet_slices()
    square = slices == 4
    order = block_order()
    first, second = (order[1], order[0]) if square else (None, None)
    turns = [3, second, first, 0] if square else list(range(slices - 1, -1, -1))

    def relay():
        return remote(
            normed_near.at[1], normed_far, send_normed, come_normed, "fsdp", f ^ order[1]
        )

    if square:
        relay().start()
    for d in range(slices):
        dy_copy(d).wait()

    def back_copy(d, target, landing):
        return remote(
            back_send.at[d], back_come.at[landing - 1], send_back.at[d], come_back.at[landing],
            "fsdp", f ^ target,
        )

    def out_copy(slot, d):
        return pltpu.make_async_copy(out_stage.at[slot], out_parts.at[d], out_sem.at[slot])

    def token_block(turn, carry):
        d, before = carry
        place = pl.ds(pl.multiple_of(d * local, local), local)
        hidden_sum[...] = dot(dy_all[d], down_ref[...])

        def part(i, _):
            rows = pl.ds(pl.multiple_of(i * strip, strip), strip)
            here = pl.ds(pl.multiple_of(d * local + i * strip, strip), strip)
            gate = gate_all[here, :].astype(jnp.float32)
            up = up_all[here, :].astype(jnp.float32)
            sigmoid = 1.0 / (1.0 + jnp.exp(-gate))
            grad = hidden_sum[rows, :]
            gate_grad[here, :] = (
                grad * up * sigmoid * (1.0 + gate * (1.0 - sigmoid))
            ).astype(jnp.bfloat16)
            up_grad[here, :] = (grad * gate * sigmoid).astype(jnp.bfloat16)
            return 0

        lax.fori_loop(0, local // strip, part, 0)
        units = hidden.shape[1]
        back = against(gate_grad[place, :], gate_up_ref[:, pl.ds(0, units)])
        back = back + against(up_grad[place, :], gate_up_ref[:, pl.ds(units, units)])
        back_send[d] = back.astype(jnp.bfloat16)
        if square:

            @pl.when(turn == 0)
            def _():
                back_copy(3, first, 3).start()

            @pl.when(turn == 2)
            def _():
                back_copy(3, first, 3).wait_recv()
                back_send[second] = (
                    back_send[second].astype(jnp.float32) + back_come[2].astype(jnp.float32)
                ).astype(jnp.bfloat16)
                back_copy(second, second, second).start()
                back_copy(first, first, first).start()

        else:

            @pl.when(d > 0)
            def _():
                back_copy(d, d, d).start()

        @pl.when(turn > 1)
        def _():
            out_copy(lax.rem(turn, 2), before).wait()

        out_stage[lax.rem(turn, 2)] = against(hidden[place, :], down_ref[...]).astype(jnp.bfloat16)
        out_copy(lax.rem(turn, 2), d).start()
        following = 0
        for i in reversed(range(slices - 1)):
            following = jnp.where(turn == i, turns[i + 1], following)
        return following, d

    lax.fori_loop(0, slices, token_block, (jnp.int32(turns[0]), jnp.int32(0)))
    out_copy(0, 0).wait()
    out_copy(1, 0).wait()
    grad_rows(x_ref, [gate_grad, up_grad], gate_up_grad_out, grad_stage, grad_sem)
    if square:
        relay().wait()
        back_copy(3, first, 3).wait_send()
    for d in (1, 2) if square else range(1, slices):
        back_copy(d, d, d).wait()
    home = [back_send[0]] + [back_come[d - 1] for d in ((1, 2) if square else range(1, slices))]
    back_ref[...] = functools.reduce(jnp.add, [p.astype(jnp.float32) for p in home])


ANY = pl.BlockSpec(memory_space=pl.ANY)


def feed_first(x, upstream_all, gate_up_slice, normed):
    slices, local, width = upstream_all.shape
    ff_cols = gate_up_slice.shape[1] // 2
    tokens = slices * local
    units = jax.ShapeDtypeStruct((tokens, ff_cols), jnp.bfloat16)
    high = pltpu.VMEM((local, ff_cols), jnp.float32)
    sems = pltpu.SemaphoreType.DMA((slices,))
    return pl.pallas_call(
        functools.partial(feed_first_kernel, slices=slices, strip=32),
        in_specs=[ANY] + [VMEM] * 3,
        out_specs=[VMEM] * 4 + [ANY] * 2,
        out_shape=[
            jax.ShapeDtypeStruct((slices, local, width), jnp.bfloat16),
            units,
            units,
            units,
            jax.ShapeDtypeStruct((width, ff_cols), jnp.bfloat16),
            jax.ShapeDtypeStruct((local, width), jnp.bfloat16),
        ],
        scratch_shapes=[
            high,
            high,
            pltpu.VMEM((2, 256, ff_cols), jnp.bfloat16),
            pltpu.VMEM((slices, local, width), jnp.bfloat16),
            sems,
            sems,
            pltpu.SemaphoreType.DMA((2,)),
            sems,
            pltpu.SemaphoreType.DMA,
            pltpu.SemaphoreType.DMA,
        ],
        compiler_params=pltpu.CompilerParams(
            vmem_limit_bytes=60 << 20, collective_id=4, has_side_effects=True
        ),
        cost_estimate=pl.CostEstimate(
            flops=10 * tokens * width * ff_cols, bytes_accessed=30 << 20, transcendentals=0
        ),
    )(upstream_all, x, gate_up_slice, normed)


def feed_second(
    x_all, upstream_all, gate_all, up_all, hidden, gate_up_slice, down_slice, normed_near
):
    slices, local, width = x_all.shape
    ff_cols = gate_up_slice.shape[1] // 2
    tokens = slices * local
    blocks = pltpu.VMEM((slices, local, width), jnp.bfloat16)
    low = pltpu.VMEM((tokens, ff_cols), jnp.bfloat16)
    sems = pltpu.SemaphoreType.DMA((slices,))
    pair = pltpu.SemaphoreType.DMA((2,))
    return pl.pallas_call(
        functools.partial(feed_second_kernel, slices=slices, strip=32),
        in_specs=[ANY] + [VMEM] * 6 + [ANY],
        out_specs=[VMEM] + [ANY] * 3,
        out_shape=[
            jax.ShapeDtypeStruct((local, width), jnp.float32),
            jax.ShapeDtypeStruct((slices, local, width), jnp.bfloat16),
            jax.ShapeDtypeStruct((width, 2 * ff_cols), jnp.bfloat16),
            jax.ShapeDtypeStruct((local, width), jnp.bfloat16),
        ],
        scratch_shapes=[
            blocks,
            low,
            low,
            pltpu.VMEM((local, ff_cols), jnp.float32),
            blocks,
            pltpu.VMEM((slices - 1, local, width), jnp.bfloat16),
            pltpu.VMEM((2, local, width), jnp.bfloat16),
            pltpu.VMEM((2, 256, 2 * ff_cols), jnp.bfloat16),
            sems,
            sems,
            pair,
            pair,
            sems,
            pltpu.SemaphoreType.DMA,
            pltpu.SemaphoreType.DMA,
        ],
        compiler_params=pltpu.CompilerParams(
            vmem_limit_bytes=62 << 20, collective_id=5, has_side_effects=True
        ),
        cost_estimate=pl.CostEstimate(
            flops=20 * tokens * width * ff_cols, bytes_accessed=40 << 20, transcendentals=0
        ),
    )(
        upstream_all, x_all, gate_all, up_all, hidden, gate_up_slice, down_slice,
        normed_near,
    )


def home_kernel(*refs, count, results, moves, gains):
    slices, f = lax.axis_size("fsdp"), lax.axis_index("fsdp")
    group, s = lax.axis_size("seq"), lax.axis_index("seq")
    inputs, refs = refs[: count + gains], refs[count + gains :]
    outputs, refs = refs[: results + gains], refs[results + gains :]
    landed, refs = refs[:count], refs[count:]
    send, come = refs[:2]
    depth = inputs[0].shape[0] // slices
    if gains:
        meet_spread(range(1, group))
    else:
        meet_slices()

    def copy(k, d):
        rows = pl.ds(pl.multiple_of((f ^ d) * depth, depth), depth)
        return remote(
            inputs[k].at[rows, :], landed[k].at[d], send.at[k, d], come.at[k, d], "fsdp", f ^ d
        )

    if gains:
        seq_come, tiles, tile_come, seq_send, seq_sem, tile_send, tile_sem = refs[2:]

        def seq_copy(d):
            return remote(
                inputs[count].at[s ^ d], seq_come.at[d], seq_send.at[d], seq_sem.at[d], "seq", s ^ d
            )

        def tile_copy(d):
            return remote(
                tiles.at[f ^ d], tile_come.at[d], tile_send.at[d], tile_sem.at[d], "fsdp", f ^ d
            )

        for d in range(1, group):
            seq_copy(d).start()
    for k in range(count):
        for d in range(1, slices):
            copy(k, d).start()
    for k in range(count):
        landed[k][0] = inputs[k][pl.ds(pl.multiple_of(f * depth, depth), depth), :]
    if gains:
        seq_come[0] = inputs[count][s]
        for d in range(1, group):
            seq_copy(d).wait()
        total = functools.reduce(jnp.add, [seq_come[d] for d in range(group)])
        part = total.shape[1] // slices
        tiles[...] = jnp.zeros_like(tiles)
        for t in range(slices):
            tiles[t, :, pl.ds(0, part)] = total[:, t * part : (t + 1) * part]
        for d in range(1, slices):
            tile_copy(d).start()
        tile_come[0] = tiles[f]
    for k in range(count):
        for d in range(1, slices):
            copy(k, d).wait()
    for t in range(slices):
        for source, first, width, result, base in moves:
            outputs[result][:, pl.ds(base + t * width, width)] = landed[source][
                f ^ t, :, pl.ds(first, width)
            ]
    if gains:
        for d in range(1, slices):
            tile_copy(d).wait()
        outputs[results][...] = functools.reduce(jnp.add, [tile_come[d] for d in range(slices)])


def bring_home(sources, moves, widths, gains, group, slices, number):
    depth = sources[0].shape[0] // slices
    shapes = [jax.ShapeDtypeStruct((depth, width), jnp.bfloat16) for width in widths]
    scratch = [pltpu.VMEM((slices, depth, s.shape[1]), jnp.bfloat16) for s in sources]
    scratch += [pltpu.SemaphoreType.DMA((len(sources), slices))] * 2
    extra = []
    if gains is not None:
        extra = [gains]
        shapes.append(jax.ShapeDtypeStruct((8, 128), jnp.float32))
        scratch += [
            pltpu.VMEM(gains.shape, jnp.float32),
            pltpu.VMEM((slices, 8, 128), jnp.float32),
            pltpu.VMEM((slices, 8, 128), jnp.float32),
        ]
        scratch += [pltpu.SemaphoreType.DMA((group,))] * 2
        scratch += [pltpu.SemaphoreType.DMA((slices,))] * 2
    return pl.pallas_call(
        functools.partial(
            home_kernel, count=len(sources), results=len(widths), moves=moves, gains=len(extra)
        ),
        in_specs=[VMEM] * (len(sources) + len(extra)),
        out_specs=[VMEM] * len(shapes),
        out_shape=shapes,
        scratch_shapes=scratch,
        compiler_params=pltpu.CompilerParams(
            vmem_limit_bytes=32 << 20, collective_id=number, has_side_effects=True
        ),
        cost_estimate=pl.CostEstimate(flops=10 << 30, bytes_accessed=4 << 20, transcendentals=0),
    )(*sources, *extra)


def swap(piece, axis, offset):
    size = lax.axis_size(axis)
    return lax.ppermute(piece, axis, [(i, i ^ offset) for i in range(size)])


def gather_swap(piece, axis):
    return [piece] + [swap(piece, axis, d) for d in range(1, lax.axis_size(axis))]


def exchange_swap(stack, axis):
    me = lax.axis_index(axis)
    pieces = [
        lax.dynamic_index_in_dim(stack, me ^ d, 0, keepdims=False)
        for d in range(lax.axis_size(axis))
    ]
    return [pieces[0]] + [swap(p, axis, d) for d, p in enumerate(pieces) if d]


def reduce_swap(parts, axis):
    total = parts[0].astype(jnp.float32)
    for d in range(1, len(parts)):
        total = total + swap(parts[d], axis, d).astype(jnp.float32)
    return total


def scatter_rows(partial, after=()):
    partial, *_ = lax.optimization_barrier((partial, *after))
    return lax.psum_scatter(partial, "seq", scatter_dimension=0, tiled=True)


def adam_update(weight, first, second, grad, rate, decay):
    first_new = beta_first * first + (1.0 - beta_first) * grad
    second_new = beta_second * second + (1.0 - beta_second) * grad * grad
    first_hat = first_new / (1.0 - beta_first**STEP)
    second_hat = second_new / (1.0 - beta_second**STEP)
    weight_new = weight - rate * (
        first_hat / (jnp.sqrt(second_hat) + adam_epsilon) + decay * weight
    )
    return (first_new, second_new, weight_new)


def body(
    inputs,
    cotangent,
    w_inward,
    w_outward,
    w_gate_up,
    w_down,
    gains,
    first_inward,
    first_outward,
    first_gate_up,
    first_down,
    first_gains,
    second_inward,
    second_outward,
    second_gate_up,
    second_down,
    second_gains,
):
    rows = inputs[0].astype(jnp.float32)
    upstream = cotangent[0]
    local = rows.shape[0]
    group = lax.axis_size("seq")
    slices = lax.axis_size("fsdp")
    kv_width = KV_HEADS * HEAD_DIM
    inward_cols = D + 2 * kv_width
    ff_cols = FF // slices
    depth = w_inward.shape[0]
    position = (lax.axis_index("seq") * local + jnp.arange(local)).astype(jnp.float32)

    low_gains = jnp.pad(jnp.transpose(gains.astype(jnp.bfloat16)), ((0, 0), (0, 126)))
    feed_gate_up, feed_down, in_rows = share_weights(
        w_inward, low_gains, w_gate_up, w_down, group, slices
    )
    gate_up_slice = lax.all_gather(feed_gate_up, "seq", axis=0, tiled=True)
    exponent = jnp.arange(HEAD_DIM // 2).astype(jnp.float32) * (-2.0 / HEAD_DIM)
    angle = position[:, None] * jnp.power(rope_base, exponent)[None, :]
    cosine, sine = jnp.cos(angle), jnp.sin(angle)
    (
        inward_gains, normed, query, gains_full, kv_all, attended, logs, outward_full,
        middle, normed_second, upstream_all, normed_near,
    ) = attend_forward(in_rows, w_outward, inputs[0], cosine, sine, upstream, group, slices)
    gain_first, gain_second = gains_full[0], gains_full[1]
    scale_first = rms_scale(rows)
    scale_second = rms_scale(middle)
    down_slice = lax.all_gather(feed_down, "seq", axis=0, tiled=True)
    outward_full = outward_full.reshape(D, D)
    normed_all, gate_all, up_all, hidden, down_partial, normed_other = feed_first(
        normed_second, upstream_all, gate_up_slice, normed
    )
    normed_second_grad, out_parts, gate_up_partial, normed_far = feed_second(
        normed_all, upstream_all, gate_all, up_all, hidden, gate_up_slice, down_slice,
        normed_near,
    )
    down_mine = scatter_rows(down_partial)
    gate_up_mine = scatter_rows(gate_up_partial)
    middle_back, gain_second_grad = norm_back(middle, scale_second, gain_second, normed_second_grad)
    middle_grad = upstream.astype(jnp.float32) + middle_back
    branch_low = middle_grad.astype(jnp.bfloat16)
    attended_grad = against(branch_low, outward_full).astype(jnp.bfloat16)
    inward_grad, inward_slices, attended_all, branch_all, out_come = attend_backward(
        attended_grad, query, attended, logs, kv_all, branch_low,
        cosine, sine, out_parts, group, slices,
    )
    inward_grad, inward_slices, attended_all, branch_all, down_mine, normed_far = (
        lax.optimization_barrier(
            (inward_grad, inward_slices, attended_all, branch_all, down_mine, normed_far)
        )
    )
    inward_grad_blocks = exchange_swap(inward_slices, "fsdp")
    outward_partial = outer(attended_all.reshape(-1, D), branch_all.reshape(-1, D // slices))
    outward_partial = outward_partial.astype(jnp.bfloat16)

    if slices == 4:
        own, one, two, far = inward_grad_blocks
        even = lax.rem(lax.axis_index("seq"), 2) == 0
        near_blocks = jnp.concatenate([own, jnp.where(even, two, one)], axis=0)
        inward_partial = (
            outer(normed_near.reshape(-1, D), near_blocks)
            + outer(normed_other, jnp.where(even, one, two))
            + outer(normed_far, far)
        )
    else:
        inward_partial = outer(
            normed_near.reshape(-1, D), jnp.concatenate(inward_grad_blocks, axis=0)
        )
    inward_partial = inward_partial.astype(jnp.bfloat16)
    slice_cols = inward_partial.shape[1]
    inward_partial, gate_up_mine, inward_grad = lax.optimization_barrier(
        (jnp.concatenate([inward_partial, outward_partial], axis=1), gate_up_mine, inward_grad)
    )
    inward_mine = scatter_rows(inward_partial)
    normed_grad = against(inward_grad, inward_gains)
    rows_back, gain_first_grad = norm_back(rows, scale_first, gain_first, normed_grad)
    input_grad = middle_grad + rows_back
    gain_grads = jnp.stack([gain_first_grad, gain_second_grad]).reshape(2, group, D // group)
    gain_grads = jnp.pad(gain_grads.transpose(1, 0, 2), ((0, 0), (0, 6), (0, 0)))
    result = middle + functools.reduce(
        jnp.add,
        [p.astype(jnp.float32) for p in [out_parts[0]] + [out_come[d] for d in range(slices - 1)]],
    )
    gate_up_sum, down_sum, gains_sum = bring_home(
        [gate_up_mine, down_mine],
        [(0, 0, ff_cols, 0, 0), (0, ff_cols, ff_cols, 0, FF), (1, 0, ff_cols, 1, 0)],
        [2 * FF, FF], gain_grads, group, slices, 6,
    )
    inward_sum, outward_sum = bring_home(
        [inward_mine],
        [(0, 0, slice_cols, 0, 0), (0, slice_cols, D // slices, 1, 0)],
        [inward_cols, D], None, group, slices, 7,
    )
    gate_up_sum, down_sum, inward_sum, outward_sum = [
        field.astype(jnp.float32) for field in (gate_up_sum, down_sum, inward_sum, outward_sum)
    ]
    gains_sum = gains_sum[:2, :depth]
    first_inward_new, second_inward_new, inward_new = adam_update(
        w_inward, first_inward, second_inward, inward_sum, 0.02, weight_decay
    )
    first_outward_new, second_outward_new, outward_new = adam_update(
        w_outward, first_outward, second_outward, outward_sum, 0.15, weight_decay
    )
    first_gate_up_new, second_gate_up_new, gate_up_new = adam_update(
        w_gate_up, first_gate_up, second_gate_up, gate_up_sum, 0.02, weight_decay
    )
    first_down_new, second_down_new, down_new = adam_update(
        w_down, first_down, second_down, down_sum, 0.015, weight_decay
    )
    first_gains_new, second_gains_new, gains_new = adam_update(
        gains, first_gains, second_gains, gains_sum, 0.6, 0.0
    )
    return (
        result[None].astype(jnp.bfloat16),
        input_grad[None],
        first_inward_new,
        second_inward_new,
        inward_new,
        first_outward_new,
        second_outward_new,
        outward_new,
        first_gate_up_new,
        second_gate_up_new,
        gate_up_new,
        first_down_new,
        second_down_new,
        down_new,
        first_gains_new,
        second_gains_new,
        gains_new,
    )


def solution(mesh):
    in_specs = (
        P("fsdp", "seq", None),
        P("fsdp", "seq", None),
        P(("seq", "fsdp"), None),
        P(("seq", "fsdp"), None),
        P(("seq", "fsdp"), None),
        P(("seq", "fsdp"), None),
        P(None, ("seq", "fsdp")),
        P(("seq", "fsdp"), None),
        P(("seq", "fsdp"), None),
        P(("seq", "fsdp"), None),
        P(("seq", "fsdp"), None),
        P(None, ("seq", "fsdp")),
        P(("seq", "fsdp"), None),
        P(("seq", "fsdp"), None),
        P(("seq", "fsdp"), None),
        P(("seq", "fsdp"), None),
        P(None, ("seq", "fsdp")),
    )
    out_specs = (
        P("fsdp", "seq", None),
        P("fsdp", "seq", None),
        P(("seq", "fsdp"), None),
        P(("seq", "fsdp"), None),
        P(("seq", "fsdp"), None),
        P(("seq", "fsdp"), None),
        P(("seq", "fsdp"), None),
        P(("seq", "fsdp"), None),
        P(("seq", "fsdp"), None),
        P(("seq", "fsdp"), None),
        P(("seq", "fsdp"), None),
        P(("seq", "fsdp"), None),
        P(("seq", "fsdp"), None),
        P(("seq", "fsdp"), None),
        P(None, ("seq", "fsdp")),
        P(None, ("seq", "fsdp")),
        P(None, ("seq", "fsdp")),
    )
    return jax.shard_map(body, mesh=mesh, in_specs=in_specs, out_specs=out_specs, check_vma=False)
```

```python
import functools

import jax
import jax.numpy as jnp
from jax import lax
from jax.experimental import pallas as pl
from jax.experimental.pallas import tpu as pltpu
from jax.sharding import PartitionSpec as P

D = 2048
FF = 5632
HEADS = 32
KV_HEADS = 4
HEAD_DIM = 64
STEP = 10


epsilon = 1e-05
adam_epsilon = 1e-08
beta_first = 0.9
beta_second = 0.95
rope_base = 10000.0
weight_decay = 0.1
masked_value = -1e30


def rotate(field, position, sign):
    half = field.shape[-1] // 2
    exponent = jnp.arange(half).astype(jnp.float32) * (-2.0 / field.shape[-1])
    frequency = jnp.power(rope_base, exponent)
    angle = position[:, None] * frequency[None, :]
    cosine = jnp.cos(angle)[:, None, :]
    sine = sign * jnp.sin(angle)[:, None, :]
    first = field[..., :half]
    second = field[..., half:]
    return jnp.concatenate(
        [first * cosine - second * sine, second * cosine + first * sine], axis=-1
    )


def rms_scale(rows):
    return lax.rsqrt(jnp.mean(rows * rows, axis=-1, keepdims=True) + epsilon)


def norm_back(rows, scale_rows, gain, grad):
    weighted = grad * gain
    row_grad = scale_rows * weighted - rows * scale_rows**3 * jnp.mean(
        weighted * rows, axis=-1, keepdims=True
    )
    gain_grad = jnp.sum(grad * rows * scale_rows, axis=0)
    return (row_grad, gain_grad)


def dot(left, right):
    return jnp.dot(left, right, preferred_element_type=jnp.float32)


def outer(left, right):
    return lax.dot_general(
        left, right, (((0,), (0,)), ((), ())), preferred_element_type=jnp.float32
    )


def against(left, right):
    return lax.dot_general(
        left, right, (((1,), (1,)), ((), ())), preferred_element_type=jnp.float32
    )


def stack_heads(field, heads):
    return jnp.concatenate(
        [field[:, h * HEAD_DIM : (h + 1) * HEAD_DIM] for h in range(heads)], axis=0
    )


def unstack_heads(field, heads):
    rows = field.shape[0] // heads
    return jnp.concatenate([field[h * rows : (h + 1) * rows] for h in range(heads)], axis=1)


def masked_scores(keys, queries, block, first):
    scores = against(keys, queries)
    key_place = lax.broadcasted_iota(jnp.int32, scores.shape, 0)
    query_place = first + lax.rem(lax.broadcasted_iota(jnp.int32, scores.shape, 1), block)
    return jnp.where(key_place <= query_place, scores, masked_value)


def remote(source, target, send, arrive, axis, device):
    return pltpu.make_async_remote_copy(
        src_ref=source,
        dst_ref=target,
        send_sem=send,
        recv_sem=arrive,
        device_id={axis: device},
        device_id_type=pl.DeviceIdType.MESH,
    )


VMEM = pl.BlockSpec(memory_space=pltpu.VMEM)


def core_pair(index):
    return index // 2, lax.rem(index, 2)


def pass_rows_start(rows, send, come, near):
    s = lax.axis_index("seq")
    for d in [1] + near:
        rows_copy(rows, send, come, d, s, s ^ d).start()


def pass_rows_finish(rows, send, come, forward, passed, near):
    s = lax.axis_index("seq")
    for d in near:
        rows_copy(rows, send, come, d, s ^ d, s ^ d).wait_recv()
        rows_copy(rows, forward, passed, d, s ^ d, s ^ 1).start()
    rows_copy(rows, send, come, 1, s ^ 1, s ^ 1).wait()
    for d in near:
        rows_copy(rows, send, come, d, s, s ^ d).wait_send()
        rows_copy(rows, forward, passed, d, s ^ d, s ^ 1).wait_send()
        rows_copy(rows, forward, passed, d, s ^ 1 ^ d, s ^ 1).wait_recv()


def rows_copy(rows, send, come, d, owner, target):
    place, half = core_pair(owner)
    return remote(rows.at[place, half], rows.at[place, half], send.at[d], come.at[d], "seq", target)


def share_kernel(
    in_ref, gain_ref, gate_up_ref, down_ref, feed_gate_up, feed_down, in_rows,
    low_gate_up, low_down, send_feed, come_feed, send_in, come_in, pass_in, passed_in,
):
    group, slices = lax.axis_size("seq"), lax.axis_size("fsdp")
    s, f = lax.axis_index("seq"), lax.axis_index("fsdp")
    pair, core = core_pair(s)
    depth, inward_cols = in_ref.shape
    ff_cols = FF // slices
    near = list(range(2, group, 2))
    in_rows[pair, core, :, pl.ds(0, inward_cols)] = in_ref[...].astype(jnp.bfloat16)
    in_rows[pair, core, :, pl.ds(inward_cols, 128)] = gain_ref[...]
    meet_spread(near)
    pass_rows_start(in_rows, send_in, come_in, near)
    feeds = ((low_gate_up, feed_gate_up), (low_down, feed_down))

    def feed_copy(k, d, owner, target):
        low, feed = feeds[k]
        return remote(
            low.at[target],
            feed.at[pl.ds(pl.multiple_of(owner * depth, depth), depth), :],
            send_feed.at[k, d], come_feed.at[k, d], "fsdp", target,
        )

    for t in range(slices):
        columns = pl.ds(t * ff_cols, ff_cols)
        low_gate_up[t, :, pl.ds(0, ff_cols)] = gate_up_ref[:, columns].astype(jnp.bfloat16)
        low_gate_up[t, :, pl.ds(ff_cols, ff_cols)] = gate_up_ref[
            :, pl.ds(FF + t * ff_cols, ff_cols)
        ].astype(jnp.bfloat16)
        low_down[t] = down_ref[:, columns].astype(jnp.bfloat16)

        @pl.when(f != t)
        def _():
            for k in range(2):
                feed_copy(k, f ^ t, f, t).start()

    mine = pl.ds(pl.multiple_of(f * depth, depth), depth)
    for low, feed in feeds:
        feed[mine, :] = low[f]
    pass_rows_finish(in_rows, send_in, come_in, pass_in, passed_in, near)
    for d in range(1, slices):
        for k in range(2):
            feed_copy(k, d, f ^ d, f ^ d).wait()


def share_weights(w_inward, gain_columns, w_gate_up, w_down, group, slices):
    depth = w_inward.shape[0]
    ff_cols = FF // slices
    width = w_inward.shape[1] + 128
    sems = [pltpu.SemaphoreType.DMA((2, slices))] * 2 + [pltpu.SemaphoreType.DMA((group,))] * 4
    return pl.pallas_call(
        share_kernel,
        in_specs=[VMEM] * 4,
        out_specs=[VMEM] * 3,
        out_shape=[
            jax.ShapeDtypeStruct((slices * depth, 2 * ff_cols), jnp.bfloat16),
            jax.ShapeDtypeStruct((slices * depth, ff_cols), jnp.bfloat16),
            jax.ShapeDtypeStruct((group // 2, 2, depth, width), jnp.bfloat16),
        ],
        scratch_shapes=[
            pltpu.VMEM((slices, depth, 2 * ff_cols), jnp.bfloat16),
            pltpu.VMEM((slices, depth, ff_cols), jnp.bfloat16),
        ]
        + sems,
        compiler_params=pltpu.CompilerParams(
            vmem_limit_bytes=48 << 20, collective_id=2, has_side_effects=True
        ),
    )(w_inward, gain_columns, w_gate_up, w_down)


def block_order():
    slices = lax.axis_size("fsdp")
    if slices != 4:
        return list(range(1, slices))
    core = lax.rem(lax.axis_index("seq"), 2)
    return [2 - core, 1 + core, 3]


def gather_blocks(source, place, send, come):
    f, slices = lax.axis_index("fsdp"), lax.axis_size("fsdp")
    order = block_order()
    square = slices == 4
    near = [1, 2] if square else order

    def direct(d, owner, holder):
        return remote(source, place(owner, holder), send.at[d], come.at[d], "fsdp", f ^ d)

    def relay(owner, holder):
        return remote(
            place(order[0], 0), place(owner, holder), send.at[3], come.at[3], "fsdp", f ^ order[1]
        )

    def start():
        for d in near:
            direct(d, 0, d).start()

    def take(turn):
        if square and turn == 2:
            relay(3, 0).wait_recv()
        else:
            direct(order[turn], order[turn], 0).wait_recv()
        if square and turn == 0:
            relay(order[0], order[1]).start()

    def finish():
        for d in near:
            direct(d, 0, d).wait_send()
        if square:
            relay(order[0], order[1]).wait_send()

    return order, start, take, finish


def spread_copies(rows, full, send, come, forward, passed):
    s, f = lax.axis_index("seq"), lax.axis_index("fsdp")
    core = lax.rem(s, 2)
    order, begin, take, sent = gather_blocks(
        rows.at[:, core], lambda owner, holder: full.at[:, core, f ^ owner], send, come
    )

    def second(d, half):
        block = full.at[:, half, f ^ d]
        return remote(block, block, forward.at[d], passed.at[d], "seq", s ^ 1)

    def local():
        full[:, :, f] = rows[...]

    def early():
        take(0)
        second(order[0], core).start()

    def finish():
        for turn, d in enumerate(order[1:]):
            take(turn + 1)
            second(d, core).start()
        sent()
        for d in range(1, lax.axis_size("fsdp")):
            second(d, core).wait_send()
            second(d, 1 - core).wait_recv()

    return begin, local, early, finish


def meet_spread(extra=()):
    barrier = pltpu.get_barrier_semaphore()
    s, f = lax.axis_index("seq"), lax.axis_index("fsdp")
    near = sorted({1, *extra})
    slices = lax.axis_size("fsdp")
    for d in near:
        pl.semaphore_signal(
            barrier, inc=1, device_id={"seq": s ^ d}, device_id_type=pl.DeviceIdType.MESH
        )
    for d in range(1, slices):
        pl.semaphore_signal(
            barrier, inc=1, device_id={"fsdp": f ^ d}, device_id_type=pl.DeviceIdType.MESH
        )
    pl.semaphore_wait(barrier, len(near) + slices - 1)


def spread_part(
    rows, out_ref, full, out_rows, send, come, forward, passed,
    send_out, come_out, pass_out, passed_out, follow,
):
    near = list(range(2, lax.axis_size("seq"), 2))
    pair, core = core_pair(lax.axis_index("seq"))
    start, local, early, finish = spread_copies(rows, full, send, come, forward, passed)
    start()
    out_rows[pair, core] = out_ref[...].astype(jnp.bfloat16)
    pass_rows_start(out_rows, send_out, come_out, near)
    local()
    early()
    pass_rows_finish(out_rows, send_out, come_out, pass_out, passed_out, near)
    follow()
    finish()


def projections(x_ref, cosine_ref, sine_ref, full, normed, query, kv, gains):
    depth = full.shape[0] * 2 * full.shape[2] * full.shape[3]
    width, kv_width = HEADS * HEAD_DIM, KV_HEADS * HEAD_DIM

    def weights(first, count):
        return full[:, :, :, :, pl.ds(first, count)].reshape(depth, count)

    def turn(field):
        parts = []
        for i in range(field.shape[1] // 128):
            part = field[:, i * 128 : (i + 1) * 128]
            lane = lax.rem(lax.broadcasted_iota(jnp.int32, part.shape, 1), HEAD_DIM)
            other = jnp.where(
                lane < HEAD_DIM // 2,
                pltpu.roll(part, 128 - HEAD_DIM // 2, 1),
                pltpu.roll(part, HEAD_DIM // 2, 1),
            )
            parts.append(part * cosine_ref[...] + other * sine_ref[...])
        return jnp.concatenate(parts, axis=1)

    def keys_and_values():
        gains[...] = weights(width + 2 * kv_width, 128).astype(jnp.float32).T[:2]
        x = x_ref[...].astype(jnp.float32)
        normed[...] = (x * rms_scale(x) * gains[0:1, :]).astype(jnp.bfloat16)
        mixed = dot(normed[...], weights(width, 2 * kv_width))
        keys, values = turn(mixed[:, :kv_width]), mixed[:, kv_width:]
        kv[...] = jnp.concatenate(
            [
                field[:, h * HEAD_DIM : (h + 1) * HEAD_DIM]
                for h in range(KV_HEADS)
                for field in (keys, values)
            ],
            axis=1,
        ).astype(jnp.bfloat16)

    def queries():
        def query_part(i, _):
            first = pl.multiple_of(i * 512, 512)
            query[:, pl.ds(first, 512)] = turn(dot(normed[...], weights(first, 512))).astype(
                jnp.bfloat16
            )
            return 0

        lax.fori_loop(0, width // 512, query_part, 0)

    return keys_and_values, queries


def forward_kernel(
    in_rows, out_ref, x_ref, cosine_ref, sine_ref, dy_ref,
    in_full, normed, query_ref, gains, kv_all, mixed_ref, logs, out_full, middle, normed_second, dy_all, normed_near,
    kv_ref, out_rows, queries, largest, total, mixed,
    send_in, come_in, pass_in, passed_in, send_z, come_z, pass_z, passed_z,
    send_kv, come_kv, pass_kv, passed_kv, send_rows, come_rows, pass_rows, passed_rows,
    send_dy, come_dy, send_normed, come_normed, own_sem,
):
    group, s = lax.axis_size("seq"), lax.axis_index("seq")
    place, core = core_pair(s)
    local = query_ref.shape[0]
    per_head = HEADS // KV_HEADS
    width, pair = per_head * HEAD_DIM, 2 * HEAD_DIM
    near = list(range(2, group, 2))
    meet_spread(range(1, group))
    find_keys, find_queries = projections(
        x_ref, cosine_ref, sine_ref, in_full, normed, query_ref, kv_ref, gains
    )
    spread_start, spread_local, spread_early, spread_finish = spread_copies(
        out_rows, out_full, send_rows, come_rows, pass_rows, passed_rows
    )

    dy_order, dy_start, dy_take, dy_sent = gather_blocks(
        dy_ref, lambda owner, holder: dy_all.at[owner ^ holder], send_dy, come_dy
    )
    slices, f = lax.axis_size("fsdp"), lax.axis_index("fsdp")
    square = slices == 4

    def normed_copy(d):
        slot = 1 if square else d
        return remote(
            normed, normed_near.at[slot], send_normed.at[slot], come_normed.at[slot], "fsdp", f ^ d
        )

    near_normed = dy_order[:1] if square else range(1, slices)
    own_dy = pltpu.make_async_copy(dy_ref, dy_all.at[0], own_sem.at[0])
    own_dy.start()

    def links_early():
        spread_early()
        dy_start()

    def links_late():
        dy_take(0)
        for d in near_normed:
            normed_copy(d).start()

    def kv_copy(d, owner, target):
        chip, half = core_pair(owner)
        return remote(kv_ref, kv_all.at[chip, half], send_kv.at[d], come_kv.at[d], "seq", target)

    def hand_on(chip, half):
        block = kv_all.at[chip, half]
        return remote(block, block, pass_kv.at[chip, half], passed_kv.at[chip, half], "seq", s ^ 1)

    spread_part(
        in_rows, out_ref, in_full, out_rows, send_in, come_in, pass_in, passed_in,
        send_z, come_z, pass_z, passed_z, spread_start,
    )
    find_keys()
    kv_copy(1, s, s ^ 1).start()
    for d in near:

        @pl.when((s ^ d) > s)
        def _():
            kv_copy(d, s, s ^ d).start()

    spread_local()
    find_queries()
    kv_all[place, core] = kv_ref[...]
    for h in range(KV_HEADS):
        field = query_ref[:, pl.ds(h * width, width)]
        queries[h] = stack_heads(field, per_head) * jnp.bfloat16(HEAD_DIM**-0.5)
    links_early()

    def scores_of(h, chip, masked):
        kv = kv_all[chip, :, :, pl.ds(pl.multiple_of(h * pair, pair), pair)]
        kv = kv.reshape(2 * local, pair)
        keys, values = kv[:, :HEAD_DIM], kv[:, HEAD_DIM:]
        if masked:
            return masked_scores(keys, queries[h], local, core * local), values
        return against(keys, queries[h]), values

    def keep(heads, states):
        for h, (new, new_total, new_mixed) in zip(heads, states):
            largest[h], total[h], mixed[h] = new, new_total, new_mixed

    def own_head(h):
        scores, values = scores_of(h, place, True)
        new = jnp.max(scores, axis=0, keepdims=True)
        weights = jnp.exp(scores - new)
        return (
            new,
            jnp.sum(weights, axis=0, keepdims=True),
            outer(values, weights.astype(jnp.bfloat16)),
        )

    def own_chip(i, _):
        heads = (2 * i, 2 * i + 1)
        keep(heads, [own_head(h) for h in heads])
        return 0

    kv_copy(1, s ^ 1, s ^ 1).wait_recv()
    lax.fori_loop(0, KV_HEADS // 2, own_chip, 0)

    @pl.when(place == 0)
    def _():
        links_late()

    def earlier_chip(turn, _):
        chip = place - 1 - turn

        @pl.when(turn == 0)
        def _():
            links_late()

        owner = 2 * chip + core
        kv_copy(owner ^ s, owner, owner).wait_recv()
        hand_on(chip, core).start()
        hand_on(chip, 1 - core).wait_recv()

        def head(h):
            scores, values = scores_of(h, chip, False)
            old = largest[h]
            new = jnp.maximum(old, jnp.max(scores, axis=0, keepdims=True))
            fade = jnp.exp(old - new)
            weights = jnp.exp(scores - new)
            return (
                new,
                total[h] * fade + jnp.sum(weights, axis=0, keepdims=True),
                mixed[h] * fade + outer(values, weights.astype(jnp.bfloat16)),
            )

        def two_heads(i, _):
            heads = (2 * i, 2 * i + 1)
            keep(heads, [head(h) for h in heads])
            return 0

        lax.fori_loop(0, KV_HEADS // 2, two_heads, 0)
        return 0

    lax.fori_loop(0, place, earlier_chip, 0)

    for h in range(KV_HEADS):
        logs[h] = largest[h] + jnp.log(total[h])
        mixed_ref[:, pl.ds(h * width, width)] = unstack_heads(
            (mixed[h] / total[h]).T, per_head
        ).astype(mixed_ref.dtype)
    kv_copy(1, s, s ^ 1).wait_send()
    for d in near:

        @pl.when((s ^ d) > s)
        def _():
            kv_copy(d, s, s ^ d).wait_send()

    def handed(chip, _):
        hand_on(chip, core).wait_send()
        return 0

    lax.fori_loop(0, place, handed, 0)
    spread_finish()

    depth = out_full.shape[0] * 2 * out_full.shape[2] * out_full.shape[3]

    def middle_part(i, _):
        columns = pl.ds(pl.multiple_of(i * 512, 512), 512)
        weights = out_full[:, :, :, :, columns].reshape(depth, 512)
        middle[:, columns] = x_ref[:, columns].astype(jnp.float32) + dot(mixed_ref[...], weights)
        return 0

    lax.fori_loop(0, middle.shape[1] // 512, middle_part, 0)
    field = middle[...]
    normed_second[...] = (field * rms_scale(field) * gains[1:2, :]).astype(jnp.bfloat16)
    own_normed = pltpu.make_async_copy(normed, normed_near.at[0], own_sem.at[1])
    own_normed.start()
    for turn in range(1, len(dy_order)):
        dy_take(turn)
    dy_sent()
    for d in near_normed:
        normed_copy(d).wait()
    own_dy.wait()
    own_normed.wait()


def backward_kernel(
    grad_ref, query_ref, mixed_ref, logs, kv_all, branch_ref,
    cosine_ref, sine_ref, cosine_rows, sine_rows, out_parts,
    inward_grad, inward_slices, attended_all, branch_all, out_come, kv_grad,
    queries, grads, inner, query_sum, parts, part_come, final_come,
    send_part, come_part, send_final, come_final, send_slice, come_slice,
    send_mixed, come_mixed, send_out, come_out,
):
    group, s = lax.axis_size("seq"), lax.axis_index("seq")
    place, core = core_pair(s)
    local = query_ref.shape[0]
    per_head = HEADS // KV_HEADS
    width, pair = per_head * HEAD_DIM, 2 * HEAD_DIM
    scale = HEAD_DIM**-0.5
    slices, f = lax.axis_size("fsdp"), lax.axis_index("fsdp")
    share = branch_all.shape[2]
    meet_spread(range(1, group))

    def slice_copy(d, target):
        columns = pl.ds(pl.multiple_of(target * share, 128), share)
        return remote(
            branch_ref.at[:, columns], branch_all.at[d], send_slice.at[d], come_slice.at[d],
            "fsdp", target,
        )

    gathers = [
        gather_blocks(mixed_ref, lambda owner, holder: attended_all.at[owner ^ holder],
                      send_mixed, come_mixed),
    ]

    def out_copy(d):
        return remote(
            out_parts.at[d], out_come.at[d - 1], send_out.at[d], come_out.at[d], "fsdp", f ^ d
        )

    def gathers_early():
        for _, _, take, _ in gathers:
            take(0)

    def part_copy(chip, half):
        return remote(
            parts.at[chip, half], part_come.at[chip], send_part.at[chip], come_part.at[chip],
            "seq", s ^ 1,
        )

    def final_copy(chip, sender):
        return remote(
            parts.at[chip, core], final_come.at[sender], send_final.at[chip], come_final.at[sender],
            "seq", 2 * chip + core,
        )

    for d in range(1, slices):
        slice_copy(d, f ^ d).start()
    for _, begin, _, _ in gathers:
        begin()
    for d in range(1, slices):
        out_copy(d).start()
    attended_all[0] = mixed_ref[...]
    branch_all[0] = branch_ref[:, pl.ds(pl.multiple_of(f * share, 128), share)]
    for h in range(KV_HEADS):
        columns = pl.ds(h * width, width)
        queries[h] = stack_heads(query_ref[:, columns], per_head) * jnp.bfloat16(scale)
        grad = stack_heads(grad_ref[:, columns], per_head)
        grads[h] = grad
        product = grad.astype(jnp.float32) * stack_heads(mixed_ref[:, columns], per_head).astype(
            jnp.float32
        )
        inner[h] = jnp.sum(product.T, axis=0, keepdims=True)
    query_sum[...] = jnp.zeros_like(query_sum)

    def head_grads(h, chip, masked):
        columns = pl.ds(pl.multiple_of(h * pair, pair), pair)
        kv = kv_all[chip, :, :, columns].reshape(2 * local, pair)
        keys, values = kv[:, :HEAD_DIM], kv[:, HEAD_DIM:]
        if masked:
            scores = masked_scores(keys, queries[h], local, core * local)
        else:
            scores = against(keys, queries[h])
        shares = jnp.exp(scores - logs[h])
        share_grad = against(values, grads[h])
        score_grad = (shares * (share_grad - inner[h])).astype(jnp.bfloat16)
        value_grad = dot(shares.astype(jnp.bfloat16), grads[h])
        key_grad = dot(score_grad, queries[h])
        part = jnp.concatenate([key_grad, value_grad], axis=1).astype(jnp.bfloat16)
        return columns, part.reshape(2, local, pair), query_sum[h] + outer(keys, score_grad)

    def all_heads(chip, masked):
        def two_heads(i, _):
            heads = (2 * i, 2 * i + 1)
            done = [head_grads(h, chip, masked) for h in heads]
            for h, (columns, part, total) in zip(heads, done):
                parts[chip, :, :, columns] = part
                query_sum[h] = total
            return 0

        lax.fori_loop(0, KV_HEADS // 2, two_heads, 0)

    def finish_chip(chip):
        part_copy(chip, core).wait_recv()
        parts[chip, core] = (
            parts[chip, core].astype(jnp.float32) + part_come[chip].astype(jnp.float32)
        ).astype(jnp.bfloat16)
        final_copy(chip, place).start()

    def earlier_chip(chip, _):
        all_heads(chip, False)
        part_copy(chip, 1 - core).start()

        @pl.when(chip > 0)
        def _():
            finish_chip(chip - 1)

        return 0

    lax.fori_loop(0, place, earlier_chip, 0)

    @pl.when(place > 0)
    def _():
        finish_chip(place - 1)
        gathers_early()

    all_heads(place, True)

    @pl.when(core == 1)
    def _():
        part_copy(place, 0).start()

    @pl.when(place == 0)
    def _():
        gathers_early()

    half = HEAD_DIM // 2
    for h in range(KV_HEADS):
        total = query_sum[h] * scale
        one, two = total[:half], total[half:]
        turned = jnp.concatenate(
            [
                one * cosine_ref[...] + two * sine_ref[...],
                two * cosine_ref[...] - one * sine_ref[...],
            ],
            axis=0,
        )
        inward_grad[:, pl.ds(h * width, width)] = unstack_heads(turned.T, per_head).astype(
            jnp.bfloat16
        )
    kv_grad[...] = parts[place, core].astype(jnp.float32)

    @pl.when(core == 0)
    def _():
        part_copy(place, 0).wait_recv()
        kv_grad[...] += part_come[place].astype(jnp.float32)

    def later_chip(chip, _):
        final_copy(place, chip).wait_recv()
        kv_grad[...] += final_come[chip].astype(jnp.float32)
        return 0

    lax.fori_loop(place + 1, group // 2, later_chip, 0)
    key_grads, value_grads = [], []
    for h in range(KV_HEADS):
        field = kv_grad[:, pl.ds(h * pair, pair)]
        one, two = field[:, :half], field[:, half:HEAD_DIM]
        key_grads.append(one * cosine_rows[...] + two * sine_rows[...])
        key_grads.append(two * cosine_rows[...] - one * sine_rows[...])
        value_grads.append(field[:, HEAD_DIM:])
    inward_grad[:, pl.ds(HEADS * HEAD_DIM, 2 * KV_HEADS * HEAD_DIM)] = jnp.concatenate(
        key_grads + value_grads, axis=1
    ).astype(jnp.bfloat16)
    rest = inward_grad.shape[1] - slices * inward_slices.shape[2]
    inward_grad[:, pl.ds(inward_grad.shape[1] - rest, rest)] = jnp.zeros((local, rest), jnp.bfloat16)
    part_cols = inward_slices.shape[2]
    for t in range(slices):
        inward_slices[t] = inward_grad[:, pl.ds(t * part_cols, part_cols)]

    def sent(chip, _):
        part_copy(chip, 1 - core).wait_send()
        final_copy(chip, place).wait_send()
        return 0

    lax.fori_loop(0, place, sent, 0)

    @pl.when(core == 1)
    def _():
        part_copy(place, 0).wait_send()

    for d in range(1, slices):
        out_copy(d).wait()
        slice_copy(d, f ^ d).wait()
    for order, _, take, finish in gathers:
        for turn in range(1, len(order)):
            take(turn)
        finish()


def attend_forward(rows, w_outward, x, cosine, sine, upstream, group, slices):
    local, width = x.shape
    pairs, two, depth, inward_width = rows.shape
    outward_width = w_outward.shape[1]
    kv_cols = 2 * KV_HEADS * HEAD_DIM
    columns = HEADS // KV_HEADS * local
    low = jax.ShapeDtypeStruct((local, width), jnp.bfloat16)
    tiles = KV_HEADS * group * columns * local
    four_slices = [pltpu.SemaphoreType.DMA((slices,))] * 4
    in_full, *results = pl.pallas_call(
        forward_kernel,
        in_specs=[VMEM] * 5 + [ANY],
        out_specs=[VMEM] * 10 + [ANY] * 2,
        out_shape=[
            jax.ShapeDtypeStruct((pairs, two, slices, depth, inward_width), jnp.bfloat16),
            low,
            low,
            jax.ShapeDtypeStruct((2, width), jnp.float32),
            jax.ShapeDtypeStruct((pairs, two, local, kv_cols), jnp.bfloat16),
            low,
            jax.ShapeDtypeStruct((KV_HEADS, 1, columns), jnp.float32),
            jax.ShapeDtypeStruct((pairs, two, slices, depth, outward_width), jnp.bfloat16),
            jax.ShapeDtypeStruct((local, width), jnp.float32),
            low,
            jax.ShapeDtypeStruct((slices, local, width), jnp.bfloat16),
            jax.ShapeDtypeStruct((2 if slices == 4 else slices, local, width), jnp.bfloat16),
        ],
        scratch_shapes=[
            pltpu.VMEM((local, kv_cols), jnp.bfloat16),
            pltpu.VMEM((pairs, two, depth, outward_width), jnp.bfloat16),
            pltpu.VMEM((KV_HEADS, columns, HEAD_DIM), jnp.bfloat16),
            pltpu.VMEM((KV_HEADS, 1, columns), jnp.float32),
            pltpu.VMEM((KV_HEADS, 1, columns), jnp.float32),
            pltpu.VMEM((KV_HEADS, HEAD_DIM, columns), jnp.float32),
        ]
        + four_slices
        + [pltpu.SemaphoreType.DMA((group,))] * 6
        + [pltpu.SemaphoreType.DMA((pairs, 2))] * 2
        + four_slices
        + four_slices
        + [pltpu.SemaphoreType.DMA((2,))],
        compiler_params=pltpu.CompilerParams(
            vmem_limit_bytes=60 << 20, collective_id=0, has_side_effects=True
        ),
        cost_estimate=pl.CostEstimate(
            flops=tiles * HEAD_DIM * 160, bytes_accessed=20 << 20, transcendentals=tiles
        ),
    )(
        rows, w_outward, x, jnp.tile(cosine, (1, 4)),
        jnp.tile(jnp.concatenate([-sine, sine], axis=1), (1, 2)), upstream,
    )
    return in_full.reshape(-1, inward_width), *results


def attend_backward(
    grads, query, mixed, logs, kv_all, branch, cosine, sine, out_parts, group, slices
):
    local, features = branch.shape
    per_head = HEADS // KV_HEADS
    columns = per_head * local
    kv_cols = kv_all.shape[3]
    inward_cols = features + kv_cols
    tiles = KV_HEADS * group * columns * local
    gathered = jax.ShapeDtypeStruct((slices, local, features), jnp.bfloat16)
    stacked = pltpu.VMEM((KV_HEADS, columns, HEAD_DIM), jnp.bfloat16)
    one_half = pltpu.VMEM((group // 2, local, kv_cols), jnp.bfloat16)
    return pl.pallas_call(
        backward_kernel,
        in_specs=[VMEM] * 10 + [ANY],
        out_specs=[VMEM] * 4 + [ANY],
        out_shape=[
            jax.ShapeDtypeStruct((local, inward_cols + 128), jnp.bfloat16),
            jax.ShapeDtypeStruct((slices, local, inward_cols // slices), jnp.bfloat16),
            gathered,
            jax.ShapeDtypeStruct((slices, local, features // slices), jnp.bfloat16),
            jax.ShapeDtypeStruct((slices - 1, local, features), jnp.bfloat16),
        ],
        scratch_shapes=[
            pltpu.VMEM((local, kv_cols), jnp.float32),
            stacked,
            stacked,
            pltpu.VMEM((KV_HEADS, 1, columns), jnp.float32),
            pltpu.VMEM((KV_HEADS, HEAD_DIM, columns), jnp.float32),
            pltpu.VMEM((group // 2, 2, local, kv_cols), jnp.bfloat16),
            one_half,
            one_half,
        ]
        + [pltpu.SemaphoreType.DMA((group // 2,))] * 4
        + [pltpu.SemaphoreType.DMA((slices,))] * 4
        + [pltpu.SemaphoreType.DMA((slices,))] * 2,
        compiler_params=pltpu.CompilerParams(
            vmem_limit_bytes=60 << 20, collective_id=1, has_side_effects=True
        ),
        cost_estimate=pl.CostEstimate(
            flops=tiles * HEAD_DIM * 80, bytes_accessed=20 << 20, transcendentals=tiles
        ),
    )(
        grads, query, mixed, logs, kv_all, branch,
        jnp.tile(cosine.T, (1, per_head)), jnp.tile(sine.T, (1, per_head)), cosine, sine,
        out_parts,
    )


def meet_slices():
    slices, f = lax.axis_size("fsdp"), lax.axis_index("fsdp")
    barrier = pltpu.get_barrier_semaphore()
    for d in range(1, slices):
        pl.semaphore_signal(
            barrier, inc=1, device_id={"fsdp": f ^ d}, device_id_type=pl.DeviceIdType.MESH
        )
    pl.semaphore_wait(barrier, slices - 1)


def row_copy(stage, target, sem, r):
    width = stage.shape[0]
    rows = pl.ds(pl.multiple_of(r * width, width), width)
    return pltpu.make_async_copy(stage, target.at[rows, :], sem)


def grad_rows(field, grads, target, stage, sems):
    width = stage.shape[1]
    steps = target.shape[0] // width

    def step(r, _):
        columns = pl.ds(pl.multiple_of(r * width, width), width)
        slot = lax.rem(r, 2)
        left = field[:, :, columns].reshape(grads[0].shape[0], width)

        @pl.when(r > 1)
        def _():
            row_copy(stage.at[slot], target, sems.at[slot], r - 2).wait()

        for k, grad in enumerate(grads):
            units = grad.shape[1]
            stage[slot, :, pl.ds(k * units, units)] = outer(left, grad[...]).astype(jnp.bfloat16)
        row_copy(stage.at[slot], target, sems.at[slot], r).start()
        return 0

    lax.fori_loop(0, steps, step, 0)
    for r in (steps - 2, steps - 1):
        row_copy(stage.at[r % 2], target, sems.at[r % 2], r).wait()


def feed_first_kernel(
    *refs, slices, strip
):
    (
        dy_ref, x_ref, gate_up_ref, normed_ref,
        x_all, gate_all, up_all, hidden, down_grad_out, normed_other,
        gate_sum, up_sum, grad_stage, dy_all, send_x, come_x, grad_sem, dy_sem,
        send_normed, come_normed,
    ) = refs
    f = lax.axis_index("fsdp")
    local = x_ref.shape[0]
    for d in range(slices):
        pltpu.make_async_copy(dy_ref.at[d], dy_all.at[d], dy_sem.at[d]).start()
    meet_slices()

    order, begin, take, sent = gather_blocks(
        x_ref, lambda owner, holder: x_all.at[owner ^ holder], send_x, come_x
    )
    begin()
    x_all[0] = x_ref[...]

    square = slices == 4

    def normed_copy():
        return remote(normed_ref, normed_other, send_normed, come_normed, "fsdp", f ^ order[1])

    def token_block(turn, d):
        for i in range(slices - 1):

            @pl.when(turn == i + 1)
            def _():
                take(i)
                if square and i == 2:
                    normed_copy().start()

        x = x_all[d]
        units = hidden.shape[1]
        gate_sum[...] = dot(x, gate_up_ref[:, pl.ds(0, units)])
        up_sum[...] = dot(x, gate_up_ref[:, pl.ds(units, units)])

        def part(i, _):
            rows = pl.ds(pl.multiple_of(i * strip, strip), strip)
            place = pl.ds(pl.multiple_of(d * local + i * strip, strip), strip)
            gate, up = gate_sum[rows, :], up_sum[rows, :]
            hidden[place, :] = (gate / (1.0 + jnp.exp(-gate)) * up).astype(jnp.bfloat16)
            gate_all[place, :] = gate.astype(jnp.bfloat16)
            up_all[place, :] = up.astype(jnp.bfloat16)
            return 0

        lax.fori_loop(0, local // strip, part, 0)
        following = 0
        for i in reversed(range(slices - 1)):
            following = jnp.where(turn == i, order[i], following)
        return following

    lax.fori_loop(0, slices, token_block, jnp.int32(0))
    for d in range(slices):
        pltpu.make_async_copy(dy_ref.at[d], dy_all.at[d], dy_sem.at[d]).wait()
    grad_rows(dy_all, [hidden], down_grad_out, grad_stage, grad_sem)
    sent()
    if square:
        normed_copy().wait()


def feed_second_kernel(
    *refs, slices, strip
):
    (
        dy_ref, x_ref, gate_all, up_all, hidden, gate_up_ref, down_ref, normed_near,
        back_ref, out_parts, gate_up_grad_out, normed_far,
        dy_all,
        gate_grad, up_grad, hidden_sum, back_send, back_come, out_stage, grad_stage,
        send_back, come_back, out_sem, grad_sem, dy_sem,
        send_normed, come_normed,
    ) = refs
    f = lax.axis_index("fsdp")
    local = back_ref.shape[0]

    def dy_copy(d):
        return pltpu.make_async_copy(dy_ref.at[d], dy_all.at[d], dy_sem.at[d])

    for d in range(slices):
        dy_copy(d).start()
    meet_slices()
    square = slices == 4
    order = block_order()
    first, second = (order[1], order[0]) if square else (None, None)
    turns = [3, second, first, 0] if square else list(range(slices - 1, -1, -1))

    def relay():
        return remote(
            normed_near.at[1], normed_far, send_normed, come_normed, "fsdp", f ^ order[1]
        )

    if square:
        relay().start()
    for d in range(slices):
        dy_copy(d).wait()

    def back_copy(d, target, landing):
        return remote(
            back_send.at[d], back_come.at[landing - 1], send_back.at[d], come_back.at[landing],
            "fsdp", f ^ target,
        )

    def out_copy(slot, d):
        return pltpu.make_async_copy(out_stage.at[slot], out_parts.at[d], out_sem.at[slot])

    def token_block(turn, carry):
        d, before = carry
        place = pl.ds(pl.multiple_of(d * local, local), local)
        hidden_sum[...] = dot(dy_all[d], down_ref[...])

        def part(i, _):
            rows = pl.ds(pl.multiple_of(i * strip, strip), strip)
            here = pl.ds(pl.multiple_of(d * local + i * strip, strip), strip)
            gate = gate_all[here, :].astype(jnp.float32)
            up = up_all[here, :].astype(jnp.float32)
            sigmoid = 1.0 / (1.0 + jnp.exp(-gate))
            grad = hidden_sum[rows, :]
            gate_grad[here, :] = (
                grad * up * sigmoid * (1.0 + gate * (1.0 - sigmoid))
            ).astype(jnp.bfloat16)
            up_grad[here, :] = (grad * gate * sigmoid).astype(jnp.bfloat16)
            return 0

        lax.fori_loop(0, local // strip, part, 0)
        units = hidden.shape[1]
        back = against(gate_grad[place, :], gate_up_ref[:, pl.ds(0, units)])
        back = back + against(up_grad[place, :], gate_up_ref[:, pl.ds(units, units)])
        back_send[d] = back.astype(jnp.bfloat16)
        if square:

            @pl.when(turn == 0)
            def _():
                back_copy(3, first, 3).start()

            @pl.when(turn == 2)
            def _():
                back_copy(3, first, 3).wait_recv()
                back_send[second] = (
                    back_send[second].astype(jnp.float32) + back_come[2].astype(jnp.float32)
                ).astype(jnp.bfloat16)
                back_copy(second, second, second).start()
                back_copy(first, first, first).start()

        else:

            @pl.when(d > 0)
            def _():
                back_copy(d, d, d).start()

        @pl.when(turn > 1)
        def _():
            out_copy(lax.rem(turn, 2), before).wait()

        out_stage[lax.rem(turn, 2)] = against(hidden[place, :], down_ref[...]).astype(jnp.bfloat16)
        out_copy(lax.rem(turn, 2), d).start()
        following = 0
        for i in reversed(range(slices - 1)):
            following = jnp.where(turn == i, turns[i + 1], following)
        return following, d

    lax.fori_loop(0, slices, token_block, (jnp.int32(turns[0]), jnp.int32(0)))
    out_copy(0, 0).wait()
    out_copy(1, 0).wait()
    grad_rows(x_ref, [gate_grad, up_grad], gate_up_grad_out, grad_stage, grad_sem)
    if square:
        relay().wait()
        back_copy(3, first, 3).wait_send()
    for d in (1, 2) if square else range(1, slices):
        back_copy(d, d, d).wait()
    home = [back_send[0]] + [back_come[d - 1] for d in ((1, 2) if square else range(1, slices))]
    back_ref[...] = functools.reduce(jnp.add, [p.astype(jnp.float32) for p in home])


ANY = pl.BlockSpec(memory_space=pl.ANY)


def feed_first(x, upstream_all, gate_up_slice, normed):
    slices, local, width = upstream_all.shape
    ff_cols = gate_up_slice.shape[1] // 2
    tokens = slices * local
    units = jax.ShapeDtypeStruct((tokens, ff_cols), jnp.bfloat16)
    high = pltpu.VMEM((local, ff_cols), jnp.float32)
    sems = pltpu.SemaphoreType.DMA((slices,))
    return pl.pallas_call(
        functools.partial(feed_first_kernel, slices=slices, strip=32),
        in_specs=[ANY] + [VMEM] * 3,
        out_specs=[VMEM] * 4 + [ANY] * 2,
        out_shape=[
            jax.ShapeDtypeStruct((slices, local, width), jnp.bfloat16),
            units,
            units,
            units,
            jax.ShapeDtypeStruct((width, ff_cols), jnp.bfloat16),
            jax.ShapeDtypeStruct((local, width), jnp.bfloat16),
        ],
        scratch_shapes=[
            high,
            high,
            pltpu.VMEM((2, 256, ff_cols), jnp.bfloat16),
            pltpu.VMEM((slices, local, width), jnp.bfloat16),
            sems,
            sems,
            pltpu.SemaphoreType.DMA((2,)),
            sems,
            pltpu.SemaphoreType.DMA,
            pltpu.SemaphoreType.DMA,
        ],
        compiler_params=pltpu.CompilerParams(
            vmem_limit_bytes=60 << 20, collective_id=4, has_side_effects=True
        ),
        cost_estimate=pl.CostEstimate(
            flops=10 * tokens * width * ff_cols, bytes_accessed=30 << 20, transcendentals=0
        ),
    )(upstream_all, x, gate_up_slice, normed)


def feed_second(
    x_all, upstream_all, gate_all, up_all, hidden, gate_up_slice, down_slice, normed_near
):
    slices, local, width = x_all.shape
    ff_cols = gate_up_slice.shape[1] // 2
    tokens = slices * local
    blocks = pltpu.VMEM((slices, local, width), jnp.bfloat16)
    low = pltpu.VMEM((tokens, ff_cols), jnp.bfloat16)
    sems = pltpu.SemaphoreType.DMA((slices,))
    pair = pltpu.SemaphoreType.DMA((2,))
    return pl.pallas_call(
        functools.partial(feed_second_kernel, slices=slices, strip=32),
        in_specs=[ANY] + [VMEM] * 6 + [ANY],
        out_specs=[VMEM] + [ANY] * 3,
        out_shape=[
            jax.ShapeDtypeStruct((local, width), jnp.float32),
            jax.ShapeDtypeStruct((slices, local, width), jnp.bfloat16),
            jax.ShapeDtypeStruct((width, 2 * ff_cols), jnp.bfloat16),
            jax.ShapeDtypeStruct((local, width), jnp.bfloat16),
        ],
        scratch_shapes=[
            blocks,
            low,
            low,
            pltpu.VMEM((local, ff_cols), jnp.float32),
            blocks,
            pltpu.VMEM((slices - 1, local, width), jnp.bfloat16),
            pltpu.VMEM((2, local, width), jnp.bfloat16),
            pltpu.VMEM((2, 256, 2 * ff_cols), jnp.bfloat16),
            sems,
            sems,
            pair,
            pair,
            sems,
            pltpu.SemaphoreType.DMA,
            pltpu.SemaphoreType.DMA,
        ],
        compiler_params=pltpu.CompilerParams(
            vmem_limit_bytes=62 << 20, collective_id=5, has_side_effects=True
        ),
        cost_estimate=pl.CostEstimate(
            flops=20 * tokens * width * ff_cols, bytes_accessed=40 << 20, transcendentals=0
        ),
    )(
        upstream_all, x_all, gate_all, up_all, hidden, gate_up_slice, down_slice,
        normed_near,
    )


def home_kernel(*refs, count, results, moves, gains):
    slices, f = lax.axis_size("fsdp"), lax.axis_index("fsdp")
    group, s = lax.axis_size("seq"), lax.axis_index("seq")
    inputs, refs = refs[: count + gains], refs[count + gains :]
    outputs, refs = refs[: results + gains], refs[results + gains :]
    landed, refs = refs[:count], refs[count:]
    send, come = refs[:2]
    depth = inputs[0].shape[0] // slices
    if gains:
        meet_spread(range(1, group))
    else:
        meet_slices()

    def copy(k, d):
        rows = pl.ds(pl.multiple_of((f ^ d) * depth, depth), depth)
        return remote(
            inputs[k].at[rows, :], landed[k].at[d], send.at[k, d], come.at[k, d], "fsdp", f ^ d
        )

    if gains:
        seq_come, tiles, tile_come, seq_send, seq_sem, tile_send, tile_sem = refs[2:]

        def seq_copy(d):
            return remote(
                inputs[count].at[s ^ d], seq_come.at[d], seq_send.at[d], seq_sem.at[d], "seq", s ^ d
            )

        def tile_copy(d):
            return remote(
                tiles.at[f ^ d], tile_come.at[d], tile_send.at[d], tile_sem.at[d], "fsdp", f ^ d
            )

        for d in range(1, group):
            seq_copy(d).start()
    for k in range(count):
        for d in range(1, slices):
            copy(k, d).start()
    for k in range(count):
        landed[k][0] = inputs[k][pl.ds(pl.multiple_of(f * depth, depth), depth), :]
    if gains:
        seq_come[0] = inputs[count][s]
        for d in range(1, group):
            seq_copy(d).wait()
        total = functools.reduce(jnp.add, [seq_come[d] for d in range(group)])
        part = total.shape[1] // slices
        tiles[...] = jnp.zeros_like(tiles)
        for t in range(slices):
            tiles[t, :, pl.ds(0, part)] = total[:, t * part : (t + 1) * part]
        for d in range(1, slices):
            tile_copy(d).start()
        tile_come[0] = tiles[f]
    for k in range(count):
        for d in range(1, slices):
            copy(k, d).wait()
    for t in range(slices):
        for source, first, width, result, base in moves:
            outputs[result][:, pl.ds(base + t * width, width)] = landed[source][
                f ^ t, :, pl.ds(first, width)
            ]
    if gains:
        for d in range(1, slices):
            tile_copy(d).wait()
        outputs[results][...] = functools.reduce(jnp.add, [tile_come[d] for d in range(slices)])


def bring_home(sources, moves, widths, gains, group, slices, number):
    depth = sources[0].shape[0] // slices
    shapes = [jax.ShapeDtypeStruct((depth, width), jnp.bfloat16) for width in widths]
    scratch = [pltpu.VMEM((slices, depth, s.shape[1]), jnp.bfloat16) for s in sources]
    scratch += [pltpu.SemaphoreType.DMA((len(sources), slices))] * 2
    extra = []
    if gains is not None:
        extra = [gains]
        shapes.append(jax.ShapeDtypeStruct((8, 128), jnp.float32))
        scratch += [
            pltpu.VMEM(gains.shape, jnp.float32),
            pltpu.VMEM((slices, 8, 128), jnp.float32),
            pltpu.VMEM((slices, 8, 128), jnp.float32),
        ]
        scratch += [pltpu.SemaphoreType.DMA((group,))] * 2
        scratch += [pltpu.SemaphoreType.DMA((slices,))] * 2
    return pl.pallas_call(
        functools.partial(
            home_kernel, count=len(sources), results=len(widths), moves=moves, gains=len(extra)
        ),
        in_specs=[VMEM] * (len(sources) + len(extra)),
        out_specs=[VMEM] * len(shapes),
        out_shape=shapes,
        scratch_shapes=scratch,
        compiler_params=pltpu.CompilerParams(
            vmem_limit_bytes=32 << 20, collective_id=number, has_side_effects=True
        ),
        cost_estimate=pl.CostEstimate(flops=10 << 30, bytes_accessed=4 << 20, transcendentals=0),
    )(*sources, *extra)


def swap(piece, axis, offset):
    size = lax.axis_size(axis)
    return lax.ppermute(piece, axis, [(i, i ^ offset) for i in range(size)])


def gather_swap(piece, axis):
    return [piece] + [swap(piece, axis, d) for d in range(1, lax.axis_size(axis))]


def exchange_swap(stack, axis):
    me = lax.axis_index(axis)
    pieces = [
        lax.dynamic_index_in_dim(stack, me ^ d, 0, keepdims=False)
        for d in range(lax.axis_size(axis))
    ]
    return [pieces[0]] + [swap(p, axis, d) for d, p in enumerate(pieces) if d]


def reduce_swap(parts, axis):
    total = parts[0].astype(jnp.float32)
    for d in range(1, len(parts)):
        total = total + swap(parts[d], axis, d).astype(jnp.float32)
    return total


def scatter_rows(partial, after=()):
    partial, *_ = lax.optimization_barrier((partial, *after))
    return lax.psum_scatter(partial, "seq", scatter_dimension=0, tiled=True)


def adam_update(weight, first, second, grad, rate, decay):
    first_new = beta_first * first + (1.0 - beta_first) * grad
    second_new = beta_second * second + (1.0 - beta_second) * grad * grad
    first_hat = first_new / (1.0 - beta_first**STEP)
    second_hat = second_new / (1.0 - beta_second**STEP)
    weight_new = weight - rate * (
        first_hat / (jnp.sqrt(second_hat) + adam_epsilon) + decay * weight
    )
    return (first_new, second_new, weight_new)


def body(
    inputs,
    cotangent,
    w_inward,
    w_outward,
    w_gate_up,
    w_down,
    gains,
    first_inward,
    first_outward,
    first_gate_up,
    first_down,
    first_gains,
    second_inward,
    second_outward,
    second_gate_up,
    second_down,
    second_gains,
):
    rows = inputs[0].astype(jnp.float32)
    upstream = cotangent[0]
    local = rows.shape[0]
    group = lax.axis_size("seq")
    slices = lax.axis_size("fsdp")
    kv_width = KV_HEADS * HEAD_DIM
    inward_cols = D + 2 * kv_width
    ff_cols = FF // slices
    depth = w_inward.shape[0]
    position = (lax.axis_index("seq") * local + jnp.arange(local)).astype(jnp.float32)

    low_gains = jnp.pad(jnp.transpose(gains.astype(jnp.bfloat16)), ((0, 0), (0, 126)))
    feed_gate_up, feed_down, in_rows = share_weights(
        w_inward, low_gains, w_gate_up, w_down, group, slices
    )
    gate_up_slice = lax.all_gather(feed_gate_up, "seq", axis=0, tiled=True)
    exponent = jnp.arange(HEAD_DIM // 2).astype(jnp.float32) * (-2.0 / HEAD_DIM)
    angle = position[:, None] * jnp.power(rope_base, exponent)[None, :]
    cosine, sine = jnp.cos(angle), jnp.sin(angle)
    (
        inward_gains, normed, query, gains_full, kv_all, attended, logs, outward_full,
        middle, normed_second, upstream_all, normed_near,
    ) = attend_forward(in_rows, w_outward, inputs[0], cosine, sine, upstream, group, slices)
    gain_first, gain_second = gains_full[0], gains_full[1]
    scale_first = rms_scale(rows)
    scale_second = rms_scale(middle)
    down_slice = lax.all_gather(feed_down, "seq", axis=0, tiled=True)
    outward_full = outward_full.reshape(D, D)
    normed_all, gate_all, up_all, hidden, down_partial, normed_other = feed_first(
        normed_second, upstream_all, gate_up_slice, normed
    )
    normed_second_grad, out_parts, gate_up_partial, normed_far = feed_second(
        normed_all, upstream_all, gate_all, up_all, hidden, gate_up_slice, down_slice,
        normed_near,
    )
    down_mine = scatter_rows(down_partial)
    gate_up_mine = scatter_rows(gate_up_partial)
    middle_back, gain_second_grad = norm_back(middle, scale_second, gain_second, normed_second_grad)
    middle_grad = upstream.astype(jnp.float32) + middle_back
    branch_low = middle_grad.astype(jnp.bfloat16)
    attended_grad = against(branch_low, outward_full).astype(jnp.bfloat16)
    inward_grad, inward_slices, attended_all, branch_all, out_come = attend_backward(
        attended_grad, query, attended, logs, kv_all, branch_low,
        cosine, sine, out_parts, group, slices,
    )
    inward_grad, inward_slices, attended_all, branch_all, down_mine, normed_far = (
        lax.optimization_barrier(
            (inward_grad, inward_slices, attended_all, branch_all, down_mine, normed_far)
        )
    )
    inward_grad_blocks = exchange_swap(inward_slices, "fsdp")
    outward_partial = outer(attended_all.reshape(-1, D), branch_all.reshape(-1, D // slices))
    outward_partial = outward_partial.astype(jnp.bfloat16)

    if slices == 4:
        own, one, two, far = inward_grad_blocks
        even = lax.rem(lax.axis_index("seq"), 2) == 0
        near_blocks = jnp.concatenate([own, jnp.where(even, two, one)], axis=0)
        inward_partial = (
            outer(normed_near.reshape(-1, D), near_blocks)
            + outer(normed_other, jnp.where(even, one, two))
            + outer(normed_far, far)
        )
    else:
        inward_partial = outer(
            normed_near.reshape(-1, D), jnp.concatenate(inward_grad_blocks, axis=0)
        )
    inward_partial = inward_partial.astype(jnp.bfloat16)
    slice_cols = inward_partial.shape[1]
    inward_partial, gate_up_mine, inward_grad = lax.optimization_barrier(
        (jnp.concatenate([inward_partial, outward_partial], axis=1), gate_up_mine, inward_grad)
    )
    inward_mine = scatter_rows(inward_partial)
    normed_grad = against(inward_grad, inward_gains)
    rows_back, gain_first_grad = norm_back(rows, scale_first, gain_first, normed_grad)
    input_grad = middle_grad + rows_back
    gain_grads = jnp.stack([gain_first_grad, gain_second_grad]).reshape(2, group, D // group)
    gain_grads = jnp.pad(gain_grads.transpose(1, 0, 2), ((0, 0), (0, 6), (0, 0)))
    result = middle + functools.reduce(
        jnp.add,
        [p.astype(jnp.float32) for p in [out_parts[0]] + [out_come[d] for d in range(slices - 1)]],
    )
    gate_up_sum, down_sum, gains_sum = bring_home(
        [gate_up_mine, down_mine],
        [(0, 0, ff_cols, 0, 0), (0, ff_cols, ff_cols, 0, FF), (1, 0, ff_cols, 1, 0)],
        [2 * FF, FF], gain_grads, group, slices, 6,
    )
    inward_sum, outward_sum = bring_home(
        [inward_mine],
        [(0, 0, slice_cols, 0, 0), (0, slice_cols, D // slices, 1, 0)],
        [inward_cols, D], None, group, slices, 7,
    )
    gate_up_sum, down_sum, inward_sum, outward_sum = [
        field.astype(jnp.float32) for field in (gate_up_sum, down_sum, inward_sum, outward_sum)
    ]
    gains_sum = gains_sum[:2, :depth]
    first_inward_new, second_inward_new, inward_new = adam_update(
        w_inward, first_inward, second_inward, inward_sum, 0.02, weight_decay
    )
    first_outward_new, second_outward_new, outward_new = adam_update(
        w_outward, first_outward, second_outward, outward_sum, 0.15, weight_decay
    )
    first_gate_up_new, second_gate_up_new, gate_up_new = adam_update(
        w_gate_up, first_gate_up, second_gate_up, gate_up_sum, 0.02, weight_decay
    )
    first_down_new, second_down_new, down_new = adam_update(
        w_down, first_down, second_down, down_sum, 0.015, weight_decay
    )
    first_gains_new, second_gains_new, gains_new = adam_update(
        gains, first_gains, second_gains, gains_sum, 0.6, 0.0
    )
    return (
        result[None].astype(jnp.bfloat16),
        input_grad[None],
        first_inward_new,
        second_inward_new,
        inward_new,
        first_outward_new,
        second_outward_new,
        outward_new,
        first_gate_up_new,
        second_gate_up_new,
        gate_up_new,
        first_down_new,
        second_down_new,
        down_new,
        first_gains_new,
        second_gains_new,
        gains_new,
    )


def solution(mesh):
    in_specs = (
        P("fsdp", "seq", None),
        P("fsdp", "seq", None),
        P(("seq", "fsdp"), None),
        P(("seq", "fsdp"), None),
        P(("seq", "fsdp"), None),
        P(("seq", "fsdp"), None),
        P(None, ("seq", "fsdp")),
        P(("seq", "fsdp"), None),
        P(("seq", "fsdp"), None),
        P(("seq", "fsdp"), None),
        P(("seq", "fsdp"), None),
        P(None, ("seq", "fsdp")),
        P(("seq", "fsdp"), None),
        P(("seq", "fsdp"), None),
        P(("seq", "fsdp"), None),
        P(("seq", "fsdp"), None),
        P(None, ("seq", "fsdp")),
    )
    out_specs = (
        P("fsdp", "seq", None),
        P("fsdp", "seq", None),
        P(("seq", "fsdp"), None),
        P(("seq", "fsdp"), None),
        P(("seq", "fsdp"), None),
        P(("seq", "fsdp"), None),
        P(("seq", "fsdp"), None),
        P(("seq", "fsdp"), None),
        P(("seq", "fsdp"), None),
        P(("seq", "fsdp"), None),
        P(("seq", "fsdp"), None),
        P(("seq", "fsdp"), None),
        P(("seq", "fsdp"), None),
        P(("seq", "fsdp"), None),
        P(None, ("seq", "fsdp")),
        P(None, ("seq", "fsdp")),
        P(None, ("seq", "fsdp")),
    )
    return jax.shard_map(body, mesh=mesh, in_specs=in_specs, out_specs=out_specs, check_vma=False)
```
